32 devices in a mesh: dp: 8 (over z, x), tensor: 4 (over y, core).
Axes of the slice: x: 2, y: 2, z: 4, core: 2. Of those that a mesh axis runs over, the one named last changes fastest.
Arguments:
- block_input: bfloat16 [16384, 2048], P('dp'), may hold values from -6 to 6
- cotangent: bfloat16 [16384, 2048], P('dp')
- segment_ids: int32 [8, 2048], P('dp'), may hold values from 0 to 15, never falling along the last dimension, each value on 1 to 1024 neighbouring positions
- w_in: float32 [2048, 7, 2048], P('dp', None, 'tensor')
- w_in_m: float32 [2048, 7, 2048], P('dp', None, 'tensor'), may hold values from -0.00024414062 to 0.00024414062
- w_in_v: float32 [2048, 7, 2048], P('dp', None, 'tensor'), may hold values from 1.0490417e-09 to 4.172325e-09
- w_outs: float32 [2048, 5, 2048], P('dp', None, 'tensor')
- w_outs_m: float32 [2048, 5, 2048], P('dp', None, 'tensor'), may hold values from -0.00024414062 to 0.00024414062
- w_outs_v: float32 [2048, 5, 2048], P('dp', None, 'tensor'), may hold values from 1.0490417e-09 to 4.172325e-09
- in_bias: float32 [7, 32, 64], P(None, 'tensor', 'dp'), may hold values from -1.5 to 1.5
- in_bias_m: float32 [7, 32, 64], P(None, 'tensor', 'dp'), may hold values from -0.00024414062 to 0.00024414062
- in_bias_v: float32 [7, 32, 64], P(None, 'tensor', 'dp'), may hold values from 1.0490417e-09 to 4.172325e-09
- vectors: float32 [4, 2048], P(None, 'dp')
- vectors_m: float32 [4, 2048], P(None, 'dp'), may hold values from -0.0009765625 to 0.0009765625
- vectors_v: float32 [4, 2048], P(None, 'dp'), may hold values from 1.66893e-08 to 6.67572e-08
Outputs:
- output: bfloat16 [16384, 2048], P('dp')
- block_input_gradient: bfloat16 [16384, 2048], P('dp')
- grad_norm: float32 [], replicated
- new_w_in: float32 [2048, 7, 2048], P('dp', None, 'tensor')
- new_w_in_m: float32 [2048, 7, 2048], P('dp', None, 'tensor')
- new_w_in_v: float32 [2048, 7, 2048], P('dp', None, 'tensor')
- new_w_outs: float32 [2048, 5, 2048], P('dp', None, 'tensor')
- new_w_outs_m: float32 [2048, 5, 2048], P('dp', None, 'tensor')
- new_w_outs_v: float32 [2048, 5, 2048], P('dp', None, 'tensor')
- new_in_bias: float32 [7, 32, 64], P(None, 'tensor', 'dp')
- new_in_bias_m: float32 [7, 32, 64], P(None, 'tensor', 'dp')
- new_in_bias_v: float32 [7, 32, 64], P(None, 'tensor', 'dp')
- new_vectors: float32 [4, 2048], P(None, 'dp')
- new_vectors_m: float32 [4, 2048], P(None, 'dp')
- new_vectors_v: float32 [4, 2048], P(None, 'dp')
The draws below stay inside these ranges and needn't reach their ends.
Inputs may be any that keep to these rules, and one draw needn't show every extreme that they name: `segment_ids`: along each packed row of 2048 tokens the ids never fall; a document is a run of equal ids within one row.
All inputs are finite; a program needn't handle non-finite values.
Results may differ from the reference program's by a relative error of at most 0.006.
The reference program's roundings to bfloat16 on the way count: a program that leaves them out, or rounds other values in their place, can miss the bound.
Values may be sent and summed in bfloat16 or wider, within the bound.
No kernel may reach another device: no remote copies, remote signals or barrier semaphores. Data moves between devices by JAX's collectives and lax.ppermute only.
A program may use at most 384 MiB of HBM per device.

```python
import math
from functools import partial
import jax
import jax.numpy as jnp
import numpy as np
from jax import lax

D = 2048
HEADS = 32
HDIM = 64
ROT = 32
FF = 8192
SEQ = 2048
STEP = 10
NROWS = 8
TOKENS = 16384


def ramp(count, top):
    return 1.0 + (top - 1.0) * jnp.arange(count, dtype=jnp.float32) / (count - 1)


def base_draw(key, shape):
    return jax.random.normal(key, shape, jnp.float32)


def rise_top():
    return 1.732


def draw_cotangent(key, part):
    top = rise_top()
    scale = ramp(D, top) * (2.0 / (1.0 + top))
    return (base_draw(key, (TOKENS, D)) * scale[None, :]).astype(jnp.bfloat16)


def draw_w_in(key, part):
    slot_scale = jnp.where(jnp.arange(7) < 2, 1.5, 1.0).astype(jnp.float32) / jnp.sqrt(jnp.float32(D))
    return base_draw(key, (D, 7, D)) * slot_scale[None, :, None]


def draw_w_outs(key, part):
    top = rise_top()
    slot_scale = jnp.where(jnp.arange(5) < 1, 4.0 / jnp.sqrt(jnp.float32(D)), 1.0 / jnp.sqrt(jnp.float32(FF))).astype(jnp.float32)
    column_scale = ramp(D, top) * (2.0 / (1.0 + top))
    return base_draw(key, (D, 5, D)) * slot_scale[None, :, None] * column_scale[None, None, :]


def draw_vectors(key, part):
    top = rise_top()
    gain_key = jax.random.fold_in(key, 11)
    rest_key = jax.random.fold_in(key, 12)
    rough = jnp.exp(jax.random.uniform(gain_key, (D,), jnp.float32, -0.35, 0.35))
    norm_gain = 0.7 * ramp(D, top) * rough
    rest = base_draw(rest_key, (3, D)) * jnp.array([0.1, 0.2, 0.2], jnp.float32)[:, None]
    return jnp.concatenate([norm_gain[None, :], rest], 0)


def block_scale(key, shape, split, smallest, largest):
    gain, own = 1.0, jax.random.fold_in(key, 6)
    for axis_at, blocks in split:
        draws = jnp.exp(jax.random.uniform(jax.random.fold_in(own, axis_at), (blocks,), jnp.float32, smallest / len(split), largest / len(split)))
        gain = gain * jnp.repeat(draws, shape[axis_at] // blocks).reshape([-1 if axis == axis_at else 1 for axis in range(len(shape))])
    return gain


def profile(number_of, total, most, skew):
    portions = [(1 << 20) // math.isqrt(rank ** skew) + 1 for rank in range(2, number_of + 1)]
    spare, counts = total - most - (number_of - 1), [1] * (number_of - 1)
    while spare > 0:
        movable = [i for i in range(number_of - 1) if counts[i] < most]
        pool, budget = sum([portions[i] for i in movable]), spare
        for i in movable:
            more = min(most - counts[i], max(1, budget * portions[i] // pool), spare)
            counts[i] = counts[i] + more
            spare = spare - more
    return np.array([most] + counts)


def ragged(key, count, total, most, lean):
    if count == 2:
        one = jax.random.randint(key, (), max(1, total - most), min(most, total - 1) + 1)
        return jnp.stack([one, total - one])
    lengths = jnp.asarray(profile(count, total, most, lean), jnp.int32)
    twos = (count - 1) // 2
    giver, sink = lengths[1:1 + 2 * twos:2], lengths[2:2 + 2 * twos:2]
    margin = jnp.minimum(giver - 1, most - sink)
    shifted = jax.random.randint(jax.random.fold_in(key, 1), (twos,), 0, 1 << 20) % (margin + 1)
    lengths = lengths.at[1:1 + 2 * twos:2].set(giver - shifted).at[2:2 + 2 * twos:2].set(sink + shifted)
    return lengths[jax.random.permutation(jax.random.fold_in(key, 2), count)]


def noise(own_key, extent, deviation, bound, shards=(), kind=jnp.bfloat16):
    gain = block_scale(own_key, extent, shards, -0.22, 0.18) if shards else 1.0
    drawn = jax.random.normal(own_key, extent, jnp.float32) * deviation * gain
    return jnp.minimum(jnp.maximum(drawn, -bound), bound).astype(kind)


def setup_inputs(seed: int = 0) -> dict:
    streams_of = jax.random.split(jax.random.key(seed), 16)
    block_input = noise(streams_of[0], (TOKENS, D), 1.0, 6.0, ((0, 8),))
    cotangent = draw_cotangent(jax.random.fold_in(streams_of[15], 71), 0)
    segment_ids = jax.vmap(lambda own: jnp.searchsorted(jnp.cumsum(ragged(own, max(3, SEQ // 128), SEQ, SEQ // 2, 2)), jnp.arange(SEQ), side="right"))(jax.random.split(streams_of[2], NROWS)).reshape((NROWS, SEQ)).astype(jnp.int32)
    w_in = draw_w_in(jax.random.fold_in(streams_of[15], 71), 0)
    w_in_m = noise(streams_of[4], (D, 7, D), (0.032 / D), 0.00024414062, ((0, 8), (2, 4)), jnp.float32)
    w_in_v = jnp.clip(jnp.exp(math.log(4.172325152040912e-09) - 1.38059635 * jax.random.uniform(streams_of[5], (D, 7, D), jnp.float32) ** block_scale(streams_of[5], (D, 7, D), ((0, 8), (2, 4)), -0.2, 0.2)), 1.0490417423625331e-09, 4.172325152040912e-09)
    w_outs = draw_w_outs(jax.random.fold_in(streams_of[15], 71), 0)
    w_outs_m = noise(streams_of[7], (D, 5, D), (0.032 / D), 0.00024414062, ((0, 8), (2, 4)), jnp.float32)
    w_outs_v = jnp.clip(jnp.exp(math.log(4.172325152040912e-09) - 1.38059635 * jax.random.uniform(streams_of[8], (D, 5, D), jnp.float32) ** block_scale(streams_of[8], (D, 5, D), ((0, 8), (2, 4)), -0.2, 0.2)), 1.0490417423625331e-09, 4.172325152040912e-09)
    in_bias = noise(streams_of[9], (7, HEADS, HDIM), 0.1, 1.5, ((1, 4), (2, 8)), jnp.float32)
    in_bias_m = noise(streams_of[10], (7, HEADS, HDIM), (0.032 / D), 0.00024414062, ((1, 4), (2, 8)), jnp.float32)
    in_bias_v = jnp.clip(jnp.exp(math.log(4.172325152040912e-09) - 1.38059635 * jax.random.uniform(streams_of[11], (7, HEADS, HDIM), jnp.float32) ** block_scale(streams_of[11], (7, HEADS, HDIM), ((1, 4), (2, 8)), -0.2, 0.2)), 1.0490417423625331e-09, 4.172325152040912e-09)
    vectors = draw_vectors(jax.random.fold_in(streams_of[15], 71), 0)
    vectors_m = noise(streams_of[13], (4, D), (0.128 / D), 0.0009765625, ((1, 8),), jnp.float32)
    vectors_v = jnp.clip(jnp.exp(math.log(6.67572024326546e-08) - 1.3862944 * jax.random.uniform(streams_of[14], (4, D), jnp.float32) ** block_scale(streams_of[14], (4, D), ((1, 8),), -0.2, 0.2)), 1.668930060816365e-08, 6.67572024326546e-08)
    return {"block_input": block_input, "cotangent": cotangent, "segment_ids": segment_ids, "w_in": w_in, "w_in_m": w_in_m, "w_in_v": w_in_v, "w_outs": w_outs, "w_outs_m": w_outs_m, "w_outs_v": w_outs_v, "in_bias": in_bias, "in_bias_m": in_bias_m, "in_bias_v": in_bias_v, "vectors": vectors, "vectors_m": vectors_m, "vectors_v": vectors_v}


@jax.custom_vjp
def lowered_weights(v):
    return lax.optimization_barrier(v.astype(jnp.bfloat16)).astype(jnp.float32)

@jax.custom_vjp
def low_back(v):
    return v

def low_keep(v):
    return (lowered_weights(v), None)

def low_pass(kept, grad):
    return (grad,)

def back_keep(v):
    return (v, None)

def back_low(kept, grad):
    return (lowered_weights(grad),)
lowered_weights.defvjp(low_keep, low_pass)
low_back.defvjp(back_keep, back_low)
BETA_ONE = 0.9
BETA_TWO = 0.95
EPSILON = 1e-08
CLIP_AT = 1.0
RATE_MATRIX = 0.06
RATE_VECTOR = 0.6
DECAY_MATRIX = 0.1
HIGHEST = lax.Precision.HIGHEST

def rotate(values, cosines, sines):
    half = cosines.shape[-1]
    first = values[..., :half]
    second = values[..., half:2 * half]
    return jnp.concatenate([first * cosines - second * sines, second * cosines + first * sines, values[..., 2 * half:]], -1)

def angles(seg_row):
    length = seg_row.shape[0]
    place = jnp.arange(length, dtype=jnp.int32)
    boundary = jnp.concatenate([jnp.ones((1,), jnp.bool_), seg_row[1:] != seg_row[:-1]])
    start = lax.cummax(jnp.where(boundary, place, 0), axis=0)
    offset = (place - start).astype(jnp.float32)
    freq = 10000.0 ** (-jnp.arange(ROT // 2, dtype=jnp.float32) * 2.0 / ROT)
    theta = offset[:, None] * freq[None, :]
    return (jnp.cos(theta)[:, None, :], jnp.sin(theta)[:, None, :])

def head_attend(query, keys, vals, allowed):
    raw = jnp.dot(query, keys.T, precision=HIGHEST) * HDIM ** (-0.5)
    scores = jnp.where(allowed, low_back(raw), -1e+30)
    top = lax.optimization_barrier(jnp.max(scores, -1, keepdims=True))
    lse = top + jnp.log(lax.optimization_barrier(jnp.sum(jnp.exp(scores - top), -1, keepdims=True)))
    probs = lowered_weights(jnp.exp(scores - lse))
    return jnp.dot(probs, vals, precision=HIGHEST)

def layer_row(x_row, seg_row, w_in, w_outs, in_bias, vectors):
    row_mean = lax.optimization_barrier(jnp.mean(x_row, -1, keepdims=True))
    centered_rows = x_row - row_mean
    row_variance = lax.optimization_barrier(jnp.mean(centered_rows * centered_rows, -1, keepdims=True))
    standardized_input = centered_rows * lax.rsqrt(row_variance + 1e-05)
    normalized_rows = lowered_weights(standardized_input * vectors[0] + vectors[1])
    z = jnp.dot(normalized_rows, w_in.reshape(D, 7 * D), precision=HIGHEST) + in_bias.reshape(7 * D)
    z = low_back(z).reshape(SEQ, 7, D)
    cosines, sines = angles(seg_row)
    query = lowered_weights(rotate(z[:, 0].reshape(SEQ, HEADS, HDIM), cosines, sines))
    keys = lowered_weights(rotate(z[:, 1].reshape(SEQ, HEADS, HDIM), cosines, sines))
    vals = lowered_weights(z[:, 2].reshape(SEQ, HEADS, HDIM))
    place = jnp.arange(SEQ, dtype=jnp.int32)
    allowed = (seg_row[:, None] == seg_row[None, :]) & (place[:, None] >= place[None, :])
    attend = jax.checkpoint(partial(head_attend, allowed=allowed))
    stacked = (jnp.transpose(query, (1, 0, 2)), jnp.transpose(keys, (1, 0, 2)), jnp.transpose(vals, (1, 0, 2)))
    mixed = lax.map(lambda trio: attend(trio[0], trio[1], trio[2]), stacked)
    attn = jnp.transpose(mixed, (1, 0, 2)).reshape(SEQ, D)
    attn = low_back(lowered_weights(attn))
    hidden = lowered_weights(jax.nn.gelu(z[:, 3:].reshape(SEQ, 4 * D), approximate=True))
    joined = jnp.concatenate([attn, hidden], 1)
    branch = jnp.dot(joined, w_outs.reshape(D, 5 * D).T, precision=HIGHEST)
    return x_row + branch + vectors[2] + vectors[3]

def forward(x_all, segment_ids, w_in, w_outs, in_bias, vectors):
    w_in_low = lowered_weights(w_in)
    w_outs_low = lowered_weights(w_outs)
    bias_low = lowered_weights(in_bias)
    vectors_low = lowered_weights(vectors)

    def step(carry, pair):
        return (carry, layer_row(pair[0], pair[1], w_in_low, w_outs_low, bias_low, vectors_low))
    carry, rows = lax.scan(jax.checkpoint(step), jnp.zeros((), jnp.float32), (x_all.reshape(NROWS, SEQ, D), segment_ids))
    return rows.reshape(TOKENS, D)

def adamw(weight, first, second, grad, factor, rate, decay):
    clipped = grad * factor
    first = BETA_ONE * first + (1.0 - BETA_ONE) * clipped
    second = BETA_TWO * second + (1.0 - BETA_TWO) * clipped * clipped
    first_hat = first / (1.0 - BETA_ONE ** STEP)
    second_hat = second / (1.0 - BETA_TWO ** STEP)
    weight = weight - rate * (first_hat / (jnp.sqrt(second_hat) + EPSILON) + decay * weight)
    return (weight, first, second)

def reference(block_input, cotangent, segment_ids, w_in, w_in_m, w_in_v, w_outs, w_outs_m, w_outs_v, in_bias, in_bias_m, in_bias_v, vectors, vectors_m, vectors_v):
    x_float = block_input.astype(jnp.float32)
    back = cotangent.astype(jnp.float32)

    def whole(a, b, c, d, e):
        return forward(a, segment_ids, b, c, d, e)
    out, pull = jax.vjp(whole, x_float, w_in, w_outs, in_bias, vectors)
    d_x, g_in, g_outs, g_bias, g_vec = pull(back)
    squares = jnp.sum(g_in * g_in) + jnp.sum(g_outs * g_outs) + jnp.sum(g_bias * g_bias) + jnp.sum(g_vec * g_vec)
    grad_norm = jnp.sqrt(squares)
    factor = CLIP_AT / jnp.maximum(grad_norm, CLIP_AT)
    new_in = adamw(w_in, w_in_m, w_in_v, g_in, factor, RATE_MATRIX, DECAY_MATRIX)
    new_outs = adamw(w_outs, w_outs_m, w_outs_v, g_outs, factor, RATE_MATRIX, DECAY_MATRIX)
    new_bias = adamw(in_bias, in_bias_m, in_bias_v, g_bias, factor, RATE_VECTOR, 0.0)
    new_vec = adamw(vectors, vectors_m, vectors_v, g_vec, factor, RATE_VECTOR, 0.0)
    return (out.astype(jnp.bfloat16), d_x.astype(jnp.bfloat16), grad_norm, new_in[0], new_in[1], new_in[2], new_outs[0], new_outs[1], new_outs[2], new_bias[0], new_bias[1], new_bias[2], new_vec[0], new_vec[1], new_vec[2])
```

```python
from functools import partial

import jax
import jax.numpy as jnp
from jax import lax
from jax.experimental import pallas as pl
from jax.experimental.pallas import tpu as pltpu
from jax.sharding import PartitionSpec as P

HDIM = 64
ROT = 32
STEP = 10

BETA_ONE = 0.9
BETA_TWO = 0.95
EPSILON = 1e-08
CLIP_AT = 1.0
RATE_MATRIX = 0.06
RATE_VECTOR = 0.6
DECAY_MATRIX = 0.1

F32 = jnp.float32
BF16 = jnp.bfloat16
LANES = 128
ANY = pl.BlockSpec(memory_space=pl.ANY)
VMEM_LIMIT = 60 * 1024 * 1024


def nn(a, b):
    return lax.dot_general(a, b, (((1,), (0,)), ((), ())), preferred_element_type=F32)


def nt(a, b):
    return lax.dot_general(a, b, (((1,), (1,)), ((), ())), preferred_element_type=F32)


def whole(*shape):
    return pl.BlockSpec(shape, lambda *_: (0,) * len(shape))


def launch(kernel, grid, in_specs, out_specs, out_shape, args, *, scalars=(), scratch=(), flops=0, moved=0, aliases={}):
    return pl.pallas_call(
        kernel,
        grid_spec=pltpu.PrefetchScalarGridSpec(
            num_scalar_prefetch=len(scalars),
            grid=grid,
            in_specs=in_specs,
            out_specs=out_specs,
            scratch_shapes=list(scratch),
        ),
        out_shape=out_shape,
        input_output_aliases=aliases,
        compiler_params=pltpu.CompilerParams(vmem_limit_bytes=VMEM_LIMIT),
        cost_estimate=pl.CostEstimate(flops=int(flops), bytes_accessed=int(moved), transcendentals=0),
    )(*scalars, *args)


def adamw(weight, first, second, grad, factor, rate, decay):
    clipped = grad * factor
    first = BETA_ONE * first + (1.0 - BETA_ONE) * clipped
    second = BETA_TWO * second + (1.0 - BETA_TWO) * clipped * clipped
    first_hat = first / (1.0 - BETA_ONE**STEP)
    second_hat = second / (1.0 - BETA_TWO**STEP)
    weight = weight - rate * (first_hat / (jnp.sqrt(second_hat) + EPSILON) + decay * weight)
    return (weight, first, second)


def load_weights(order_ref, blocks, slots, store, sem, rows, local):
    copies = []
    for r, refs in enumerate(blocks):
        at = pl.ds(pl.multiple_of(order_ref[r] * rows, rows), rows)
        for column, (group, slot) in enumerate(slots):
            copies.append(
                pltpu.make_async_copy(
                    refs[group].at[slot], store.at[at, column * local : (column + 1) * local], sem
                )
            )
    for copy in copies:
        copy.start()
    for copy in copies:
        copy.wait()


def turn(values, table, sign):
    return (
        values * table[0]
        + sign * (pltpu.roll(values, LANES - ROT // 2, 1) * table[1])
        + sign * (pltpu.roll(values, ROT // 2, 1) * table[2])
    )


def cast_group(w_in, w_outs, slots, deps):
    _, rows, local = w_in.shape

    def kernel(*refs):
        ins, out = refs[: len(slots)], refs[-1]
        for i, ref in enumerate(ins):
            out[i] = ref[0].astype(BF16)

    specs = [
        pl.BlockSpec((1, rows, local), lambda i, s=slot: (s, 0, 0)) for _, slot in slots
    ]
    args = [w_in if which == 0 else w_outs for which, _ in slots]
    n = len(slots)
    return launch(
        kernel,
        (1,),
        specs + [ANY] * len(deps),
        whole(n, rows, local),
        jax.ShapeDtypeStruct((n, rows, local), BF16),
        args + list(deps),
        moved=n * rows * local * 6,
    )


def norm_kernel(x_ref, g_ref, vec_ref, normed_ref, normed_t_ref, g_t_ref):
    x = x_ref[...].astype(F32)
    mean = jnp.mean(x, -1, keepdims=True)
    centered = x - mean
    var = jnp.mean(centered * centered, -1, keepdims=True)
    hat = centered * lax.rsqrt(var + 1e-05)
    normed = (hat * vec_ref[0:1, :] + vec_ref[1:2, :]).astype(BF16)
    normed_ref[...] = normed
    normed_t_ref[...] = normed.T
    g_t_ref[...] = g_ref[...].T


def normalize(x, g, vec):
    tokens, width = x.shape
    tile = min(256, tokens)
    row = pl.BlockSpec((tile, width), lambda i: (i, 0))
    col = pl.BlockSpec((width, tile), lambda i: (0, i))
    shape = jax.ShapeDtypeStruct((tokens, width), BF16)
    shape_t = jax.ShapeDtypeStruct((width, tokens), BF16)
    return launch(
        norm_kernel,
        (tokens // tile,),
        [row, row, whole(4, width)],
        (row, col, col),
        (shape, shape_t, shape_t),
        (x, g, vec),
        flops=tokens * width * 10,
        moved=tokens * width * 10,
    )


def qkv_project(order, normed, g, bias, tables, blocks):
    tokens, width = normed.shape
    n_blocks = len(blocks)
    _, rows, local = blocks[0].shape
    tile = min(512, tokens)

    def kernel(order_ref, x_ref, g_ref, bias_ref, table_ref, *rest):
        refs = rest[:n_blocks]
        q_ref, k_ref, v_ref, da_ref, store, sem = rest[n_blocks:]

        @pl.when(pl.program_id(0) == 0)
        def _():
            load_weights(order_ref, [[r] for r in refs], [(0, s) for s in range(4)], store, sem, rows, local)

        x = x_ref[...]
        for slot, out in ((0, q_ref), (1, k_ref)):
            z = nn(x, store[:, slot * local : (slot + 1) * local]) + bias_ref[slot : slot + 1, :]
            for pair in range(local // LANES):
                at = slice(pair * LANES, (pair + 1) * LANES)
                out[:, at] = turn(z[:, at], table_ref, 1.0).astype(BF16)
        v_ref[...] = (nn(x, store[:, 2 * local : 3 * local]) + bias_ref[2:3, :]).astype(BF16)
        da_ref[...] = nn(g_ref[...], store[:, 3 * local : 4 * local]).astype(BF16)

    row = pl.BlockSpec((tile, width), lambda i, *_: (i, 0))
    out = pl.BlockSpec((tile, local), lambda i, *_: (i, 0))
    shape = jax.ShapeDtypeStruct((tokens, local), BF16)
    return launch(
        kernel,
        (tokens // tile,),
        [row, row, whole(7, local), pl.BlockSpec((3, tile, LANES), lambda i, *_: (0, i, 0))] + [ANY] * n_blocks,
        (out,) * 4,
        (shape,) * 4,
        (normed, g, bias, tables, *blocks),
        scalars=(order,),
        scratch=(pltpu.VMEM((width, 4 * local), BF16), pltpu.SemaphoreType.DMA),
        flops=2 * tokens * width * 4 * local,
        moved=tokens * width * 4 + width * local * 8,
    )


def attend(low, query, keys, vals, d_attn, start, tables):
    tokens, local = query.shape
    block = min(256, tokens)
    count = tokens // block
    pairs = local // LANES
    scale = HDIM ** (-0.5)

    def kernel(low_ref, q_ref, k_ref, v_ref, do_ref, start_ref, table_ref, o_ref, dq_ref, dk_ref, dv_ref, db_ref,
               k_half, v_half, k_t, v_t, s_buf, dp_buf, o_t, dq_t, dk_sum, dv_sum):
        i = pl.program_id(1)
        first_lanes = lax.broadcasted_iota(jnp.int32, (1, LANES), 1) < HDIM

        @pl.when(i == 0)
        def _():
            zero = jnp.zeros((), BF16)
            for b in range(count):
                at = slice(b * block, (b + 1) * block)
                for source, half, flipped in ((k_ref, k_half, k_t), (v_ref, v_half, v_t)):
                    part = source[at, :]
                    half[0, at, :] = jnp.where(first_lanes, part, zero)
                    half[1, at, :] = jnp.where(first_lanes, zero, part)
                    flipped[b] = part.T
            dk_sum[...] = jnp.zeros_like(dk_sum)
            dv_sum[...] = jnp.zeros_like(dv_sum)
            db_ref[...] = jnp.zeros_like(db_ref)

        q = q_ref[...]
        do = do_ref[...]
        zero = jnp.zeros((), BF16)
        q_cat = jnp.concatenate([jnp.where(first_lanes, q, zero), jnp.where(first_lanes, zero, q)], 0)
        do_cat = jnp.concatenate([jnp.where(first_lanes, do, zero), jnp.where(first_lanes, zero, do)], 0)
        t_place = i * block + lax.broadcasted_iota(jnp.int32, (1, block), 1)
        t_start = start_ref[...]
        low_block = low_ref[i]
        o_t[...] = jnp.zeros_like(o_t)
        dq_t[...] = jnp.zeros_like(dq_t)

        def score(b, tops):
            at = pl.ds(pl.multiple_of(b * block, block), block)
            u_place = b * block + lax.broadcasted_iota(jnp.int32, (block, 1), 0)
            allowed = (u_place >= t_start) & (u_place <= t_place)
            new = []
            for h in range(2):
                s = jnp.where(allowed, nt(k_half[h, at, :], q) * scale, -1e30)
                s_buf[h, b] = s
                new.append(jnp.maximum(tops[h], jnp.max(s, 0, keepdims=True)))
            return tuple(new)

        lowest = jnp.full((1, block), -jnp.inf, F32)
        tops = lax.fori_loop(low_block, i + 1, score, (lowest, lowest))

        def weigh(b, sums):
            at = pl.ds(pl.multiple_of(b * block, block), block)
            new = []
            for h in range(2):
                p = jnp.exp(s_buf[h, b] - tops[h])
                dp = nt(v_half[h, at, :], do)
                s_buf[h, b] = p
                dp_buf[h, b] = dp
                new.append(sums[2 * h] + jnp.sum(p, 0, keepdims=True))
                new.append(sums[2 * h + 1] + jnp.sum(p * dp, 0, keepdims=True))
            return tuple(new)

        none = jnp.zeros((1, block), F32)
        sums = lax.fori_loop(low_block, i + 1, weigh, (none,) * 4)
        inverse = [1.0 / sums[0], 1.0 / sums[2]]
        delta = [sums[1] * inverse[0], sums[3] * inverse[1]]

        def spread(b, carry):
            at = pl.ds(pl.multiple_of(b * block, block), block)
            probs, grads = [], []
            for h in range(2):
                rows = slice(h * HDIM, (h + 1) * HDIM)
                p = s_buf[h, b] * inverse[h]
                ds = (p * (dp_buf[h, b] - delta[h])).astype(BF16)
                p = p.astype(BF16)
                o_t[rows, :] += nn(v_t[b, rows, :], p)
                dq_t[rows, :] += nn(k_t[b, rows, :], ds)
                probs.append(p)
                grads.append(ds)
            dv_sum[at, :] += nn(jnp.concatenate(probs, 1), do_cat)
            dk_sum[at, :] += nn(jnp.concatenate(grads, 1), q_cat)
            return carry

        lax.fori_loop(low_block, i + 1, spread, 0)
        o_ref[...] = o_t[...].T.astype(BF16)
        here = pl.ds(pl.multiple_of(i * block, block), block)
        dq = turn(dq_t[...].T * scale, [table_ref[n, here, :] for n in range(3)], -1.0).astype(BF16)
        dq_ref[...] = dq
        db_ref[0:1, :] += jnp.sum(dq.astype(F32), 0, keepdims=True)

        @pl.when(i == count - 1)
        def _():
            dk = turn(dk_sum[...] * scale, table_ref, -1.0).astype(BF16)
            dv = dv_sum[...].astype(BF16)
            dk_ref[...] = dk
            dv_ref[...] = dv
            db_ref[1:2, :] = jnp.sum(dk.astype(F32), 0, keepdims=True)
            db_ref[2:3, :] = jnp.sum(dv.astype(F32), 0, keepdims=True)

    part = pl.BlockSpec((block, LANES), lambda p, i, *_: (i, p))
    column = pl.BlockSpec((tokens, LANES), lambda p, i, *_: (0, p))
    shape = jax.ShapeDtypeStruct((tokens, local), BF16)
    return launch(
        kernel,
        (pairs, count),
        [
            part,
            column,
            column,
            part,
            pl.BlockSpec((1, block), lambda p, i, *_: (0, i)),
            whole(3, tokens, LANES),
        ],
        (part, part, column, column, pl.BlockSpec((3, LANES), lambda p, i, *_: (0, p))),
        (shape,) * 4 + (jax.ShapeDtypeStruct((3, local), F32),),
        (query, keys, vals, d_attn, start, tables),
        scalars=(low,),
        scratch=(
            pltpu.VMEM((2, tokens, LANES), BF16),
            pltpu.VMEM((2, tokens, LANES), BF16),
            pltpu.VMEM((count, LANES, block), BF16),
            pltpu.VMEM((count, LANES, block), BF16),
            pltpu.VMEM((2, count, block, block), F32),
            pltpu.VMEM((2, count, block, block), F32),
            pltpu.VMEM((LANES, block), F32),
            pltpu.VMEM((LANES, block), F32),
            pltpu.VMEM((tokens, LANES), F32),
            pltpu.VMEM((tokens, LANES), F32),
        ),
        flops=tokens * tokens * local * 24,
        moved=tokens * local * 20,
    )


def hidden_slot(order, normed, g, bias, blocks):
    tokens, width = normed.shape
    n_blocks = len(blocks)
    _, rows, local = blocks[0].shape
    tile = min(512, tokens)

    def kernel(order_ref, x_ref, g_ref, bias_ref, *rest):
        refs = rest[:n_blocks]
        h_ref, dz_ref, db_ref, store, sem = rest[n_blocks:]

        @pl.when(pl.program_id(0) == 0)
        def _():
            load_weights(order_ref, [[r] for r in refs], [(0, 0), (0, 1)], store, sem, rows, local)
            db_ref[...] = jnp.zeros_like(db_ref)

        v = nn(x_ref[...], store[:, :local]) + bias_ref[...]
        dh = nn(g_ref[...], store[:, local:])
        square = v * v
        t = jnp.tanh(0.7978845608 * (v + 0.044715 * (square * v)))
        half = 0.5 * (1.0 + t)
        h_ref[...] = (v * half).astype(BF16)
        slope = half + (0.5 * v) * (1.0 - t * t) * (0.7978845608 + (3.0 * 0.044715 * 0.7978845608) * square)
        dz = (dh * slope).astype(BF16)
        dz_ref[...] = dz
        db_ref[...] += jnp.sum(dz.astype(F32), 0, keepdims=True)

    row = pl.BlockSpec((tile, width), lambda i, *_: (i, 0))
    out = pl.BlockSpec((tile, local), lambda i, *_: (i, 0))
    shape = jax.ShapeDtypeStruct((tokens, local), BF16)
    return launch(
        kernel,
        (tokens // tile,),
        [row, row, whole(1, local)] + [ANY] * n_blocks,
        (out, out, whole(1, local)),
        (shape, shape, jax.ShapeDtypeStruct((1, local), F32)),
        (normed, g, bias, *blocks),
        scalars=(order,),
        scratch=(pltpu.VMEM((width, 2 * local), BF16), pltpu.SemaphoreType.DMA),
        flops=4 * tokens * width * local,
        moved=tokens * width * 4 + width * local * 4,
    )


def grad_blocks(dest, normed_t, g_t, sides, received, split):
    width, tokens = normed_t.shape
    count = dest.shape[0]
    n = len(sides)
    local = sides[0][1].shape[1]
    rows = width // (lax.axis_size("dp"))

    def kernel(dest_ref, x_ref, g_ref, *rest):
        rights = rest[:n]
        adds = rest[n : n + len(received)]
        outs = rest[n + len(received) :]
        step = pl.program_id(0)
        for i, (left, _) in enumerate(sides):
            total = nn((x_ref if left == 0 else g_ref)[...], rights[i][...])
            for add in adds:
                total += add[0, i].astype(F32)
            if not split:
                outs[0][0, i] = total.astype(BF16)
            else:
                for j, out in enumerate(outs):

                    @pl.when(step == j)
                    def _(out=out, total=total, i=i):
                        out[i] = total.astype(out.dtype)

    left = pl.BlockSpec((rows, tokens), lambda i, dest_ref: (dest_ref[i], 0))
    piece = pl.BlockSpec((1, n, rows, local), lambda i, *_: (i, 0, 0, 0))
    if split:
        out_specs = (whole(n, rows, local),) * count
        out_shape = tuple(
            jax.ShapeDtypeStruct((n, rows, local), F32 if j == 0 else BF16) for j in range(count)
        )
    else:
        out_specs = piece
        out_shape = jax.ShapeDtypeStruct((count, n, rows, local), BF16)
    return launch(
        kernel,
        (count,),
        [left, left] + [whole(tokens, local)] * n + [piece] * len(received),
        out_specs,
        out_shape,
        (normed_t, g_t, *[right for _, right in sides], *received),
        scalars=(dest,),
        flops=2 * count * rows * tokens * n * local,
        moved=count * rows * tokens * 4 + n * tokens * local * 2 + count * n * rows * local * 2,
    )


def project_back(order, shares, lefts, groups, slots, received, split):
    tokens, local = lefts[0].shape
    count = shares.shape[0]
    share = tokens // lax.axis_size("tensor")
    tile = min(256, share)
    steps = share // tile
    n_blocks = len(groups)
    n_groups = len(groups[0])
    rows = groups[0][0].shape[1]
    width = rows * n_blocks
    m = len(lefts)
    flat = [ref for refs in groups for ref in refs]

    def kernel(order_ref, shares_ref, *rest):
        left_refs = rest[:m]
        refs = rest[m : m + len(flat)]
        adds = rest[m + len(flat) : m + len(flat) + len(received)]
        outs = rest[m + len(flat) + len(received) : -2]
        store, sem = rest[-2:]
        step, part = pl.program_id(0), pl.program_id(1)

        @pl.when((step == 0) & (part == 0))
        def _():
            nested = [refs[r * n_groups : (r + 1) * n_groups] for r in range(n_blocks)]
            load_weights(order_ref, nested, slots, store, sem, rows, local)

        total = nt(jnp.concatenate([left[...] for left in left_refs], 1), store[...])
        for add in adds:
            total += add[...].astype(F32)
        if not split:
            outs[0][...] = total.astype(BF16)
        else:
            at = pl.ds(pl.multiple_of(part * tile, tile), tile)
            for j, out in enumerate(outs):

                @pl.when(step == j)
                def _(out=out):
                    out[at, :] = total.astype(out.dtype)

    left = pl.BlockSpec((tile, local), lambda i, j, o_ref, s_ref: (s_ref[i] * steps + j, 0))
    piece = pl.BlockSpec((tile, width), lambda i, j, *_: (i * steps + j, 0))
    if split:
        out_specs = (whole(share, width),) * count
        out_shape = tuple(jax.ShapeDtypeStruct((share, width), F32 if j == 0 else BF16) for j in range(count))
    else:
        out_specs = piece
        out_shape = jax.ShapeDtypeStruct((count * share, width), BF16)
    return launch(
        kernel,
        (count, steps),
        [left] * m + [ANY] * len(flat) + [piece] * len(received),
        out_specs,
        out_shape,
        (*lefts, *flat, *received),
        scalars=(order, shares),
        scratch=(pltpu.VMEM((width, m * local), BF16), pltpu.SemaphoreType.DMA),
        flops=2 * count * share * width * m * local,
        moved=width * m * local * 2 + count * share * (m * local + width) * 2,
    )


def finish_output(mine, own, received, x, vec):
    share, width = own.shape
    tile = min(256, share)
    steps = share // tile

    def kernel(mine_ref, own_ref, x_ref, vec_ref, *rest):
        total = own_ref[...]
        for ref in rest[:-1]:
            total += ref[...].astype(F32)
        rest[-1][...] = (x_ref[...].astype(F32) + total + vec_ref[2:3, :] + vec_ref[3:4, :]).astype(BF16)

    row = pl.BlockSpec((tile, width), lambda i, *_: (i, 0))
    far = pl.BlockSpec((tile, width), lambda i, mine_ref: (mine_ref[0] * steps + i, 0))
    return launch(
        kernel,
        (steps,),
        [row, far, whole(4, width)] + [row] * len(received),
        row,
        jax.ShapeDtypeStruct((share, width), BF16),
        (own, x, vec, *received),
        scalars=(mine,),
        moved=share * width * 10,
    )


def finish_input(mine, own, received, x, g, vec):
    share, width = own.shape
    tile = min(256, share)
    steps = share // tile

    def kernel(mine_ref, own_ref, x_ref, g_ref, vec_ref, *rest):
        grad_ref, rows_ref = rest[-2:]
        dn = own_ref[...]
        for ref in rest[:-2]:
            dn += ref[...].astype(F32)
        x = x_ref[...].astype(F32)
        g = g_ref[...].astype(F32)
        mean = jnp.mean(x, -1, keepdims=True)
        centered = x - mean
        var = jnp.mean(centered * centered, -1, keepdims=True)
        inverse = lax.rsqrt(var + 1e-05)
        hat = centered * inverse
        e = dn * vec_ref[0:1, :]
        back = inverse * (e - jnp.mean(e, -1, keepdims=True) - hat * jnp.mean(e * hat, -1, keepdims=True))
        grad_ref[...] = (g + back).astype(BF16)

        @pl.when(pl.program_id(0) == 0)
        def _():
            rows_ref[...] = jnp.zeros_like(rows_ref)

        rows_ref[0:1, :] += jnp.sum(dn * hat, 0, keepdims=True)
        rows_ref[1:2, :] += jnp.sum(dn, 0, keepdims=True)
        rows_ref[2:3, :] += jnp.sum(g, 0, keepdims=True)

    row = pl.BlockSpec((tile, width), lambda i, *_: (i, 0))
    far = pl.BlockSpec((tile, width), lambda i, mine_ref: (mine_ref[0] * steps + i, 0))
    return launch(
        kernel,
        (steps,),
        [row, far, far, whole(4, width)] + [row] * len(received),
        (row, whole(3, width)),
        (jax.ShapeDtypeStruct((share, width), BF16), jax.ShapeDtypeStruct((3, width), F32)),
        (own, x, g, vec, *received),
        scalars=(mine,),
        moved=share * width * 12,
    )


def lay_out(order, parts):
    share, width = parts[0].shape
    count = len(parts)
    tile = min(256, share)
    steps = share // tile

    def kernel(order_ref, *rest):
        for r in range(count):

            @pl.when(pl.program_id(0) == r)
            def _(r=r):
                rest[count][...] = rest[r][...]

    def fetch(r):
        return pl.BlockSpec(
            (tile, width), lambda i, j, *_: (jnp.where(i == r, j, jnp.where(i < r, 0, steps - 1)), 0)
        )

    return launch(
        kernel,
        (count, steps),
        [fetch(r) for r in range(count)],
        pl.BlockSpec((tile, width), lambda i, j, order_ref: (order_ref[i] * steps + j, 0)),
        jax.ShapeDtypeStruct((share * count, width), parts[0].dtype),
        parts,
        scalars=(order,),
        moved=share * count * width * 4,
    )


def total_group(grads, own, received, places, slots_in_all):
    n, rows, local = own.shape

    def kernel(places_ref, own_ref, *rest):
        out, squares = rest[-2:]
        total = own_ref[0]
        for ref in rest[: len(received)]:
            total += ref[0].astype(F32)
        out[0] = total

        @pl.when(pl.program_id(0) == 0)
        def _():
            squares[...] = jnp.zeros_like(squares)

        squares[...] += jnp.sum(total * total, 0, keepdims=True)

    piece = pl.BlockSpec((1, rows, local), lambda i, *_: (i, 0, 0))
    out = pl.BlockSpec((1, rows, local), lambda i, places_ref: (places_ref[i], 0, 0))
    first = grads is None
    return launch(
        kernel,
        (n,),
        [piece] * (1 + len(received)) + ([] if first else [ANY]),
        (out, whole(1, local)),
        (jax.ShapeDtypeStruct((slots_in_all, rows, local), F32), jax.ShapeDtypeStruct((1, local), F32)),
        (own, *received) + (() if first else (grads,)),
        scalars=(places,),
        aliases={} if first else {2 + len(received): 0},
        moved=n * rows * local * 14,
    )


def double_up(values, axis, count):
    me = lax.axis_index(axis)
    bit = 1
    while bit < count:
        other = lax.ppermute(values, axis, [(i, i ^ bit) for i in range(count)])
        high = (me & bit) != 0
        values = jnp.where(high, jnp.concatenate([other, values], 0), jnp.concatenate([values, other], 0))
        bit *= 2
    return values


def total_over(values, axis, count):
    bit = 1
    while bit < count:
        values = values + lax.ppermute(values, axis, [(i, i ^ bit) for i in range(count)])
        bit *= 2
    return values


def shift(values, axis, count, inner, outer_by, inner_by):
    outer = count // inner
    pairs = [
        (o * inner + i, (o + outer_by) % outer * inner + (i + inner_by) % inner)
        for o in range(outer)
        for i in range(inner)
    ]
    return lax.ppermute(values, axis, pairs)


def body(
    block_input,
    cotangent,
    segment_ids,
    w_in,
    w_in_m,
    w_in_v,
    w_outs,
    w_outs_m,
    w_outs_v,
    in_bias,
    in_bias_m,
    in_bias_v,
    vectors,
    vectors_m,
    vectors_v,
):
    n_dp = lax.axis_size("dp")
    n_tensor = lax.axis_size("tensor")
    inner = 2 if n_dp <= 8 else 4
    outer = n_dp // inner
    cores = 2
    ways = n_tensor // cores
    me = lax.axis_index("dp")
    mine = lax.axis_index("tensor")
    my_outer, my_inner = me // inner, me % inner
    my_way, my_core = mine // cores, mine % cores
    tokens, width = block_input.shape
    _, slots_in, local = w_in.shape
    slots_out = w_outs.shape[1]
    hidden_slots = slots_out - 1

    def numbers(values):
        return jnp.stack([jnp.asarray(v, jnp.int32) for v in values])

    order = numbers(
        [
            (my_outer - o) % outer * inner + (my_inner - i) % inner
            for o in range(outer)
            for i in range(inner)
        ]
    )
    dests = [
        numbers([(my_outer + o) % outer * inner + (my_inner + i) % inner for o in range(outer)])
        for i in range(inner)
    ]
    share_order = numbers(
        [(my_way - w) % ways * cores + (my_core - c) % cores for w in range(ways) for c in range(cores)]
    )
    share_dests = [
        numbers([(my_way + w) % ways * cores + (my_core + c) % cores for w in range(ways)])
        for c in range(cores)
    ]
    share_mine = numbers([mine])

    w_in_s = w_in.transpose(1, 0, 2)
    w_outs_s = w_outs.transpose(1, 0, 2)

    def gather(own):
        blocks = []
        held = [own] + [shift(own, "dp", n_dp, inner, o, 0) for o in range(1, outer)]
        for part in held:
            blocks.append(part)
            for i in range(1, inner):
                blocks.append(shift(part, "dp", n_dp, inner, 0, i))
        return blocks

    first_slots = [(0, 0), (0, 1), (0, 2), (1, 0)]
    group_slots = [first_slots] + [[(0, 3 + s), (1, 1 + s)] for s in range(hidden_slots)]

    small = jnp.concatenate([in_bias.reshape(1, -1), vectors.reshape(1, -1)], 1).astype(BF16).astype(F32)
    small = double_up(small, "dp", n_dp)
    bias_size = in_bias.size
    bias = small[:, :bias_size].reshape((n_dp,) + in_bias.shape).transpose(1, 2, 0, 3).reshape(slots_in, local)
    vec = small[:, bias_size:].reshape((n_dp,) + vectors.shape).transpose(1, 0, 2).reshape(4, width)

    groups = []
    for g, slots in enumerate(group_slots):
        deps = groups[g - 2][-1:] if g >= 2 else []
        groups.append(gather(cast_group(w_in_s, w_outs_s, slots, deps)))

    seg = segment_ids[0]
    start = jnp.sum((seg[None, :] < seg[:, None]).astype(jnp.int32), 1)
    block = min(256, tokens)
    low = start[::block] // block
    place = (jnp.arange(tokens, dtype=jnp.int32) - start).astype(F32)
    freq = 10000.0 ** (-jnp.arange(ROT // 2, dtype=F32) * 2.0 / ROT)
    theta = place[:, None] * freq[None, :]
    cosine, sine = jnp.cos(theta), jnp.sin(theta)
    rest = jnp.zeros((tokens, HDIM - ROT), F32)
    none = jnp.zeros_like(sine)
    tables = jnp.stack(
        [
            jnp.concatenate([cosine, cosine, rest + 1.0] * 2, 1),
            jnp.concatenate([-sine, none, rest] * 2, 1),
            jnp.concatenate([none, sine, rest] * 2, 1),
        ]
    )

    normed, normed_t, g_t = normalize(block_input, cotangent, vec)

    query, keys, vals, d_attn = qkv_project(order, normed, cotangent, bias, tables, groups[0])
    attn, d_query, d_keys, d_vals, d_bias_attn = attend(
        low, query, keys, vals, d_attn, start.reshape(1, tokens), tables
    )

    def send_back(sides):
        received = []
        for i in range(1, inner):
            out = grad_blocks(dests[i], normed_t, g_t, sides, [], False)
            received.append(shift(out, "dp", n_dp, inner, 0, i))
        outs = grad_blocks(dests[0], normed_t, g_t, sides, received, True)
        return outs[0], [shift(outs[o], "dp", n_dp, inner, o, 0) for o in range(1, outer)]

    hidden, d_hidden, d_bias_hidden = [], [], []
    shares = [send_back([(0, d_query), (0, d_keys), (0, d_vals), (1, attn)])]
    for s in range(hidden_slots):
        h, dz, db = hidden_slot(order, normed, cotangent, bias[3 + s : 4 + s], groups[1 + s])
        hidden.append(h)
        d_hidden.append(dz)
        d_bias_hidden.append(db)
        shares.append(send_back([(0, dz), (1, h)]))

    by_owner = [[group[r] for group in groups] for r in range(n_dp)]

    def sum_tensor(lefts, slots):
        received = []
        for c in range(1, cores):
            out = project_back(order, share_dests[c], lefts, by_owner, slots, [], False)
            received.append(shift(out, "tensor", n_tensor, cores, 0, c))
        outs = project_back(order, share_dests[0], lefts, by_owner, slots, received, True)
        return outs[0], [shift(outs[w], "tensor", n_tensor, cores, w, 0) for w in range(1, ways)]

    def gather_tensor(own):
        parts = []
        held = [own] + [shift(own, "tensor", n_tensor, cores, w, 0) for w in range(1, ways)]
        for part in held:
            parts.append(part)
            for c in range(1, cores):
                parts.append(shift(part, "tensor", n_tensor, cores, 0, c))
        return lay_out(share_order, parts)

    own, received = sum_tensor(
        [d_query, d_keys, d_vals] + d_hidden, [(0, 0), (0, 1), (0, 2)] + [(1 + s, 0) for s in range(hidden_slots)]
    )
    d_x, vector_rows = finish_input(share_mine, own, received, block_input, cotangent, vec)
    block_input_gradient = gather_tensor(d_x)

    own, received = sum_tensor([attn] + hidden, [(0, 3)] + [(1 + s, 1) for s in range(hidden_slots)])
    output = gather_tensor(finish_output(share_mine, own, received, block_input, vec))

    vector_rows = total_over(vector_rows.reshape(1, -1), "tensor", n_tensor)
    d_bias = jnp.concatenate([d_bias_attn] + d_bias_hidden, 0)
    small = total_over(jnp.concatenate([d_bias.reshape(1, -1), vector_rows], 1), "dp", n_dp)
    g_bias = lax.dynamic_index_in_dim(
        small[0, : slots_in * local].reshape(slots_in, in_bias.shape[1], n_dp, in_bias.shape[2]), me, 2, False
    )
    g_vec = lax.dynamic_index_in_dim(small[0, slots_in * local :].reshape(3, n_dp, width // n_dp), me, 1, False)
    g_vec = jnp.concatenate([g_vec, g_vec[2:]], 0)

    grads, squares = None, []
    for slots, (own, received) in zip(group_slots, shares):
        places = jnp.asarray([s if which == 0 else slots_in + s for which, s in slots], jnp.int32)
        grads, part = total_group(grads, own, received, places, slots_in + slots_out)
        squares.append(part)
    g_in, g_outs = grads[:slots_in], grads[slots_in:]
    local_squares = (
        jnp.sum(jnp.concatenate(squares, 0)) + jnp.sum(g_bias * g_bias) + jnp.sum(g_vec * g_vec) * (1.0 / n_tensor)
    )
    local_squares = total_over(jnp.full((1, LANES), local_squares), "tensor", n_tensor)
    local_squares = total_over(local_squares, "dp", n_dp)
    grad_norm = jnp.sqrt(local_squares[0, 0])
    factor = CLIP_AT / jnp.maximum(grad_norm, CLIP_AT)

    def slot_major(*arrays):
        return [a.transpose(1, 0, 2) for a in arrays]

    new_in = slot_major(*adamw(w_in_s, *slot_major(w_in_m, w_in_v), g_in, factor, RATE_MATRIX, DECAY_MATRIX))
    new_outs = slot_major(*adamw(w_outs_s, *slot_major(w_outs_m, w_outs_v), g_outs, factor, RATE_MATRIX, DECAY_MATRIX))
    new_bias = adamw(in_bias, in_bias_m, in_bias_v, g_bias, factor, RATE_VECTOR, 0.0)
    new_vec = adamw(vectors, vectors_m, vectors_v, g_vec, factor, RATE_VECTOR, 0.0)
    return (output, block_input_gradient, grad_norm, *new_in, *new_outs, *new_bias, *new_vec)


def solution(mesh):
    rows = P("dp", None)
    matrix = P("dp", None, "tensor")
    small = P(None, "tensor", "dp")
    vector = P(None, "dp")
    return jax.shard_map(
        body,
        mesh=mesh,
        in_specs=(rows,) * 3 + (matrix,) * 6 + (small,) * 3 + (vector,) * 3,
        out_specs=(rows, rows, P()) + (matrix,) * 6 + (small,) * 3 + (vector,) * 3,
        check_vma=False,
    )
```

```python
import jax
import jax.numpy as jnp
from jax import lax
from jax.experimental import pallas as pl
from jax.experimental.pallas import tpu as pltpu
from jax.sharding import PartitionSpec as P

HDIM = 64
ROT = 32
STEP = 10

BETA_ONE = 0.9
BETA_TWO = 0.95
EPSILON = 1e-08
CLIP_AT = 1.0
RATE_MATRIX = 0.06
RATE_VECTOR = 0.6
DECAY_MATRIX = 0.1

F32 = jnp.float32
BF16 = jnp.bfloat16
LANES = 128
ANY = pl.BlockSpec(memory_space=pltpu.HBM)
VMEM_LIMIT = 60 * 1024 * 1024


def nn(a, b):
    return lax.dot_general(a, b, (((1,), (0,)), ((), ())), preferred_element_type=F32)


def nt(a, b):
    return lax.dot_general(a, b, (((1,), (1,)), ((), ())), preferred_element_type=F32)


def whole(*shape):
    return pl.BlockSpec(shape, lambda *_: (0,) * len(shape))


class Line:
    def __init__(self):
        self.last = ()


LINE = Line()


def launch(kernel, grid, in_specs, out_specs, out_shape, args, *, scalars=(), scratch=(), flops=0, moved=0, aliases={}, after=(), weight=1):
    extra = len(after)
    ahead = len(scalars) + len(args)

    def trimmed(*refs):
        return kernel(*refs[:ahead], *refs[ahead + extra :])

    return pl.pallas_call(
        trimmed,
        grid_spec=pltpu.PrefetchScalarGridSpec(
            num_scalar_prefetch=len(scalars),
            grid=grid,
            in_specs=list(in_specs) + [ANY] * extra,
            out_specs=out_specs,
            scratch_shapes=list(scratch),
        ),
        out_shape=out_shape,
        input_output_aliases=aliases,
        compiler_params=pltpu.CompilerParams(vmem_limit_bytes=VMEM_LIMIT),
        cost_estimate=pl.CostEstimate(flops=200000000 * weight, bytes_accessed=1, transcendentals=0),
    )(*scalars, *args, *after)


def in_line(call, *args, **more):
    out = call(*args, after=LINE.last, **more)
    LINE.last = (out[-1] if isinstance(out, (tuple, list)) else out,)
    return out


def gate(*arrays, weight=1):
    n = len(arrays)

    def kernel(*refs):
        pass

    out = in_line(
        launch,
        kernel,
        (1,),
        [ANY] * n,
        (ANY,) * n,
        tuple(jax.ShapeDtypeStruct(a.shape, a.dtype) for a in arrays),
        arrays,
        aliases={i: i for i in range(n)},
        weight=weight,
    )
    return list(out)


def adamw(weight, first, second, grad, factor, rate, decay):
    clipped = grad * factor
    first = BETA_ONE * first + (1.0 - BETA_ONE) * clipped
    second = BETA_TWO * second + (1.0 - BETA_TWO) * clipped * clipped
    first_hat = first / (1.0 - BETA_ONE**STEP)
    second_hat = second / (1.0 - BETA_TWO**STEP)
    weight = weight - rate * (first_hat / (jnp.sqrt(second_hat) + EPSILON) + decay * weight)
    return (weight, first, second)


def load_weights(place_ref, groups, slots, store, sem):
    copies = []
    for column, (group, slot) in enumerate(slots):
        at = 0
        for part in groups[group]:
            owners, _, rows, local = part.shape
            for r in range(owners):
                to = pl.ds(pl.multiple_of(place_ref[at] * rows, rows), rows)
                copies.append(
                    pltpu.make_async_copy(
                        part.at[r, slot], store.at[to, column * local : (column + 1) * local], sem
                    )
                )
                at += 1
    for copy in copies:
        copy.start()
    for copy in copies:
        copy.wait()


def turn(values, table, sign):
    return (
        values * table[0]
        + sign * (pltpu.roll(values, LANES - ROT // 2, 1) * table[1])
        + sign * (pltpu.roll(values, ROT // 2, 1) * table[2])
    )


def cast_group(w_in, w_outs, slots, deps):
    _, rows, local = w_in.shape

    def kernel(*refs):
        ins, out = refs[: len(slots)], refs[-1]
        for i, ref in enumerate(ins):
            out[i] = ref[0].astype(BF16)

    specs = [
        pl.BlockSpec((1, rows, local), lambda i, s=slot: (s, 0, 0)) for _, slot in slots
    ]
    args = [w_in if which == 0 else w_outs for which, _ in slots]
    n = len(slots)
    return launch(
        kernel,
        (1,),
        specs,
        whole(n, rows, local),
        jax.ShapeDtypeStruct((n, rows, local), BF16),
        args,
        moved=n * rows * local * 6,
        after=deps,
    )


def norm_kernel(x_ref, g_ref, vec_ref, normed_ref, normed_t_ref, g_t_ref):
    x = x_ref[...].astype(F32)
    mean = jnp.mean(x, -1, keepdims=True)
    centered = x - mean
    var = jnp.mean(centered * centered, -1, keepdims=True)
    hat = centered * lax.rsqrt(var + 1e-05)
    normed = (hat * vec_ref[0:1, :] + vec_ref[1:2, :]).astype(BF16)
    normed_ref[...] = normed
    normed_t_ref[...] = normed.T
    g_t_ref[...] = g_ref[...].T


def normalize(x, g, vec, after=()):
    tokens, width = x.shape
    tile = min(256, tokens)
    row = pl.BlockSpec((tile, width), lambda i: (i, 0))
    col = pl.BlockSpec((width, tile), lambda i: (0, i))
    shape = jax.ShapeDtypeStruct((tokens, width), BF16)
    shape_t = jax.ShapeDtypeStruct((width, tokens), BF16)
    return launch(
        norm_kernel,
        (tokens // tile,),
        [row, row, whole(4, width)],
        (row, col, col),
        (shape, shape_t, shape_t),
        (x, g, vec),
        flops=tokens * width * 10,
        moved=tokens * width * 10,
        after=after,
    )


def qkv_project(places, normed, g, bias, tables, groups, slots, after=()):
    tokens, width = normed.shape
    local = groups[0][0].shape[3]
    flat = [part for group in groups for part in group]
    cut = len(groups[0])
    tile = min(512, tokens)

    def kernel(place_ref, x_ref, g_ref, bias_ref, table_ref, *rest):
        parts, (q_ref, k_ref, v_ref, da_ref, store, sem) = rest[:-6], rest[-6:]

        @pl.when(pl.program_id(0) == 0)
        def _():
            nested = [parts[k : k + cut] for k in range(0, len(flat), cut)]
            load_weights(place_ref, nested, slots, store, sem)

        x = x_ref[...]
        for slot, out, scale in ((0, q_ref, HDIM ** (-0.5)), (1, k_ref, 1.0)):
            z = nn(x, store[:, slot * local : (slot + 1) * local]) + bias_ref[slot : slot + 1, :]
            for pair in range(local // LANES):
                at = slice(pair * LANES, (pair + 1) * LANES)
                out[:, at] = (turn(z[:, at], table_ref, 1.0) * scale).astype(BF16)
        v_ref[...] = (nn(x, store[:, 2 * local : 3 * local]) + bias_ref[2:3, :]).astype(BF16)
        da_ref[...] = nn(g_ref[...], store[:, 3 * local : 4 * local]).astype(BF16)

    row = pl.BlockSpec((tile, width), lambda i, *_: (i, 0))
    out = pl.BlockSpec((tile, local), lambda i, *_: (i, 0))
    shape = jax.ShapeDtypeStruct((tokens, local), BF16)
    return launch(
        kernel,
        (tokens // tile,),
        [row, row, whole(7, local), pl.BlockSpec((3, tile, LANES), lambda i, *_: (0, i, 0))] + [ANY] * len(flat),
        (out,) * 4,
        (shape,) * 4,
        (normed, g, bias, tables, *flat),
        scalars=(places,),
        scratch=(pltpu.VMEM((width, 4 * local), BF16), pltpu.SemaphoreType.DMA),
        flops=2 * tokens * width * 4 * local,
        moved=tokens * width * 4 + width * local * 8,
        after=after,
    )


def attend(first, pairs, held, low, query, keys, vals, d_attn, start, tables, after=()):
    tokens, local = query.shape
    block = min(256, tokens)
    count = tokens // block
    scale = HDIM ** (-0.5)

    def kernel(low_ref, q_ref, k_ref, v_ref, do_ref, start_ref, table_ref, *rest):
        (o_ref, dq_ref, dk_ref, dv_ref, db_ref,
               k_half, v_half, k_t, v_t, s_buf, dp_buf, o_t, dq_t, dk_sum, dv_sum) = rest[len(held):]
        i = pl.program_id(1)
        first_lanes = lax.broadcasted_iota(jnp.int32, (1, LANES), 1) < HDIM

        @pl.when(i == 0)
        def _():
            zero = jnp.zeros((), BF16)
            for b in range(count):
                at = slice(b * block, (b + 1) * block)
                for source, half, flipped in ((k_ref, k_half, k_t), (v_ref, v_half, v_t)):
                    part = source[at, :]
                    half[0, at, :] = jnp.where(first_lanes, part, zero)
                    half[1, at, :] = jnp.where(first_lanes, zero, part)
                    flipped[b] = part.T
            dk_sum[...] = jnp.zeros_like(dk_sum)
            dv_sum[...] = jnp.zeros_like(dv_sum)
            db_ref[...] = jnp.zeros_like(db_ref)

        q = q_ref[...]
        do = do_ref[...]
        zero = jnp.zeros((), BF16)
        q_cat = jnp.concatenate([jnp.where(first_lanes, q, zero), jnp.where(first_lanes, zero, q)], 0)
        do_cat = jnp.concatenate([jnp.where(first_lanes, do, zero), jnp.where(first_lanes, zero, do)], 0)
        t_place = i * block + lax.broadcasted_iota(jnp.int32, (1, block), 1)
        t_start = start_ref[...]
        low_block = low_ref[i]
        o_t[...] = jnp.zeros_like(o_t)
        dq_t[...] = jnp.zeros_like(dq_t)

        def score(b, tops):
            at = pl.ds(pl.multiple_of(b * block, block), block)
            u_place = b * block + lax.broadcasted_iota(jnp.int32, (block, 1), 0)
            allowed = (u_place >= t_start) & (u_place <= t_place)
            new = []
            for h in range(2):
                s = jnp.where(allowed, nt(k_half[h, at, :], q), -1e30)
                s_buf[h, b] = s
                new.append(jnp.maximum(tops[h], jnp.max(s, 0, keepdims=True)))
            return tuple(new)

        lowest = jnp.full((1, block), -jnp.inf, F32)
        tops = lax.fori_loop(low_block, i + 1, score, (lowest, lowest))

        def weigh(b, sums):
            at = pl.ds(pl.multiple_of(b * block, block), block)
            new = []
            for h in range(2):
                p = jnp.exp(s_buf[h, b] - tops[h])
                dp = nt(v_half[h, at, :], do)
                s_buf[h, b] = p
                dp_buf[h, b] = dp
                new.append(sums[2 * h] + jnp.sum(p, 0, keepdims=True))
                new.append(sums[2 * h + 1] + jnp.sum(p * dp, 0, keepdims=True))
            return tuple(new)

        none = jnp.zeros((1, block), F32)
        sums = lax.fori_loop(low_block, i + 1, weigh, (none,) * 4)
        inverse = [1.0 / sums[0], 1.0 / sums[2]]
        delta = [sums[1] * inverse[0], sums[3] * inverse[1]]

        def spread(b, carry):
            at = pl.ds(pl.multiple_of(b * block, block), block)
            probs, grads = [], []
            for h in range(2):
                rows = slice(h * HDIM, (h + 1) * HDIM)
                p = s_buf[h, b] * inverse[h]
                ds = (p * (dp_buf[h, b] - delta[h])).astype(BF16)
                p = p.astype(BF16)
                o_t[rows, :] += nn(v_t[b, rows, :], p)
                dq_t[rows, :] += nn(k_t[b, rows, :], ds)
                probs.append(p)
                grads.append(ds)
            dv_sum[at, :] += nn(jnp.concatenate(probs, 1), do_cat)
            dk_sum[at, :] += nn(jnp.concatenate(grads, 1), q_cat)
            return carry

        lax.fori_loop(low_block, i + 1, spread, 0)
        o_ref[...] = o_t[...].T.astype(BF16)
        here = pl.ds(pl.multiple_of(i * block, block), block)
        dq = turn(dq_t[...].T * scale, [table_ref[n, here, :] for n in range(3)], -1.0).astype(BF16)
        dq_ref[...] = dq
        db_ref[0:1, :] += jnp.sum(dq.astype(F32), 0, keepdims=True)

        @pl.when(i == count - 1)
        def _():
            dk = turn(dk_sum[...], table_ref, -1.0).astype(BF16)
            dv = dv_sum[...].astype(BF16)
            dk_ref[...] = dk
            dv_ref[...] = dv
            db_ref[1:2, :] = jnp.sum(dk.astype(F32), 0, keepdims=True)
            db_ref[2:3, :] = jnp.sum(dv.astype(F32), 0, keepdims=True)

    part = pl.BlockSpec((block, LANES), lambda p, i, *_: (i, p + first))
    column = pl.BlockSpec((tokens, LANES), lambda p, i, *_: (0, p + first))
    shape = jax.ShapeDtypeStruct((tokens, local), BF16)
    return launch(
        kernel,
        (pairs, count),
        [
            part,
            column,
            column,
            part,
            pl.BlockSpec((1, block), lambda p, i, *_: (0, i)),
            whole(3, tokens, LANES),
        ]
        + [ANY] * len(held),
        (part, part, column, column, pl.BlockSpec((3, LANES), lambda p, i, *_: (0, p + first))),
        (shape,) * 4 + (jax.ShapeDtypeStruct((3, local), F32),),
        (query, keys, vals, d_attn, start, tables, *held),
        scalars=(low,),
        aliases={7 + i: i for i in range(len(held))},
        scratch=(
            pltpu.VMEM((2, tokens, LANES), BF16),
            pltpu.VMEM((2, tokens, LANES), BF16),
            pltpu.VMEM((count, LANES, block), BF16),
            pltpu.VMEM((count, LANES, block), BF16),
            pltpu.VMEM((2, count, block, block), F32),
            pltpu.VMEM((2, count, block, block), F32),
            pltpu.VMEM((LANES, block), F32),
            pltpu.VMEM((LANES, block), F32),
            pltpu.VMEM((tokens, LANES), F32),
            pltpu.VMEM((tokens, LANES), F32),
        ),
        flops=tokens * tokens * local * 24,
        moved=tokens * local * 20,
        after=after,
    )


def hidden_slot(places, normed, g, bias, group, after=()):
    tokens, width = normed.shape
    local = group[0].shape[3]
    tile = min(512, tokens)

    def kernel(place_ref, x_ref, g_ref, bias_ref, *rest):
        parts, (h_ref, dz_ref, db_ref, store, sem) = rest[:-5], rest[-5:]

        @pl.when(pl.program_id(0) == 0)
        def _():
            load_weights(place_ref, [parts], [(0, 0), (0, 1)], store, sem)
            db_ref[...] = jnp.zeros_like(db_ref)

        v = nn(x_ref[...], store[:, :local]) + bias_ref[...]
        dh = nn(g_ref[...], store[:, local:])
        square = v * v
        t = jnp.tanh(0.7978845608 * (v + 0.044715 * (square * v)))
        half = 0.5 * (1.0 + t)
        h_ref[...] = (v * half).astype(BF16)
        slope = half + (0.5 * v) * (1.0 - t * t) * (0.7978845608 + (3.0 * 0.044715 * 0.7978845608) * square)
        dz = (dh * slope).astype(BF16)
        dz_ref[...] = dz
        db_ref[...] += jnp.sum(dz.astype(F32), 0, keepdims=True)

    row = pl.BlockSpec((tile, width), lambda i, *_: (i, 0))
    out = pl.BlockSpec((tile, local), lambda i, *_: (i, 0))
    shape = jax.ShapeDtypeStruct((tokens, local), BF16)
    return launch(
        kernel,
        (tokens // tile,),
        [row, row, whole(1, local)] + [ANY] * len(group),
        (out, out, whole(1, local)),
        (shape, shape, jax.ShapeDtypeStruct((1, local), F32)),
        (normed, g, bias, *group),
        scalars=(places,),
        scratch=(pltpu.VMEM((width, 2 * local), BF16), pltpu.SemaphoreType.DMA),
        flops=4 * tokens * width * local,
        moved=tokens * width * 4 + width * local * 4,
        after=after,
        weight=5,
    )


def grad_blocks(inner_at, inner, normed_t, g_t, sides, received, after=(), weight=1):
    width, tokens = normed_t.shape
    outer = lax.axis_size("dp") // inner
    owners = inner_at.shape[0]
    n = len(sides)
    cuts = len(sides[0][1])
    piece_width = sides[0][1][0].shape[1]
    local = cuts * piece_width
    rows = width // (outer * inner)

    def kernel(inner_ref, *rest):
        lefts = rest[:2]
        rights = rest[2 : 2 + n * cuts]
        adds = rest[2 + n * cuts : -1]
        out = rest[-1]
        step = pl.program_id(1)
        for i, (side, _) in enumerate(sides):

            @pl.when(step == i)
            def _(i=i, side=side):
                left = lefts[side][...].reshape(outer * rows, tokens)
                for c in range(cuts):
                    at = slice(c * piece_width, (c + 1) * piece_width)
                    total = nn(left, rights[i * cuts + c][...]).reshape(outer, rows, piece_width)
                    for add in adds:
                        total += add[:, 0, 0, :, at].astype(F32)
                    out[:, 0, 0, :, at] = total.astype(BF16)

    left = pl.BlockSpec((outer, 1, rows, tokens), lambda o, i, inner_ref, *_: (0, inner_ref[o], 0, 0))
    piece = pl.BlockSpec((outer, 1, 1, rows, local), lambda o, i, *_: (0, o, i, 0, 0))
    four = (outer, inner, rows, tokens)
    return launch(
        kernel,
        (owners, n),
        [left, left] + [whole(tokens, piece_width)] * (n * cuts) + [piece] * len(received),
        piece,
        jax.ShapeDtypeStruct((outer, owners, n, rows, local), BF16),
        (normed_t.reshape(four), g_t.reshape(four), *[right for _, rights in sides for right in rights], *received),
        scalars=(inner_at,),
        after=after,
        weight=weight,
    )


def project_back(places, shares, lefts, groups, slots, received, split, after=()):
    tokens = lefts[0].shape[0]
    local = groups[0][0].shape[3]
    count = shares.shape[0]
    share = tokens // lax.axis_size("tensor")
    tile = min(512, share)
    steps = share // tile
    width = places.shape[0] * groups[0][0].shape[2]
    m = len(lefts)
    depth = len(slots) * local
    flat = [part for group in groups for part in group]
    cut = len(groups[0])
    n_groups = len(flat)

    def kernel(place_ref, shares_ref, *rest):
        left_refs = rest[:m]
        refs = rest[m : m + n_groups]
        adds = rest[m + n_groups : m + n_groups + len(received)]
        outs = rest[m + n_groups + len(received) : -2]
        store, sem = rest[-2:]
        step, part = pl.program_id(0), pl.program_id(1)

        @pl.when((step == 0) & (part == 0))
        def _():
            nested = [refs[k : k + cut] for k in range(0, n_groups, cut)]
            load_weights(place_ref, nested, slots, store, sem)

        total = nt(jnp.concatenate([left[...] for left in left_refs], 1), store[...])
        for add in adds:
            total += add[...].astype(F32)
        if not split:
            outs[0][...] = total.astype(BF16)
        else:
            at = pl.ds(pl.multiple_of(part * tile, tile), tile)
            for j, out in enumerate(outs):

                @pl.when(step == j)
                def _(out=out):
                    out[at, :] = total.astype(out.dtype)

    def left(array):
        return pl.BlockSpec((tile, array.shape[1]), lambda i, j, p_ref, s_ref: (s_ref[i] * steps + j, 0))

    piece = pl.BlockSpec((tile, width), lambda i, j, *_: (i * steps + j, 0))
    if split:
        out_specs = (whole(share, width),) * count
        out_shape = tuple(jax.ShapeDtypeStruct((share, width), F32 if j == 0 else BF16) for j in range(count))
    else:
        out_specs = piece
        out_shape = jax.ShapeDtypeStruct((count * share, width), BF16)
    return launch(
        kernel,
        (count, steps),
        [left(array) for array in lefts] + [ANY] * n_groups + [piece] * len(received),
        out_specs,
        out_shape,
        (*lefts, *flat, *received),
        scalars=(places, shares),
        scratch=(pltpu.VMEM((width, depth), BF16), pltpu.SemaphoreType.DMA),
        flops=2 * count * share * width * depth,
        moved=width * depth * 2 + count * share * (depth + width) * 2,
        after=after,
    )


def finish_output(mine, own, received, x, vec, after=()):
    share, width = own.shape
    tile = min(256, share)
    steps = share // tile

    def kernel(mine_ref, own_ref, x_ref, vec_ref, *rest):
        total = own_ref[...]
        for ref in rest[:-1]:
            total += ref[...].astype(F32)
        rest[-1][...] = (x_ref[...].astype(F32) + total + vec_ref[2:3, :] + vec_ref[3:4, :]).astype(BF16)

    row = pl.BlockSpec((tile, width), lambda i, *_: (i, 0))
    far = pl.BlockSpec((tile, width), lambda i, mine_ref: (mine_ref[0] * steps + i, 0))
    return launch(
        kernel,
        (steps,),
        [row, far, whole(4, width)] + [row] * len(received),
        row,
        jax.ShapeDtypeStruct((share, width), BF16),
        (own, x, vec, *received),
        scalars=(mine,),
        moved=share * width * 10,
        after=after,
    )


def finish_input(mine, own, received, x, g, vec, after=()):
    share, width = own.shape
    tile = min(256, share)
    steps = share // tile

    def kernel(mine_ref, own_ref, x_ref, g_ref, vec_ref, *rest):
        grad_ref, rows_ref = rest[-2:]
        dn = own_ref[...]
        for ref in rest[:-2]:
            dn += ref[...].astype(F32)
        x = x_ref[...].astype(F32)
        g = g_ref[...].astype(F32)
        mean = jnp.mean(x, -1, keepdims=True)
        centered = x - mean
        var = jnp.mean(centered * centered, -1, keepdims=True)
        inverse = lax.rsqrt(var + 1e-05)
        hat = centered * inverse
        e = dn * vec_ref[0:1, :]
        back = inverse * (e - jnp.mean(e, -1, keepdims=True) - hat * jnp.mean(e * hat, -1, keepdims=True))
        grad_ref[...] = (g + back).astype(BF16)

        @pl.when(pl.program_id(0) == 0)
        def _():
            rows_ref[...] = jnp.zeros_like(rows_ref)

        rows_ref[0:1, :] += jnp.sum(dn * hat, 0, keepdims=True)
        rows_ref[1:2, :] += jnp.sum(dn, 0, keepdims=True)
        rows_ref[2:3, :] += jnp.sum(g, 0, keepdims=True)

    row = pl.BlockSpec((tile, width), lambda i, *_: (i, 0))
    far = pl.BlockSpec((tile, width), lambda i, mine_ref: (mine_ref[0] * steps + i, 0))
    return launch(
        kernel,
        (steps,),
        [row, far, far, whole(4, width)] + [row] * len(received),
        (row, whole(3, width)),
        (jax.ShapeDtypeStruct((share, width), BF16), jax.ShapeDtypeStruct((3, width), F32)),
        (own, x, g, vec, *received),
        scalars=(mine,),
        moved=share * width * 12,
        after=after,
    )


def lay_out(order, parts, after=()):
    share, width = parts[0].shape
    count = len(parts)
    tile = min(256, share)
    steps = share // tile

    def kernel(order_ref, *rest):
        for r in range(count):

            @pl.when(pl.program_id(0) == r)
            def _(r=r):
                rest[count][...] = rest[r][...]

    def fetch(r):
        return pl.BlockSpec(
            (tile, width), lambda i, j, *_: (jnp.where(i == r, j, jnp.where(i < r, 0, steps - 1)), 0)
        )

    return launch(
        kernel,
        (count, steps),
        [fetch(r) for r in range(count)],
        pl.BlockSpec((tile, width), lambda i, j, order_ref: (order_ref[i] * steps + j, 0)),
        jax.ShapeDtypeStruct((share * count, width), parts[0].dtype),
        parts,
        scalars=(order,),
        moved=share * count * width * 4,
        after=after,
    )


def total_group(grads, own, received, places, slots_in_all, after=()):
    n, rows, local = own.shape

    def kernel(places_ref, own_ref, *rest):
        out, squares = rest[-2:]
        total = own_ref[0].astype(F32)
        for ref in rest[: len(received)]:
            total += ref[0].astype(F32)
        out[0] = total

        @pl.when(pl.program_id(0) == 0)
        def _():
            squares[...] = jnp.zeros_like(squares)

        squares[...] += jnp.sum(total * total, 0, keepdims=True)

    piece = pl.BlockSpec((1, rows, local), lambda i, *_: (i, 0, 0))
    out = pl.BlockSpec((1, rows, local), lambda i, places_ref: (places_ref[i], 0, 0))
    first = grads is None
    return launch(
        kernel,
        (n,),
        [piece] * (1 + len(received)) + ([] if first else [ANY]),
        (out, whole(1, local)),
        (jax.ShapeDtypeStruct((slots_in_all, rows, local), F32), jax.ShapeDtypeStruct((1, local), F32)),
        (own, *received) + (() if first else (grads,)),
        scalars=(places,),
        aliases={} if first else {2 + len(received): 0},
        after=after,
    )


def collect(values, axis, count):
    rows = [values]
    for k in range(1, count):
        rows.append(lax.ppermute(values, axis, [(i, (i + k) % count) for i in range(count)]))
    rows = jnp.concatenate(rows[::-1] * 2, 0)
    return lax.dynamic_slice_in_dim(rows, count - 1 - lax.axis_index(axis), count, 0)


def total_over(values, axis, count):
    total = values
    for k in range(1, count):
        total = total + lax.ppermute(values, axis, [(i, (i + k) % count) for i in range(count)])
    return total


def shift(values, axis, count, inner, outer_by, inner_by):
    outer = count // inner
    pairs = [
        (o * inner + i, (o + outer_by) % outer * inner + (i + inner_by) % inner)
        for o in range(outer)
        for i in range(inner)
    ]
    return lax.ppermute(values, axis, pairs)


def body(
    block_input,
    cotangent,
    segment_ids,
    w_in,
    w_in_m,
    w_in_v,
    w_outs,
    w_outs_m,
    w_outs_v,
    in_bias,
    in_bias_m,
    in_bias_v,
    vectors,
    vectors_m,
    vectors_v,
):
    n_dp = lax.axis_size("dp")
    n_tensor = lax.axis_size("tensor")
    inner = 2
    outer = n_dp // inner
    cores = 2
    ways = n_tensor // cores
    me = lax.axis_index("dp")
    mine = lax.axis_index("tensor")
    my_outer, my_inner = me // inner, me % inner
    my_way, my_core = mine // cores, mine % cores
    tokens, width = block_input.shape
    _, slots_in, local = w_in.shape
    slots_out = w_outs.shape[1]
    hidden_slots = slots_out - 1

    def numbers(values):
        return jnp.stack([jnp.asarray(v, jnp.int32) for v in values])

    other_inner = 1 - my_inner
    inner_at = [numbers([my_inner]), numbers([other_inner])]
    both_inner = jnp.arange(inner, dtype=jnp.int32)
    lines = [[o * inner + i for o in range(outer)] for i in range(inner)]
    owner_places = numbers(
        [o * inner + i for i in (my_inner, other_inner) for o in range(outer)]
    )
    share_order = numbers(
        [(my_way - w) % ways * cores + (my_core - c) % cores for w in range(ways) for c in range(cores)]
    )
    share_dests = [
        numbers([(my_way + w) % ways * cores + (my_core + c) % cores for w in range(ways)])
        for c in range(cores)
    ]
    share_mine = numbers([mine])

    def to_partner(values):
        return shift(values, "dp", n_dp, inner, 0, 1)


    w_in_s = w_in.transpose(1, 0, 2)
    w_outs_s = w_outs.transpose(1, 0, 2)

    first_slots = [(0, 0), (0, 1), (0, 2), (1, 0)]
    gather_slots = [first_slots[:2], first_slots[2:]] + [[(0, 3 + s), (1, 1 + s)] for s in range(hidden_slots)]
    group_slots = [first_slots] + [[(0, 3 + s), (1, 1 + s)] for s in range(hidden_slots)]

    small = jnp.concatenate([in_bias.reshape(1, -1), vectors.reshape(1, -1)], 1).astype(BF16).astype(F32)
    small = collect(small, "dp", n_dp)
    bias_size = in_bias.size
    bias = small[:, :bias_size].reshape((n_dp,) + in_bias.shape).transpose(1, 2, 0, 3).reshape(slots_in, local)
    vec = small[:, bias_size:].reshape((n_dp,) + vectors.shape).transpose(1, 0, 2).reshape(4, width)

    LINE.last = ()
    turns = list(range(1 + hidden_slots))
    along = []
    for slots in gather_slots:
        cast = cast_group(w_in_s, w_outs_s, slots, LINE.last)
        LINE.last = (cast,)
        along.append(lax.all_gather(cast, "dp", axis=0, axis_index_groups=lines))
    groups = []

    def exchange(g):
        here = gate(along[g])[0]
        groups.append([here, to_partner(here)])

    seg = segment_ids[0]
    start = jnp.sum((seg[None, :] < seg[:, None]).astype(jnp.int32), 1)
    block = min(256, tokens)
    low = start[::block] // block
    place = (jnp.arange(tokens, dtype=jnp.int32) - start).astype(F32)
    freq = 10000.0 ** (-jnp.arange(ROT // 2, dtype=F32) * 2.0 / ROT)
    freq = jnp.tile(jnp.concatenate([freq, freq, jnp.zeros((HDIM - ROT,), F32)]), LANES // HDIM)
    theta = place[:, None] * freq[None, :]
    sine = jnp.sin(theta)
    feature = jnp.arange(LANES) % HDIM
    tables = jnp.stack(
        [
            jnp.cos(theta),
            jnp.where(feature < ROT // 2, -sine, 0.0),
            jnp.where((feature >= ROT // 2) & (feature < ROT), sine, 0.0),
        ]
    )
    LINE.last = LINE.last + (tables, low)

    normed, normed_t, g_t = in_line(normalize, block_input, cotangent, vec)

    hidden, d_hidden, d_bias_hidden, sides = [], [], [], {}

    def hidden_step(s):
        h, dz, db = in_line(hidden_slot, owner_places, normed, cotangent, bias[3 + s : 4 + s], groups[2 + s])
        hidden.append(h)
        d_hidden.append(dz)
        d_bias_hidden.append(db)
        sides[1 + s] = [(0, [dz]), (1, [h])]

    legs, shares = {}, {}

    def scatter(out):
        outer_blocks, owners, n, rows, columns = out.shape
        out = out.reshape(outer_blocks * owners * n, rows, columns)
        out = lax.psum_scatter(out, "dp", scatter_dimension=0, axis_index_groups=lines, tiled=True)
        return out.reshape(owners, n, rows, columns)

    def first_next(g, weight=1):
        out = in_line(grad_blocks, inner_at[1], inner, normed_t, g_t, sides[g], [], weight=weight)
        legs[g] = [to_partner(out)]

    def second_next(g):
        out = in_line(grad_blocks, inner_at[0], inner, normed_t, g_t, sides[g], legs[g])
        shares[g] = (scatter(out)[0], [])

    def line_first(g):
        out = scatter(in_line(grad_blocks, both_inner, inner, normed_t, g_t, sides[g], []))
        sent = lax.dynamic_index_in_dim(out, other_inner, 0, False)
        shares[g] = (lax.dynamic_index_in_dim(out, my_inner, 0, False), [to_partner(sent)])

    exchange(0)
    exchange(1)
    groups[0][1] = gate(groups[0][1], weight=5)[0]
    to_exchange = list(range(2, 2 + hidden_slots))
    in_first = [(0, 0), (0, 1), (1, 0), (1, 1)]
    qkvd = in_line(qkv_project, owner_places, normed, cotangent, bias, tables, groups[:2], in_first)
    pairs = local // LANES
    held = ()
    for first in range(pairs):
        if to_exchange and len(to_exchange) > 1:
            exchange(to_exchange.pop(0))
        held = in_line(attend, first, 1, held, low, *qkvd, start.reshape(1, tokens), tables)
    while to_exchange:
        exchange(to_exchange.pop(0))
    attn, d_query, d_keys, d_vals, d_bias_attn = held
    sides[0] = [(0, [d_query]), (0, [d_keys]), (0, [d_vals]), (1, [attn])]
    line_first(0)
    for s in range(hidden_slots):
        hidden_step(s)

    def first_half(lefts, slots):
        received = []
        for c in range(1, cores):
            out = in_line(project_back, owner_places, share_dests[c], lefts, groups, slots, [], False)
            received.append(shift(out, "tensor", n_tensor, cores, 0, c))
        return received

    def second_half(lefts, slots, received):
        outs = in_line(project_back, owner_places, share_dests[0], lefts, groups, slots, received, True)
        return outs[0], [shift(outs[w], "tensor", n_tensor, cores, w, 0) for w in range(1, ways)]

    def send_share(own):
        return [own] + [shift(own, "tensor", n_tensor, cores, w, 0) for w in range(1, ways)]

    def gather_share(held):
        parts = []
        for part in [held[0]] + gate(*held[1:]):
            parts.append(part)
            for c in range(1, cores):
                parts.append(shift(part, "tensor", n_tensor, cores, 0, c))
        return parts

    back = (
        [d_query, d_keys, d_vals] + d_hidden,
        in_first[:3] + [(2 + s, 0) for s in range(hidden_slots)],
    )
    ahead = ([attn] + hidden, in_first[3:] + [(2 + s, 1) for s in range(hidden_slots)])
    grads, squares = None, []

    def total_next(g):
        slots, (own, received) = group_slots[g], shares[g]
        places = jnp.asarray([s if which == 0 else slots_in + s for which, s in slots], jnp.int32)
        out, part = in_line(total_group, grads, own, received, places, slots_in + slots_out)
        squares.append(part)
        return out

    first_next(1, 5000)
    back_half = first_half(*back)
    first_next(2)
    ahead_half = first_half(*ahead)
    second_next(1)
    first_next(3)
    own, received = second_half(*back, back_half)
    second_next(2)
    ahead_own, ahead_received = second_half(*ahead, ahead_half)
    second_next(3)
    for g in range(4, 1 + hidden_slots):
        first_next(g)
    d_x, vector_rows = in_line(finish_input, share_mine, own, received, block_input, cotangent, vec)
    back_held = send_share(d_x)
    for g in range(4, 1 + hidden_slots):
        second_next(g)
    out_held = send_share(
        in_line(finish_output, share_mine, ahead_own, ahead_received, block_input, vec)
    )
    for g in turns[:2]:
        grads = total_next(g)
    back_parts = gather_share(back_held)
    block_input_gradient = in_line(lay_out, share_order, back_parts)
    for g in turns[2:-1]:
        grads = total_next(g)
    out_parts = gather_share(out_held)
    output = in_line(lay_out, share_order, out_parts)

    vector_rows = total_over(vector_rows.reshape(1, -1), "tensor", n_tensor)
    d_bias = jnp.concatenate([d_bias_attn] + d_bias_hidden, 0)
    small = total_over(jnp.concatenate([d_bias.reshape(1, -1), vector_rows], 1), "dp", n_dp)
    g_bias = lax.dynamic_index_in_dim(
        small[0, : slots_in * local].reshape(slots_in, in_bias.shape[1], n_dp, in_bias.shape[2]), me, 2, False
    )
    g_vec = lax.dynamic_index_in_dim(small[0, slots_in * local :].reshape(3, n_dp, width // n_dp), me, 1, False)
    g_vec = jnp.concatenate([g_vec, g_vec[2:]], 0)

    LINE.last = LINE.last + (g_bias, g_vec)
    grads = total_next(turns[-1])
    g_in, g_outs = grads[:slots_in], grads[slots_in:]
    local_squares = (
        jnp.sum(jnp.concatenate(squares, 0)) + jnp.sum(g_bias * g_bias) + jnp.sum(g_vec * g_vec) * (1.0 / n_tensor)
    )
    local_squares = total_over(jnp.full((1, LANES), local_squares), "tensor", n_tensor)
    bit = 1
    while bit < n_dp:
        pairs_at = [(i, i ^ bit) for i in range(n_dp)]
        local_squares = local_squares + lax.ppermute(local_squares, "dp", pairs_at)
        bit *= 2
    grad_norm = jnp.sqrt(local_squares[0, 0])
    factor = CLIP_AT / jnp.maximum(grad_norm, CLIP_AT)

    def slot_major(*arrays):
        return [a.transpose(1, 0, 2) for a in arrays]

    new_in = slot_major(*adamw(w_in_s, *slot_major(w_in_m, w_in_v), g_in, factor, RATE_MATRIX, DECAY_MATRIX))
    new_outs = slot_major(*adamw(w_outs_s, *slot_major(w_outs_m, w_outs_v), g_outs, factor, RATE_MATRIX, DECAY_MATRIX))
    new_bias = adamw(in_bias, in_bias_m, in_bias_v, g_bias, factor, RATE_VECTOR, 0.0)
    new_vec = adamw(vectors, vectors_m, vectors_v, g_vec, factor, RATE_VECTOR, 0.0)
    return (output, block_input_gradient, grad_norm, *new_in, *new_outs, *new_bias, *new_vec)


def solution(mesh):
    rows = P("dp", None)
    matrix = P("dp", None, "tensor")
    small = P(None, "tensor", "dp")
    vector = P(None, "dp")
    return jax.shard_map(
        body,
        mesh=mesh,
        in_specs=(rows,) * 3 + (matrix,) * 6 + (small,) * 3 + (vector,) * 3,
        out_specs=(rows, rows, P()) + (matrix,) * 6 + (small,) * 3 + (vector,) * 3,
        check_vma=False,
    )
```

```python
import jax
import jax.numpy as jnp
from jax import lax
from jax.experimental import pallas as pl
from jax.experimental.pallas import tpu as pltpu
from jax.sharding import PartitionSpec as P

HDIM = 64
ROT = 32
STEP = 10

BETA_ONE = 0.9
BETA_TWO = 0.95
EPSILON = 1e-08
CLIP_AT = 1.0
RATE_MATRIX = 0.06
RATE_VECTOR = 0.6
DECAY_MATRIX = 0.1

F32 = jnp.float32
BF16 = jnp.bfloat16
LANES = 128
ANY = pl.BlockSpec(memory_space=pltpu.HBM)
VMEM_LIMIT = 60 * 1024 * 1024


def nn(a, b):
    return lax.dot_general(a, b, (((1,), (0,)), ((), ())), preferred_element_type=F32)


def nt(a, b):
    return lax.dot_general(a, b, (((1,), (1,)), ((), ())), preferred_element_type=F32)


def whole(*shape):
    return pl.BlockSpec(shape, lambda *_: (0,) * len(shape))


class Line:
    def __init__(self):
        self.last = ()


LINE = Line()


def launch(kernel, grid, in_specs, out_specs, out_shape, args, *, scalars=(), scratch=(), flops=0, moved=0, aliases={}, after=(), weight=1):
    extra = len(after)
    ahead = len(scalars) + len(args)

    def trimmed(*refs):
        return kernel(*refs[:ahead], *refs[ahead + extra :])

    return pl.pallas_call(
        trimmed,
        grid_spec=pltpu.PrefetchScalarGridSpec(
            num_scalar_prefetch=len(scalars),
            grid=grid,
            in_specs=list(in_specs) + [ANY] * extra,
            out_specs=out_specs,
            scratch_shapes=list(scratch),
        ),
        out_shape=out_shape,
        input_output_aliases=aliases,
        compiler_params=pltpu.CompilerParams(vmem_limit_bytes=VMEM_LIMIT),
        cost_estimate=pl.CostEstimate(flops=200000000 * weight, bytes_accessed=1, transcendentals=0),
    )(*scalars, *args, *after)


def in_line(call, *args, **more):
    out = call(*args, after=LINE.last, **more)
    LINE.last = (out[-1] if isinstance(out, (tuple, list)) else out,)
    return out


def gate(*arrays, weight=1):
    n = len(arrays)

    def kernel(*refs):
        pass

    out = in_line(
        launch,
        kernel,
        (1,),
        [ANY] * n,
        (ANY,) * n,
        tuple(jax.ShapeDtypeStruct(a.shape, a.dtype) for a in arrays),
        arrays,
        aliases={i: i for i in range(n)},
        weight=weight,
    )
    return list(out)


def adamw(weight, first, second, grad, factor, rate, decay):
    clipped = grad * factor
    first = BETA_ONE * first + (1.0 - BETA_ONE) * clipped
    second = BETA_TWO * second + (1.0 - BETA_TWO) * clipped * clipped
    first_hat = first / (1.0 - BETA_ONE**STEP)
    second_hat = second / (1.0 - BETA_TWO**STEP)
    weight = weight - rate * (first_hat / (jnp.sqrt(second_hat) + EPSILON) + decay * weight)
    return (weight, first, second)


def load_weights(place_ref, groups, slots, store, sem):
    copies = []
    for column, (group, slot) in enumerate(slots):
        at = 0
        for part in groups[group]:
            owners, _, rows, local = part.shape
            for r in range(owners):
                to = pl.ds(pl.multiple_of(place_ref[at] * rows, rows), rows)
                copies.append(
                    pltpu.make_async_copy(
                        part.at[r, slot], store.at[to, column * local : (column + 1) * local], sem
                    )
                )
                at += 1
    for copy in copies:
        copy.start()
    for copy in copies:
        copy.wait()


def turn(values, table, sign):
    return (
        values * table[0]
        + sign * (pltpu.roll(values, LANES - ROT // 2, 1) * table[1])
        + sign * (pltpu.roll(values, ROT // 2, 1) * table[2])
    )


def cast_group(w_in, w_outs, slots, deps):
    _, rows, local = w_in.shape

    def kernel(*refs):
        ins, out = refs[: len(slots)], refs[-1]
        for i, ref in enumerate(ins):
            out[i] = ref[0].astype(BF16)

    specs = [
        pl.BlockSpec((1, rows, local), lambda i, s=slot: (s, 0, 0)) for _, slot in slots
    ]
    args = [w_in if which == 0 else w_outs for which, _ in slots]
    n = len(slots)
    return launch(
        kernel,
        (1,),
        specs,
        whole(n, rows, local),
        jax.ShapeDtypeStruct((n, rows, local), BF16),
        args,
        moved=n * rows * local * 6,
        after=deps,
    )


def norm_kernel(x_ref, g_ref, vec_ref, normed_ref, normed_t_ref, g_t_ref):
    x = x_ref[...].astype(F32)
    mean = jnp.mean(x, -1, keepdims=True)
    centered = x - mean
    var = jnp.mean(centered * centered, -1, keepdims=True)
    hat = centered * lax.rsqrt(var + 1e-05)
    normed = (hat * vec_ref[0:1, :] + vec_ref[1:2, :]).astype(BF16)
    normed_ref[...] = normed
    normed_t_ref[...] = normed.T
    g_t_ref[...] = g_ref[...].T


def normalize(x, g, vec, after=()):
    tokens, width = x.shape
    tile = min(256, tokens)
    row = pl.BlockSpec((tile, width), lambda i: (i, 0))
    col = pl.BlockSpec((width, tile), lambda i: (0, i))
    shape = jax.ShapeDtypeStruct((tokens, width), BF16)
    shape_t = jax.ShapeDtypeStruct((width, tokens), BF16)
    return launch(
        norm_kernel,
        (tokens // tile,),
        [row, row, whole(4, width)],
        (row, col, col),
        (shape, shape_t, shape_t),
        (x, g, vec),
        flops=tokens * width * 10,
        moved=tokens * width * 10,
        after=after,
    )


def qkv_project(places, normed, g, bias, tables, groups, slots, after=()):
    tokens, width = normed.shape
    local = groups[0][0].shape[3]
    flat = [part for group in groups for part in group]
    cut = len(groups[0])
    tile = min(512, tokens)

    def kernel(place_ref, x_ref, g_ref, bias_ref, table_ref, *rest):
        parts, (q_ref, k_ref, v_ref, da_ref, store, sem) = rest[:-6], rest[-6:]

        @pl.when(pl.program_id(0) == 0)
        def _():
            nested = [parts[k : k + cut] for k in range(0, len(flat), cut)]
            load_weights(place_ref, nested, slots, store, sem)

        x = x_ref[...]
        for slot, out, scale in ((0, q_ref, HDIM ** (-0.5)), (1, k_ref, 1.0)):
            z = nn(x, store[:, slot * local : (slot + 1) * local]) + bias_ref[slot : slot + 1, :]
            for pair in range(local // LANES):
                at = slice(pair * LANES, (pair + 1) * LANES)
                out[:, at] = (turn(z[:, at], table_ref, 1.0) * scale).astype(BF16)
        v_ref[...] = (nn(x, store[:, 2 * local : 3 * local]) + bias_ref[2:3, :]).astype(BF16)
        da_ref[...] = nn(g_ref[...], store[:, 3 * local : 4 * local]).astype(BF16)

    row = pl.BlockSpec((tile, width), lambda i, *_: (i, 0))
    out = pl.BlockSpec((tile, local), lambda i, *_: (i, 0))
    shape = jax.ShapeDtypeStruct((tokens, local), BF16)
    return launch(
        kernel,
        (tokens // tile,),
        [row, row, whole(7, local), pl.BlockSpec((3, tile, LANES), lambda i, *_: (0, i, 0))] + [ANY] * len(flat),
        (out,) * 4,
        (shape,) * 4,
        (normed, g, bias, tables, *flat),
        scalars=(places,),
        scratch=(pltpu.VMEM((width, 4 * local), BF16), pltpu.SemaphoreType.DMA),
        flops=2 * tokens * width * 4 * local,
        moved=tokens * width * 4 + width * local * 8,
        after=after,
    )


def attend(first, held, low, query, keys, vals, d_attn, start, tables, after=()):
    tokens, local = query.shape
    block = min(256, tokens)
    count = tokens // block
    pairs = attend_pairs(local)
    heads = 2 * pairs
    wide = pairs * LANES
    scale = HDIM ** (-0.5)
    lanes = [slice(p * LANES, (p + 1) * LANES) for p in range(pairs)]

    def kernel(low_ref, q_ref, k_ref, v_ref, do_ref, start_ref, table_ref, *rest):
        (o_ref, dq_ref, dk_ref, dv_ref, db_ref,
         k_half, v_half, k_t, v_t, s_buf, dp_buf, o_t, dq_t, dk_sum, dv_sum) = rest[len(held):]
        i = pl.program_id(0)
        first_lanes = lax.broadcasted_iota(jnp.int32, (1, LANES), 1) < HDIM
        zero = jnp.zeros((), BF16)

        def apart(pair):
            return jnp.where(first_lanes, pair, zero), jnp.where(first_lanes, zero, pair)

        @pl.when(i == 0)
        def _():
            for b in range(count):
                at = slice(b * block, (b + 1) * block)
                for source, half, flipped in ((k_ref, k_half, k_t), (v_ref, v_half, v_t)):
                    for p in range(pairs):
                        part = source[at, lanes[p]]
                        half[2 * p, at, :], half[2 * p + 1, at, :] = apart(part)
                        flipped[p, b] = part.T
            dk_sum[...] = jnp.zeros_like(dk_sum)
            dv_sum[...] = jnp.zeros_like(dv_sum)
            db_ref[...] = jnp.zeros_like(db_ref)

        q = [q_ref[:, at] for at in lanes]
        do = [do_ref[:, at] for at in lanes]
        q_cat = [jnp.concatenate(apart(pair), 0) for pair in q]
        do_cat = [jnp.concatenate(apart(pair), 0) for pair in do]
        t_place = i * block + lax.broadcasted_iota(jnp.int32, (1, block), 1)
        t_start = start_ref[...]
        low_block = low_ref[i]
        o_t[...] = jnp.zeros_like(o_t)
        dq_t[...] = jnp.zeros_like(dq_t)

        def score(b, tops):
            at = pl.ds(pl.multiple_of(b * block, block), block)
            u_place = b * block + lax.broadcasted_iota(jnp.int32, (block, 1), 0)
            allowed = (u_place >= t_start) & (u_place <= t_place)
            new = []
            for h in range(heads):
                s = jnp.where(allowed, nt(k_half[h, at, :], q[h // 2]), -1e30)
                s_buf[h, b] = s
                dp_buf[h, b] = nt(v_half[h, at, :], do[h // 2])
                new.append(jnp.maximum(tops[h], jnp.max(s, 0, keepdims=True)))
            return tuple(new)

        lowest = jnp.full((1, block), -jnp.inf, F32)
        tops = lax.fori_loop(low_block, i + 1, score, (lowest,) * heads)

        def weigh(b, sums):
            new = []
            for h in range(heads):
                p = jnp.exp(s_buf[h, b] - tops[h])
                s_buf[h, b] = p
                new.append(sums[2 * h] + jnp.sum(p, 0, keepdims=True))
                new.append(sums[2 * h + 1] + jnp.sum(p * dp_buf[h, b], 0, keepdims=True))
            return tuple(new)

        none = jnp.zeros((1, block), F32)
        sums = lax.fori_loop(low_block, i + 1, weigh, (none,) * (2 * heads))
        inverse = [1.0 / sums[2 * h] for h in range(heads)]
        delta = [sums[2 * h + 1] * inverse[h] for h in range(heads)]

        def spread(b, carry):
            at = pl.ds(pl.multiple_of(b * block, block), block)
            probs, grads = [], []
            for h in range(heads):
                rows = slice(h * HDIM, (h + 1) * HDIM)
                inside = slice(h % 2 * HDIM, (h % 2 + 1) * HDIM)
                p = s_buf[h, b] * inverse[h]
                ds = (p * (dp_buf[h, b] - delta[h])).astype(BF16)
                p = p.astype(BF16)
                o_t[rows, :] += nn(v_t[h // 2, b, inside, :], p)
                dq_t[rows, :] += nn(k_t[h // 2, b, inside, :], ds)
                probs.append(p)
                grads.append(ds)
            for p in range(pairs):
                dv_sum[at, lanes[p]] += nn(jnp.concatenate(probs[2 * p : 2 * p + 2], 1), do_cat[p])
                dk_sum[at, lanes[p]] += nn(jnp.concatenate(grads[2 * p : 2 * p + 2], 1), q_cat[p])
            return carry

        lax.fori_loop(low_block, i + 1, spread, 0)
        o_ref[...] = o_t[...].T.astype(BF16)
        here = pl.ds(pl.multiple_of(i * block, block), block)
        table = [table_ref[n, here, :] for n in range(3)]
        for at in lanes:
            dq = turn(dq_t[at, :].T * scale, table, -1.0).astype(BF16)
            dq_ref[:, at] = dq
            db_ref[0:1, at] += jnp.sum(dq.astype(F32), 0, keepdims=True)

        @pl.when(i == count - 1)
        def _():
            for at in lanes:
                dk = turn(dk_sum[:, at], table_ref, -1.0).astype(BF16)
                dv = dv_sum[:, at].astype(BF16)
                dk_ref[:, at] = dk
                dv_ref[:, at] = dv
                db_ref[1:2, at] = jnp.sum(dk.astype(F32), 0, keepdims=True)
                db_ref[2:3, at] = jnp.sum(dv.astype(F32), 0, keepdims=True)

    part = pl.BlockSpec((block, wide), lambda i, *_: (i, first))
    column = pl.BlockSpec((tokens, wide), lambda i, *_: (0, first))
    shape = jax.ShapeDtypeStruct((tokens, local), BF16)
    return launch(
        kernel,
        (count,),
        [part, column, column, part, pl.BlockSpec((1, block), lambda i, *_: (0, i)), whole(3, tokens, LANES)]
        + [ANY] * len(held),
        (part, part, column, column, pl.BlockSpec((3, wide), lambda i, *_: (0, first))),
        (shape,) * 4 + (jax.ShapeDtypeStruct((3, local), F32),),
        (query, keys, vals, d_attn, start, tables, *held),
        scalars=(low,),
        aliases={7 + i: i for i in range(len(held))},
        scratch=(
            pltpu.VMEM((heads, tokens, LANES), BF16),
            pltpu.VMEM((heads, tokens, LANES), BF16),
            pltpu.VMEM((pairs, count, LANES, block), BF16),
            pltpu.VMEM((pairs, count, LANES, block), BF16),
            pltpu.VMEM((heads, count, block, block), F32),
            pltpu.VMEM((heads, count, block, block), F32),
            pltpu.VMEM((wide, block), F32),
            pltpu.VMEM((wide, block), F32),
            pltpu.VMEM((tokens, wide), F32),
            pltpu.VMEM((tokens, wide), F32),
        ),
        after=after,
    )


def attend_pairs(local):
    return 2 if local % (2 * LANES) == 0 else 1


def hidden_slot(places, normed, g, bias, group, after=()):
    tokens, width = normed.shape
    local = group[0].shape[3]
    tile = min(512, tokens)

    def kernel(place_ref, x_ref, g_ref, bias_ref, *rest):
        parts, (h_ref, dz_ref, db_ref, store, sem) = rest[:-5], rest[-5:]

        @pl.when(pl.program_id(0) == 0)
        def _():
            load_weights(place_ref, [parts], [(0, 0), (0, 1)], store, sem)
            db_ref[...] = jnp.zeros_like(db_ref)

        v = nn(x_ref[...], store[:, :local]) + bias_ref[...]
        dh = nn(g_ref[...], store[:, local:])
        square = v * v
        t = jnp.tanh(0.7978845608 * (v + 0.044715 * (square * v)))
        half = 0.5 * (1.0 + t)
        h_ref[...] = (v * half).astype(BF16)
        slope = half + (0.5 * v) * (1.0 - t * t) * (0.7978845608 + (3.0 * 0.044715 * 0.7978845608) * square)
        dz = (dh * slope).astype(BF16)
        dz_ref[...] = dz
        db_ref[...] += jnp.sum(dz.astype(F32), 0, keepdims=True)

    row = pl.BlockSpec((tile, width), lambda i, *_: (i, 0))
    out = pl.BlockSpec((tile, local), lambda i, *_: (i, 0))
    shape = jax.ShapeDtypeStruct((tokens, local), BF16)
    return launch(
        kernel,
        (tokens // tile,),
        [row, row, whole(1, local)] + [ANY] * len(group),
        (out, out, whole(1, local)),
        (shape, shape, jax.ShapeDtypeStruct((1, local), F32)),
        (normed, g, bias, *group),
        scalars=(places,),
        scratch=(pltpu.VMEM((width, 2 * local), BF16), pltpu.SemaphoreType.DMA),
        flops=4 * tokens * width * local,
        moved=tokens * width * 4 + width * local * 4,
        after=after,
        weight=5,
    )


def grad_blocks(inner_at, inner, normed_t, g_t, sides, received, after=(), weight=1):
    width, tokens = normed_t.shape
    outer = lax.axis_size("dp") // inner
    owners = inner_at.shape[0]
    n = len(sides)
    cuts = len(sides[0][1])
    piece_width = sides[0][1][0].shape[1]
    local = cuts * piece_width
    rows = width // (outer * inner)

    def kernel(inner_ref, *rest):
        lefts = rest[:2]
        rights = rest[2 : 2 + n * cuts]
        adds = rest[2 + n * cuts : -1]
        out = rest[-1]
        step = pl.program_id(1)
        for i, (side, _) in enumerate(sides):

            @pl.when(step == i)
            def _(i=i, side=side):
                left = lefts[side][...].reshape(outer * rows, tokens)
                for c in range(cuts):
                    at = slice(c * piece_width, (c + 1) * piece_width)
                    total = nn(left, rights[i * cuts + c][...]).reshape(outer, rows, piece_width)
                    for add in adds:
                        total += add[:, 0, 0, :, at].astype(F32)
                    out[:, 0, 0, :, at] = total.astype(BF16)

    left = pl.BlockSpec((outer, 1, rows, tokens), lambda o, i, inner_ref, *_: (0, inner_ref[o], 0, 0))
    piece = pl.BlockSpec((outer, 1, 1, rows, local), lambda o, i, *_: (0, o, i, 0, 0))
    four = (outer, inner, rows, tokens)
    return launch(
        kernel,
        (owners, n),
        [left, left] + [whole(tokens, piece_width)] * (n * cuts) + [piece] * len(received),
        piece,
        jax.ShapeDtypeStruct((outer, owners, n, rows, local), BF16),
        (normed_t.reshape(four), g_t.reshape(four), *[right for _, rights in sides for right in rights], *received),
        scalars=(inner_at,),
        after=after,
        weight=weight,
    )


def project_back(places, shares, lefts, groups, slots, received, split, after=()):
    tokens = lefts[0].shape[0]
    local = groups[0][0].shape[3]
    count = shares.shape[0]
    share = tokens // lax.axis_size("tensor")
    tile = min(512, share)
    steps = share // tile
    width = places.shape[0] * groups[0][0].shape[2]
    m = len(lefts)
    depth = len(slots) * local
    flat = [part for group in groups for part in group]
    cut = len(groups[0])
    n_groups = len(flat)

    def kernel(place_ref, shares_ref, *rest):
        left_refs = rest[:m]
        refs = rest[m : m + n_groups]
        adds = rest[m + n_groups : m + n_groups + len(received)]
        outs = rest[m + n_groups + len(received) : -2]
        store, sem = rest[-2:]
        step, part = pl.program_id(0), pl.program_id(1)

        @pl.when((step == 0) & (part == 0))
        def _():
            nested = [refs[k : k + cut] for k in range(0, n_groups, cut)]
            load_weights(place_ref, nested, slots, store, sem)

        total = nt(jnp.concatenate([left[...] for left in left_refs], 1), store[...])
        for add in adds:
            total += add[...].astype(F32)
        if not split:
            outs[0][...] = total.astype(BF16)
        else:
            at = pl.ds(pl.multiple_of(part * tile, tile), tile)
            for j, out in enumerate(outs):

                @pl.when(step == j)
                def _(out=out):
                    out[at, :] = total.astype(out.dtype)

    def left(array):
        return pl.BlockSpec((tile, array.shape[1]), lambda i, j, p_ref, s_ref: (s_ref[i] * steps + j, 0))

    piece = pl.BlockSpec((tile, width), lambda i, j, *_: (i * steps + j, 0))
    if split:
        out_specs = (whole(share, width),) * count
        out_shape = tuple(jax.ShapeDtypeStruct((share, width), F32 if j == 0 else BF16) for j in range(count))
    else:
        out_specs = piece
        out_shape = jax.ShapeDtypeStruct((count * share, width), BF16)
    return launch(
        kernel,
        (count, steps),
        [left(array) for array in lefts] + [ANY] * n_groups + [piece] * len(received),
        out_specs,
        out_shape,
        (*lefts, *flat, *received),
        scalars=(places, shares),
        scratch=(pltpu.VMEM((width, depth), BF16), pltpu.SemaphoreType.DMA),
        flops=2 * count * share * width * depth,
        moved=width * depth * 2 + count * share * (depth + width) * 2,
        after=after,
    )


def finish_output(mine, own, received, x, vec, after=()):
    share, width = own.shape
    tile = min(256, share)
    steps = share // tile

    def kernel(mine_ref, own_ref, x_ref, vec_ref, *rest):
        total = own_ref[...]
        for ref in rest[:-1]:
            total += ref[...].astype(F32)
        rest[-1][...] = (x_ref[...].astype(F32) + total + vec_ref[2:3, :] + vec_ref[3:4, :]).astype(BF16)

    row = pl.BlockSpec((tile, width), lambda i, *_: (i, 0))
    far = pl.BlockSpec((tile, width), lambda i, mine_ref: (mine_ref[0] * steps + i, 0))
    return launch(
        kernel,
        (steps,),
        [row, far, whole(4, width)] + [row] * len(received),
        row,
        jax.ShapeDtypeStruct((share, width), BF16),
        (own, x, vec, *received),
        scalars=(mine,),
        moved=share * width * 10,
        after=after,
    )


def finish_input(mine, own, received, x, g, vec, after=()):
    share, width = own.shape
    tile = min(256, share)
    steps = share // tile

    def kernel(mine_ref, own_ref, x_ref, g_ref, vec_ref, *rest):
        grad_ref, rows_ref = rest[-2:]
        dn = own_ref[...]
        for ref in rest[:-2]:
            dn += ref[...].astype(F32)
        x = x_ref[...].astype(F32)
        g = g_ref[...].astype(F32)
        mean = jnp.mean(x, -1, keepdims=True)
        centered = x - mean
        var = jnp.mean(centered * centered, -1, keepdims=True)
        inverse = lax.rsqrt(var + 1e-05)
        hat = centered * inverse
        e = dn * vec_ref[0:1, :]
        back = inverse * (e - jnp.mean(e, -1, keepdims=True) - hat * jnp.mean(e * hat, -1, keepdims=True))
        grad_ref[...] = (g + back).astype(BF16)

        @pl.when(pl.program_id(0) == 0)
        def _():
            rows_ref[...] = jnp.zeros_like(rows_ref)

        rows_ref[0:1, :] += jnp.sum(dn * hat, 0, keepdims=True)
        rows_ref[1:2, :] += jnp.sum(dn, 0, keepdims=True)
        rows_ref[2:3, :] += jnp.sum(g, 0, keepdims=True)

    row = pl.BlockSpec((tile, width), lambda i, *_: (i, 0))
    far = pl.BlockSpec((tile, width), lambda i, mine_ref: (mine_ref[0] * steps + i, 0))
    return launch(
        kernel,
        (steps,),
        [row, far, far, whole(4, width)] + [row] * len(received),
        (row, whole(3, width)),
        (jax.ShapeDtypeStruct((share, width), BF16), jax.ShapeDtypeStruct((3, width), F32)),
        (own, x, g, vec, *received),
        scalars=(mine,),
        moved=share * width * 12,
        after=after,
    )


def lay_out(order, parts, after=()):
    share, width = parts[0].shape
    count = len(parts)
    tile = min(256, share)
    steps = share // tile

    def kernel(order_ref, *rest):
        for r in range(count):

            @pl.when(pl.program_id(0) == r)
            def _(r=r):
                rest[count][...] = rest[r][...]

    def fetch(r):
        return pl.BlockSpec(
            (tile, width), lambda i, j, *_: (jnp.where(i == r, j, jnp.where(i < r, 0, steps - 1)), 0)
        )

    return launch(
        kernel,
        (count, steps),
        [fetch(r) for r in range(count)],
        pl.BlockSpec((tile, width), lambda i, j, order_ref: (order_ref[i] * steps + j, 0)),
        jax.ShapeDtypeStruct((share * count, width), parts[0].dtype),
        parts,
        scalars=(order,),
        moved=share * count * width * 4,
        after=after,
    )


def total_group(grads, own, received, places, slots_in_all, after=(), weight=1):
    n, rows, local = own.shape

    def kernel(places_ref, own_ref, *rest):
        out, squares = rest[-2:]
        total = own_ref[0].astype(F32)
        for ref in rest[: len(received)]:
            total += ref[0].astype(F32)
        out[0] = total

        @pl.when(pl.program_id(0) == 0)
        def _():
            squares[...] = jnp.zeros_like(squares)

        squares[...] += jnp.sum(total * total, 0, keepdims=True)

    piece = pl.BlockSpec((1, rows, local), lambda i, *_: (i, 0, 0))
    out = pl.BlockSpec((1, rows, local), lambda i, places_ref: (places_ref[i], 0, 0))
    first = grads is None
    return launch(
        kernel,
        (n,),
        [piece] * (1 + len(received)) + ([] if first else [ANY]),
        (out, whole(1, local)),
        (jax.ShapeDtypeStruct((slots_in_all, rows, local), F32), jax.ShapeDtypeStruct((1, local), F32)),
        (own, *received) + (() if first else (grads,)),
        scalars=(places,),
        aliases={} if first else {2 + len(received): 0},
        after=after,
        weight=weight,
    )


def collect(values, axis, count):
    rows = [values]
    for k in range(1, count):
        rows.append(lax.ppermute(values, axis, [(i, (i + k) % count) for i in range(count)]))
    rows = jnp.concatenate(rows[::-1] * 2, 0)
    return lax.dynamic_slice_in_dim(rows, count - 1 - lax.axis_index(axis), count, 0)


def total_over(values, axis, count):
    total = values
    for k in range(1, count):
        total = total + lax.ppermute(values, axis, [(i, (i + k) % count) for i in range(count)])
    return total


def shift(values, axis, count, inner, outer_by, inner_by):
    outer = count // inner
    pairs = [
        (o * inner + i, (o + outer_by) % outer * inner + (i + inner_by) % inner)
        for o in range(outer)
        for i in range(inner)
    ]
    return lax.ppermute(values, axis, pairs)


def body(
    block_input,
    cotangent,
    segment_ids,
    w_in,
    w_in_m,
    w_in_v,
    w_outs,
    w_outs_m,
    w_outs_v,
    in_bias,
    in_bias_m,
    in_bias_v,
    vectors,
    vectors_m,
    vectors_v,
):
    n_dp = lax.axis_size("dp")
    n_tensor = lax.axis_size("tensor")
    inner = 2
    outer = n_dp // inner
    cores = 2
    ways = n_tensor // cores
    me = lax.axis_index("dp")
    mine = lax.axis_index("tensor")
    my_outer, my_inner = me // inner, me % inner
    my_way, my_core = mine // cores, mine % cores
    tokens, width = block_input.shape
    _, slots_in, local = w_in.shape
    slots_out = w_outs.shape[1]
    hidden_slots = slots_out - 1

    def numbers(values):
        return jnp.stack([jnp.asarray(v, jnp.int32) for v in values])

    other_inner = 1 - my_inner
    inner_at = [numbers([my_inner]), numbers([other_inner])]
    both_inner = jnp.arange(inner, dtype=jnp.int32)
    lines = [[o * inner + i for o in range(outer)] for i in range(inner)]
    owner_places = numbers(
        [o * inner + i for i in (my_inner, other_inner) for o in range(outer)]
    )
    share_order = numbers(
        [(my_way - w) % ways * cores + (my_core - c) % cores for w in range(ways) for c in range(cores)]
    )
    share_dests = [
        numbers([(my_way + w) % ways * cores + (my_core + c) % cores for w in range(ways)])
        for c in range(cores)
    ]
    share_mine = numbers([mine])

    def to_partner(values):
        return shift(values, "dp", n_dp, inner, 0, 1)


    w_in_s = w_in.transpose(1, 0, 2)
    w_outs_s = w_outs.transpose(1, 0, 2)

    first_slots = [(0, 0), (0, 1), (0, 2), (1, 0)]
    gather_slots = [first_slots[:2], first_slots[2:]] + [[(0, 3 + s), (1, 1 + s)] for s in range(hidden_slots)]
    joined = [list(range(s, min(s + 2, hidden_slots))) for s in range(0, hidden_slots, 2)]
    group_slots = [first_slots] + [[at for s in some for at in ((0, 3 + s), (1, 1 + s))] for some in joined]

    small = jnp.concatenate([in_bias.reshape(1, -1), vectors.reshape(1, -1)], 1).astype(BF16).astype(F32)
    small = collect(small, "dp", n_dp)
    bias_size = in_bias.size
    bias = small[:, :bias_size].reshape((n_dp,) + in_bias.shape).transpose(1, 2, 0, 3).reshape(slots_in, local)
    vec = small[:, bias_size:].reshape((n_dp,) + vectors.shape).transpose(1, 0, 2).reshape(4, width)

    LINE.last = ()
    turns = list(range(len(group_slots)))
    along = []
    for slots in gather_slots:
        cast = cast_group(w_in_s, w_outs_s, slots, LINE.last)
        LINE.last = (cast,)
        along.append(lax.all_gather(cast, "dp", axis=0, axis_index_groups=lines))
    groups = []

    def exchange(g):
        here = gate(along[g])[0]
        groups.append([here, to_partner(here)])

    seg = segment_ids[0]
    start = jnp.sum((seg[None, :] < seg[:, None]).astype(jnp.int32), 1)
    block = min(256, tokens)
    low = start[::block] // block
    place = (jnp.arange(tokens, dtype=jnp.int32) - start).astype(F32)
    freq = 10000.0 ** (-jnp.arange(ROT // 2, dtype=F32) * 2.0 / ROT)
    freq = jnp.tile(jnp.concatenate([freq, freq, jnp.zeros((HDIM - ROT,), F32)]), LANES // HDIM)
    theta = place[:, None] * freq[None, :]
    sine = jnp.sin(theta)
    feature = jnp.arange(LANES) % HDIM
    tables = jnp.stack(
        [
            jnp.cos(theta),
            jnp.where(feature < ROT // 2, -sine, 0.0),
            jnp.where((feature >= ROT // 2) & (feature < ROT), sine, 0.0),
        ]
    )
    LINE.last = LINE.last + (tables, low)

    normed, normed_t, g_t = in_line(normalize, block_input, cotangent, vec)

    hidden, d_hidden, d_bias_hidden, sides = [], [], [], {}

    def hidden_step(s):
        h, dz, db = in_line(hidden_slot, owner_places, normed, cotangent, bias[3 + s : 4 + s], groups[2 + s])
        hidden.append(h)
        d_hidden.append(dz)
        d_bias_hidden.append(db)
        sides.setdefault(1 + s // 2, []).extend([(0, [dz]), (1, [h])])

    legs, shares = {}, {}

    def scatter(out):
        outer_blocks, owners, n, rows, columns = out.shape
        out = out.reshape(outer_blocks * owners * n, rows, columns)
        out = lax.psum_scatter(out, "dp", scatter_dimension=0, axis_index_groups=lines, tiled=True)
        return out.reshape(owners, n, rows, columns)

    def first_next(g, weight=1):
        out = in_line(grad_blocks, inner_at[1], inner, normed_t, g_t, sides[g], [], weight=weight)
        legs[g] = [to_partner(out)]

    def second_next(g):
        out = in_line(grad_blocks, inner_at[0], inner, normed_t, g_t, sides[g], legs[g])
        shares[g] = (scatter(out)[0], [])

    def line_first(g):
        out = scatter(in_line(grad_blocks, both_inner, inner, normed_t, g_t, sides[g], []))
        sent = lax.dynamic_index_in_dim(out, other_inner, 0, False)
        shares[g] = (lax.dynamic_index_in_dim(out, my_inner, 0, False), [to_partner(sent)])

    exchange(0)
    exchange(1)
    groups[0][1] = gate(groups[0][1], weight=5)[0]
    exchange(2)
    to_exchange = list(range(3, 2 + hidden_slots))
    in_first = [(0, 0), (0, 1), (1, 0), (1, 1)]
    qkvd = in_line(qkv_project, owner_places, normed, cotangent, bias, tables, groups[:2], in_first)
    held = ()
    for first in range(local // (attend_pairs(local) * LANES)):
        held = in_line(attend, first, held, low, *qkvd, start.reshape(1, tokens), tables)
        if to_exchange:
            exchange(to_exchange.pop(0))
    attn, d_query, d_keys, d_vals, d_bias_attn = held
    sides[0] = [(0, [d_query]), (0, [d_keys]), (0, [d_vals]), (1, [attn])]
    line_first(0)
    while to_exchange:
        exchange(to_exchange.pop(0))
    for s in joined[0]:
        hidden_step(s)
    ahead_of = len(groups) - 1
    for s in range(len(joined[0]), hidden_slots - 1):
        groups[2 + s][1] = gate(groups[2 + s][1])[0]
        hidden_step(s)
    for g in range(min(ahead_of, 2 + len(hidden)), len(groups)):
        groups[g][1] = gate(groups[g][1])[0]
    first_next(1, 5000)
    for s in range(len(hidden), hidden_slots):
        hidden_step(s)
    for g in range(1, len(joined)):
        first_next(1 + g)

    def first_half(lefts, slots):
        received = []
        for c in range(1, cores):
            out = in_line(project_back, owner_places, share_dests[c], lefts, groups, slots, [], False)
            received.append(shift(out, "tensor", n_tensor, cores, 0, c))
        return received

    def second_half(lefts, slots, received):
        outs = in_line(project_back, owner_places, share_dests[0], lefts, groups, slots, received, True)
        return outs[0], [shift(outs[w], "tensor", n_tensor, cores, w, 0) for w in range(1, ways)]

    def send_share(own):
        return [own] + [shift(own, "tensor", n_tensor, cores, w, 0) for w in range(1, ways)]

    def gather_share(held):
        parts = []
        for part in [held[0]] + gate(*held[1:]):
            parts.append(part)
            for c in range(1, cores):
                parts.append(shift(part, "tensor", n_tensor, cores, 0, c))
        return parts

    back = (
        [d_query, d_keys, d_vals] + d_hidden,
        in_first[:3] + [(2 + s, 0) for s in range(hidden_slots)],
    )
    ahead = ([attn] + hidden, in_first[3:] + [(2 + s, 1) for s in range(hidden_slots)])
    grads, squares = None, []

    def total_next(g, weight=1):
        slots, (own, received) = group_slots[g], shares[g]
        places = jnp.asarray([s if which == 0 else slots_in + s for which, s in slots], jnp.int32)
        out, part = in_line(total_group, grads, own, received, places, slots_in + slots_out, weight=weight)
        squares.append(part)
        return out

    back_half = first_half(*back)
    ahead_half = first_half(*ahead)
    second_next(1)
    own, received = second_half(*back, back_half)
    ahead_own, ahead_received = second_half(*ahead, ahead_half)
    d_x, vector_rows = in_line(finish_input, share_mine, own, received, block_input, cotangent, vec)
    back_held = send_share(d_x)
    out_held = send_share(
        in_line(finish_output, share_mine, ahead_own, ahead_received, block_input, vec)
    )
    for g in range(2, 1 + len(joined)):
        second_next(g)
    grads = total_next(0, 5000)
    back_parts = gather_share(back_held)
    block_input_gradient = in_line(lay_out, share_order, back_parts)
    for g in turns[1:-1]:
        grads = total_next(g)
    out_parts = gather_share(out_held)
    output = in_line(lay_out, share_order, out_parts)

    vector_rows = total_over(vector_rows.reshape(1, -1), "tensor", n_tensor)
    d_bias = jnp.concatenate([d_bias_attn] + d_bias_hidden, 0)
    small = total_over(jnp.concatenate([d_bias.reshape(1, -1), vector_rows], 1), "dp", n_dp)
    g_bias = lax.dynamic_index_in_dim(
        small[0, : slots_in * local].reshape(slots_in, in_bias.shape[1], n_dp, in_bias.shape[2]), me, 2, False
    )
    g_vec = lax.dynamic_index_in_dim(small[0, slots_in * local :].reshape(3, n_dp, width // n_dp), me, 1, False)
    g_vec = jnp.concatenate([g_vec, g_vec[2:]], 0)

    LINE.last = LINE.last + (g_bias, g_vec)
    grads = total_next(turns[-1])
    g_in, g_outs = grads[:slots_in], grads[slots_in:]
    local_squares = (
        jnp.sum(jnp.concatenate(squares, 0)) + jnp.sum(g_bias * g_bias) + jnp.sum(g_vec * g_vec) * (1.0 / n_tensor)
    )
    local_squares = total_over(jnp.full((1, LANES), local_squares), "tensor", n_tensor)
    bit = 1
    while bit < n_dp:
        pairs_at = [(i, i ^ bit) for i in range(n_dp)]
        local_squares = local_squares + lax.ppermute(local_squares, "dp", pairs_at)
        bit *= 2
    grad_norm = jnp.sqrt(local_squares[0, 0])
    factor = CLIP_AT / jnp.maximum(grad_norm, CLIP_AT)

    def slot_major(*arrays):
        return [a.transpose(1, 0, 2) for a in arrays]

    new_in = slot_major(*adamw(w_in_s, *slot_major(w_in_m, w_in_v), g_in, factor, RATE_MATRIX, DECAY_MATRIX))
    new_outs = slot_major(*adamw(w_outs_s, *slot_major(w_outs_m, w_outs_v), g_outs, factor, RATE_MATRIX, DECAY_MATRIX))
    new_bias = adamw(in_bias, in_bias_m, in_bias_v, g_bias, factor, RATE_VECTOR, 0.0)
    new_vec = adamw(vectors, vectors_m, vectors_v, g_vec, factor, RATE_VECTOR, 0.0)
    return (output, block_input_gradient, grad_norm, *new_in, *new_outs, *new_bias, *new_vec)


def solution(mesh):
    rows = P("dp", None)
    matrix = P("dp", None, "tensor")
    small = P(None, "tensor", "dp")
    vector = P(None, "dp")
    return jax.shard_map(
        body,
        mesh=mesh,
        in_specs=(rows,) * 3 + (matrix,) * 6 + (small,) * 3 + (vector,) * 3,
        out_specs=(rows, rows, P()) + (matrix,) * 6 + (small,) * 3 + (vector,) * 3,
        check_vma=False,
    )
```

```python
import jax
import jax.numpy as jnp
from jax import lax
from jax.experimental import pallas as pl
from jax.experimental.pallas import tpu as pltpu
from jax.sharding import PartitionSpec as P

HDIM = 64
ROT = 32
STEP = 10

BETA_ONE = 0.9
BETA_TWO = 0.95
EPSILON = 1e-08
CLIP_AT = 1.0
RATE_MATRIX = 0.06
RATE_VECTOR = 0.6
DECAY_MATRIX = 0.1

F32 = jnp.float32
BF16 = jnp.bfloat16
LANES = 128
ANY = pl.BlockSpec(memory_space=pltpu.HBM)
VMEM_LIMIT = 60 * 1024 * 1024


def nn(a, b):
    return lax.dot_general(a, b, (((1,), (0,)), ((), ())), preferred_element_type=F32)


def nt(a, b):
    return lax.dot_general(a, b, (((1,), (1,)), ((), ())), preferred_element_type=F32)


def whole(*shape):
    return pl.BlockSpec(shape, lambda *_: (0,) * len(shape))


class Line:
    def __init__(self):
        self.last = ()
        self.weight = 1


LINE = Line()


def launch(kernel, grid, in_specs, out_specs, out_shape, args, *, scalars=(), scratch=(), flops=0, moved=0, aliases={}, after=(), weight=1):
    extra = len(after)
    ahead = len(scalars) + len(args)

    def trimmed(*refs):
        return kernel(*refs[:ahead], *refs[ahead + extra :])

    return pl.pallas_call(
        trimmed,
        grid_spec=pltpu.PrefetchScalarGridSpec(
            num_scalar_prefetch=len(scalars),
            grid=grid,
            in_specs=list(in_specs) + [ANY] * extra,
            out_specs=out_specs,
            scratch_shapes=list(scratch),
        ),
        out_shape=out_shape,
        input_output_aliases=aliases,
        compiler_params=pltpu.CompilerParams(vmem_limit_bytes=VMEM_LIMIT),
        cost_estimate=pl.CostEstimate(flops=200000000 * weight * LINE.weight, bytes_accessed=1, transcendentals=0),
    )(*scalars, *args, *after)


def in_line(call, *args, **more):
    out = call(*args, after=LINE.last, **more)
    LINE.last = (out[-1] if isinstance(out, (tuple, list)) else out,)
    return out


def gate(*arrays, weight=1):
    n = len(arrays)

    def kernel(*refs):
        pass

    out = in_line(
        launch,
        kernel,
        (1,),
        [ANY] * n,
        (ANY,) * n,
        tuple(jax.ShapeDtypeStruct(a.shape, a.dtype) for a in arrays),
        arrays,
        aliases={i: i for i in range(n)},
        weight=weight,
    )
    return list(out)


def adamw(weight, first, second, grad, factor, rate, decay):
    clipped = grad * factor
    first = BETA_ONE * first + (1.0 - BETA_ONE) * clipped
    second = BETA_TWO * second + (1.0 - BETA_TWO) * clipped * clipped
    first_hat = first / (1.0 - BETA_ONE**STEP)
    second_hat = second / (1.0 - BETA_TWO**STEP)
    weight = weight - rate * (first_hat / (jnp.sqrt(second_hat) + EPSILON) + decay * weight)
    return (weight, first, second)


def load_weights(place_ref, groups, slots, store, sem):
    copies = []
    for column, (group, slot) in enumerate(slots):
        at = 0
        for part in groups[group]:
            owners, _, rows, local = part.shape
            for r in range(owners):
                to = pl.ds(pl.multiple_of(place_ref[at] * rows, rows), rows)
                copies.append(
                    pltpu.make_async_copy(
                        part.at[r, slot], store.at[to, column * local : (column + 1) * local], sem
                    )
                )
                at += 1
    for copy in copies:
        copy.start()
    for copy in copies:
        copy.wait()


def turn(values, table, sign):
    return (
        values * table[0]
        + sign * (pltpu.roll(values, LANES - ROT // 2, 1) * table[1])
        + sign * (pltpu.roll(values, ROT // 2, 1) * table[2])
    )


def cast_group(w_in, w_outs, slots, deps):
    _, rows, local = w_in.shape

    def kernel(*refs):
        ins, out = refs[: len(slots)], refs[-1]
        for i, ref in enumerate(ins):
            out[i] = ref[0].astype(BF16)

    specs = [
        pl.BlockSpec((1, rows, local), lambda i, s=slot: (s, 0, 0)) for _, slot in slots
    ]
    args = [w_in if which == 0 else w_outs for which, _ in slots]
    n = len(slots)
    return launch(
        kernel,
        (1,),
        specs,
        whole(n, rows, local),
        jax.ShapeDtypeStruct((n, rows, local), BF16),
        args,
        moved=n * rows * local * 6,
        after=deps,
    )


def norm_kernel(x_ref, g_ref, vec_ref, normed_ref, normed_t_ref, g_t_ref):
    x = x_ref[...].astype(F32)
    mean = jnp.mean(x, -1, keepdims=True)
    centered = x - mean
    var = jnp.mean(centered * centered, -1, keepdims=True)
    hat = centered * lax.rsqrt(var + 1e-05)
    normed = (hat * vec_ref[0:1, :] + vec_ref[1:2, :]).astype(BF16)
    normed_ref[...] = normed
    normed_t_ref[...] = normed.T
    g_t_ref[...] = g_ref[...].T


def normalize(x, g, vec, after=()):
    tokens, width = x.shape
    tile = min(256, tokens)
    row = pl.BlockSpec((tile, width), lambda i: (i, 0))
    col = pl.BlockSpec((width, tile), lambda i: (0, i))
    shape = jax.ShapeDtypeStruct((tokens, width), BF16)
    shape_t = jax.ShapeDtypeStruct((width, tokens), BF16)
    return launch(
        norm_kernel,
        (tokens // tile,),
        [row, row, whole(4, width)],
        (row, col, col),
        (shape, shape_t, shape_t),
        (x, g, vec),
        flops=tokens * width * 10,
        moved=tokens * width * 10,
        after=after,
    )


def qkv_project(places, normed, g, bias, tables, groups, slots, after=()):
    tokens, width = normed.shape
    local = groups[0][0].shape[3]
    flat = [part for group in groups for part in group]
    cut = len(groups[0])
    tile = min(512, tokens)

    def kernel(place_ref, x_ref, g_ref, bias_ref, table_ref, *rest):
        parts, (q_ref, k_ref, v_ref, da_ref, store, sem) = rest[:-6], rest[-6:]

        @pl.when(pl.program_id(0) == 0)
        def _():
            nested = [parts[k : k + cut] for k in range(0, len(flat), cut)]
            load_weights(place_ref, nested, slots, store, sem)

        x = x_ref[...]
        for slot, out, scale in ((0, q_ref, HDIM ** (-0.5)), (1, k_ref, 1.0)):
            z = nn(x, store[:, slot * local : (slot + 1) * local]) + bias_ref[slot : slot + 1, :]
            for pair in range(local // LANES):
                at = slice(pair * LANES, (pair + 1) * LANES)
                out[:, at] = (turn(z[:, at], table_ref, 1.0) * scale).astype(BF16)
        v_ref[...] = (nn(x, store[:, 2 * local : 3 * local]) + bias_ref[2:3, :]).astype(BF16)
        da_ref[...] = nn(g_ref[...], store[:, 3 * local : 4 * local]).astype(BF16)

    row = pl.BlockSpec((tile, width), lambda i, *_: (i, 0))
    out = pl.BlockSpec((tile, local), lambda i, *_: (i, 0))
    shape = jax.ShapeDtypeStruct((tokens, local), BF16)
    return launch(
        kernel,
        (tokens // tile,),
        [row, row, whole(7, local), pl.BlockSpec((3, tile, LANES), lambda i, *_: (0, i, 0))] + [ANY] * len(flat),
        (out,) * 4,
        (shape,) * 4,
        (normed, g, bias, tables, *flat),
        scalars=(places,),
        scratch=(pltpu.VMEM((width, 4 * local), BF16), pltpu.SemaphoreType.DMA),
        flops=2 * tokens * width * 4 * local,
        moved=tokens * width * 4 + width * local * 8,
        after=after,
    )


def attend(first, held, low, query, keys, vals, d_attn, start, tables, after=()):
    tokens, local = query.shape
    block = min(256, tokens)
    count = tokens // block
    pairs = attend_pairs(local)
    heads = 2 * pairs
    wide = pairs * LANES
    scale = HDIM ** (-0.5)
    lanes = [slice(p * LANES, (p + 1) * LANES) for p in range(pairs)]

    def kernel(low_ref, q_ref, k_ref, v_ref, do_ref, start_ref, table_ref, *rest):
        (o_ref, dq_ref, dk_ref, dv_ref, db_ref,
         k_half, v_half, k_t, v_t, s_buf, dp_buf, o_t, dq_t, dk_sum, dv_sum) = rest[len(held):]
        i = pl.program_id(0)
        first_lanes = lax.broadcasted_iota(jnp.int32, (1, LANES), 1) < HDIM
        zero = jnp.zeros((), BF16)

        def apart(pair):
            return jnp.where(first_lanes, pair, zero), jnp.where(first_lanes, zero, pair)

        @pl.when(i == 0)
        def _():
            for b in range(count):
                at = slice(b * block, (b + 1) * block)
                for source, half, flipped in ((k_ref, k_half, k_t), (v_ref, v_half, v_t)):
                    for p in range(pairs):
                        part = source[at, lanes[p]]
                        half[2 * p, at, :], half[2 * p + 1, at, :] = apart(part)
                        flipped[p, b] = part.T
            dk_sum[...] = jnp.zeros_like(dk_sum)
            dv_sum[...] = jnp.zeros_like(dv_sum)
            db_ref[...] = jnp.zeros_like(db_ref)

        q = [q_ref[:, at] for at in lanes]
        do = [do_ref[:, at] for at in lanes]
        q_cat = [jnp.concatenate(apart(pair), 0) for pair in q]
        do_cat = [jnp.concatenate(apart(pair), 0) for pair in do]
        t_place = i * block + lax.broadcasted_iota(jnp.int32, (1, block), 1)
        t_start = start_ref[...]
        low_block = low_ref[i]
        o_t[...] = jnp.zeros_like(o_t)
        dq_t[...] = jnp.zeros_like(dq_t)

        def score(b, tops):
            at = pl.ds(pl.multiple_of(b * block, block), block)
            u_place = b * block + lax.broadcasted_iota(jnp.int32, (block, 1), 0)
            allowed = (u_place >= t_start) & (u_place <= t_place)
            new = []
            for h in range(heads):
                s = jnp.where(allowed, nt(k_half[h, at, :], q[h // 2]), -1e30)
                s_buf[h, b] = s
                dp_buf[h, b] = nt(v_half[h, at, :], do[h // 2])
                new.append(jnp.maximum(tops[h], jnp.max(s, 0, keepdims=True)))
            return tuple(new)

        lowest = jnp.full((1, block), -jnp.inf, F32)
        tops = lax.fori_loop(low_block, i + 1, score, (lowest,) * heads)

        def weigh(b, sums):
            new = []
            for h in range(heads):
                p = jnp.exp(s_buf[h, b] - tops[h])
                s_buf[h, b] = p
                new.append(sums[2 * h] + jnp.sum(p, 0, keepdims=True))
                new.append(sums[2 * h + 1] + jnp.sum(p * dp_buf[h, b], 0, keepdims=True))
            return tuple(new)

        none = jnp.zeros((1, block), F32)
        sums = lax.fori_loop(low_block, i + 1, weigh, (none,) * (2 * heads))
        inverse = [1.0 / sums[2 * h] for h in range(heads)]
        delta = [sums[2 * h + 1] * inverse[h] for h in range(heads)]

        def spread(b, carry):
            at = pl.ds(pl.multiple_of(b * block, block), block)
            probs, grads = [], []
            for h in range(heads):
                rows = slice(h * HDIM, (h + 1) * HDIM)
                inside = slice(h % 2 * HDIM, (h % 2 + 1) * HDIM)
                p = s_buf[h, b] * inverse[h]
                ds = (p * (dp_buf[h, b] - delta[h])).astype(BF16)
                p = p.astype(BF16)
                o_t[rows, :] += nn(v_t[h // 2, b, inside, :], p)
                dq_t[rows, :] += nn(k_t[h // 2, b, inside, :], ds)
                probs.append(p)
                grads.append(ds)
            for p in range(pairs):
                dv_sum[at, lanes[p]] += nn(jnp.concatenate(probs[2 * p : 2 * p + 2], 1), do_cat[p])
                dk_sum[at, lanes[p]] += nn(jnp.concatenate(grads[2 * p : 2 * p + 2], 1), q_cat[p])
            return carry

        lax.fori_loop(low_block, i + 1, spread, 0)
        o_ref[...] = o_t[...].T.astype(BF16)
        here = pl.ds(pl.multiple_of(i * block, block), block)
        table = [table_ref[n, here, :] for n in range(3)]
        for at in lanes:
            dq = turn(dq_t[at, :].T * scale, table, -1.0).astype(BF16)
            dq_ref[:, at] = dq
            db_ref[0:1, at] += jnp.sum(dq.astype(F32), 0, keepdims=True)

        @pl.when(i == count - 1)
        def _():
            for at in lanes:
                dk = turn(dk_sum[:, at], table_ref, -1.0).astype(BF16)
                dv = dv_sum[:, at].astype(BF16)
                dk_ref[:, at] = dk
                dv_ref[:, at] = dv
                db_ref[1:2, at] = jnp.sum(dk.astype(F32), 0, keepdims=True)
                db_ref[2:3, at] = jnp.sum(dv.astype(F32), 0, keepdims=True)

    part = pl.BlockSpec((block, wide), lambda i, *_: (i, first))
    column = pl.BlockSpec((tokens, wide), lambda i, *_: (0, first))
    shape = jax.ShapeDtypeStruct((tokens, local), BF16)
    return launch(
        kernel,
        (count,),
        [part, column, column, part, pl.BlockSpec((1, block), lambda i, *_: (0, i)), whole(3, tokens, LANES)]
        + [ANY] * len(held),
        (part, part, column, column, pl.BlockSpec((3, wide), lambda i, *_: (0, first))),
        (shape,) * 4 + (jax.ShapeDtypeStruct((3, local), F32),),
        (query, keys, vals, d_attn, start, tables, *held),
        scalars=(low,),
        aliases={7 + i: i for i in range(len(held))},
        scratch=(
            pltpu.VMEM((heads, tokens, LANES), BF16),
            pltpu.VMEM((heads, tokens, LANES), BF16),
            pltpu.VMEM((pairs, count, LANES, block), BF16),
            pltpu.VMEM((pairs, count, LANES, block), BF16),
            pltpu.VMEM((heads, count, block, block), F32),
            pltpu.VMEM((heads, count, block, block), F32),
            pltpu.VMEM((wide, block), F32),
            pltpu.VMEM((wide, block), F32),
            pltpu.VMEM((tokens, wide), F32),
            pltpu.VMEM((tokens, wide), F32),
        ),
        after=after,
    )


def attend_pairs(local):
    return 2 if local % (2 * LANES) == 0 else 1


def hidden_slot(places, normed, g, bias, group, after=()):
    tokens, width = normed.shape
    local = group[0].shape[3]
    tile = min(512, tokens)

    def kernel(place_ref, x_ref, g_ref, bias_ref, *rest):
        parts, (h_ref, dz_ref, db_ref, store, sem) = rest[:-5], rest[-5:]

        @pl.when(pl.program_id(0) == 0)
        def _():
            load_weights(place_ref, [parts], [(0, 0), (0, 1)], store, sem)
            db_ref[...] = jnp.zeros_like(db_ref)

        v = nn(x_ref[...], store[:, :local]) + bias_ref[...]
        dh = nn(g_ref[...], store[:, local:])
        square = v * v
        t = jnp.tanh(0.7978845608 * (v + 0.044715 * (square * v)))
        half = 0.5 * (1.0 + t)
        h_ref[...] = (v * half).astype(BF16)
        slope = half + (0.5 * v) * (1.0 - t * t) * (0.7978845608 + (3.0 * 0.044715 * 0.7978845608) * square)
        dz = (dh * slope).astype(BF16)
        dz_ref[...] = dz
        db_ref[...] += jnp.sum(dz.astype(F32), 0, keepdims=True)

    row = pl.BlockSpec((tile, width), lambda i, *_: (i, 0))
    out = pl.BlockSpec((tile, local), lambda i, *_: (i, 0))
    shape = jax.ShapeDtypeStruct((tokens, local), BF16)
    return launch(
        kernel,
        (tokens // tile,),
        [row, row, whole(1, local)] + [ANY] * len(group),
        (out, out, whole(1, local)),
        (shape, shape, jax.ShapeDtypeStruct((1, local), F32)),
        (normed, g, bias, *group),
        scalars=(places,),
        scratch=(pltpu.VMEM((width, 2 * local), BF16), pltpu.SemaphoreType.DMA),
        flops=4 * tokens * width * local,
        moved=tokens * width * 4 + width * local * 4,
        after=after,
        weight=5,
    )


def grad_blocks(inner_at, inner, normed_t, g_t, sides, received, after=(), weight=1):
    width, tokens = normed_t.shape
    outer = lax.axis_size("dp") // inner
    owners = inner_at.shape[0]
    n = len(sides)
    cuts = len(sides[0][1])
    piece_width = sides[0][1][0].shape[1]
    local = cuts * piece_width
    rows = width // (outer * inner)

    def kernel(inner_ref, *rest):
        lefts = rest[:2]
        rights = rest[2 : 2 + n * cuts]
        adds = rest[2 + n * cuts : -1]
        out = rest[-1]
        step = pl.program_id(1)
        for i, (side, _) in enumerate(sides):

            @pl.when(step == i)
            def _(i=i, side=side):
                left = lefts[side][...].reshape(outer * rows, tokens)
                for c in range(cuts):
                    at = slice(c * piece_width, (c + 1) * piece_width)
                    total = nn(left, rights[i * cuts + c][...]).reshape(outer, rows, piece_width)
                    for add in adds:
                        total += add[:, 0, 0, :, at].astype(F32)
                    out[:, 0, 0, :, at] = total.astype(BF16)

    left = pl.BlockSpec((outer, 1, rows, tokens), lambda o, i, inner_ref, *_: (0, inner_ref[o], 0, 0))
    piece = pl.BlockSpec((outer, 1, 1, rows, local), lambda o, i, *_: (0, o, i, 0, 0))
    four = (outer, inner, rows, tokens)
    return launch(
        kernel,
        (owners, n),
        [left, left] + [whole(tokens, piece_width)] * (n * cuts) + [piece] * len(received),
        piece,
        jax.ShapeDtypeStruct((outer, owners, n, rows, local), BF16),
        (normed_t.reshape(four), g_t.reshape(four), *[right for _, rights in sides for right in rights], *received),
        scalars=(inner_at,),
        after=after,
        weight=weight,
    )


def project_back(places, shares, lefts, groups, slots, received, split, after=()):
    tokens = lefts[0].shape[0]
    local = groups[0][0].shape[3]
    count = shares.shape[0]
    share = tokens // lax.axis_size("tensor")
    tile = min(512, share)
    steps = share // tile
    width = places.shape[0] * groups[0][0].shape[2]
    m = len(lefts)
    depth = len(slots) * local
    flat = [part for group in groups for part in group]
    cut = len(groups[0])
    n_groups = len(flat)

    def kernel(place_ref, shares_ref, *rest):
        left_refs = rest[:m]
        refs = rest[m : m + n_groups]
        adds = rest[m + n_groups : m + n_groups + len(received)]
        outs = rest[m + n_groups + len(received) : -2]
        store, sem = rest[-2:]
        step, part = pl.program_id(0), pl.program_id(1)

        @pl.when((step == 0) & (part == 0))
        def _():
            nested = [refs[k : k + cut] for k in range(0, n_groups, cut)]
            load_weights(place_ref, nested, slots, store, sem)

        total = nt(jnp.concatenate([left[...] for left in left_refs], 1), store[...])
        for add in adds:
            total += add[...].astype(F32)
        if not split:
            outs[0][...] = total.astype(BF16)
        else:
            at = pl.ds(pl.multiple_of(part * tile, tile), tile)
            for j, out in enumerate(outs):

                @pl.when(step == j)
                def _(out=out):
                    out[at, :] = total.astype(out.dtype)

    def left(array):
        return pl.BlockSpec((tile, array.shape[1]), lambda i, j, p_ref, s_ref: (s_ref[i] * steps + j, 0))

    piece = pl.BlockSpec((tile, width), lambda i, j, *_: (i * steps + j, 0))
    if split:
        out_specs = (whole(share, width),) * count
        out_shape = tuple(jax.ShapeDtypeStruct((share, width), F32 if j == 0 else BF16) for j in range(count))
    else:
        out_specs = piece
        out_shape = jax.ShapeDtypeStruct((count * share, width), BF16)
    return launch(
        kernel,
        (count, steps),
        [left(array) for array in lefts] + [ANY] * n_groups + [piece] * len(received),
        out_specs,
        out_shape,
        (*lefts, *flat, *received),
        scalars=(places, shares),
        scratch=(pltpu.VMEM((width, depth), BF16), pltpu.SemaphoreType.DMA),
        flops=2 * count * share * width * depth,
        moved=width * depth * 2 + count * share * (depth + width) * 2,
        after=after,
    )


def finish_output(mine, own, received, x, vec, after=()):
    share, width = own.shape
    tile = min(256, share)
    steps = share // tile

    def kernel(mine_ref, own_ref, x_ref, vec_ref, *rest):
        total = own_ref[...]
        for ref in rest[:-1]:
            total += ref[...].astype(F32)
        rest[-1][...] = (x_ref[...].astype(F32) + total + vec_ref[2:3, :] + vec_ref[3:4, :]).astype(BF16)

    row = pl.BlockSpec((tile, width), lambda i, *_: (i, 0))
    far = pl.BlockSpec((tile, width), lambda i, mine_ref: (mine_ref[0] * steps + i, 0))
    return launch(
        kernel,
        (steps,),
        [row, far, whole(4, width)] + [row] * len(received),
        row,
        jax.ShapeDtypeStruct((share, width), BF16),
        (own, x, vec, *received),
        scalars=(mine,),
        moved=share * width * 10,
        after=after,
    )


def finish_input(mine, own, received, x, g, vec, after=()):
    share, width = own.shape
    tile = min(256, share)
    steps = share // tile

    def kernel(mine_ref, own_ref, x_ref, g_ref, vec_ref, *rest):
        grad_ref, rows_ref = rest[-2:]
        dn = own_ref[...]
        for ref in rest[:-2]:
            dn += ref[...].astype(F32)
        x = x_ref[...].astype(F32)
        g = g_ref[...].astype(F32)
        mean = jnp.mean(x, -1, keepdims=True)
        centered = x - mean
        var = jnp.mean(centered * centered, -1, keepdims=True)
        inverse = lax.rsqrt(var + 1e-05)
        hat = centered * inverse
        e = dn * vec_ref[0:1, :]
        back = inverse * (e - jnp.mean(e, -1, keepdims=True) - hat * jnp.mean(e * hat, -1, keepdims=True))
        grad_ref[...] = (g + back).astype(BF16)

        @pl.when(pl.program_id(0) == 0)
        def _():
            rows_ref[...] = jnp.zeros_like(rows_ref)

        rows_ref[0:1, :] += jnp.sum(dn * hat, 0, keepdims=True)
        rows_ref[1:2, :] += jnp.sum(dn, 0, keepdims=True)
        rows_ref[2:3, :] += jnp.sum(g, 0, keepdims=True)

    row = pl.BlockSpec((tile, width), lambda i, *_: (i, 0))
    far = pl.BlockSpec((tile, width), lambda i, mine_ref: (mine_ref[0] * steps + i, 0))
    return launch(
        kernel,
        (steps,),
        [row, far, far, whole(4, width)] + [row] * len(received),
        (row, whole(3, width)),
        (jax.ShapeDtypeStruct((share, width), BF16), jax.ShapeDtypeStruct((3, width), F32)),
        (own, x, g, vec, *received),
        scalars=(mine,),
        moved=share * width * 12,
        after=after,
    )


def lay_out(order, parts, after=()):
    share, width = parts[0].shape
    count = len(parts)
    tile = min(256, share)
    steps = share // tile

    def kernel(order_ref, *rest):
        for r in range(count):

            @pl.when(pl.program_id(0) == r)
            def _(r=r):
                rest[count][...] = rest[r][...]

    def fetch(r):
        return pl.BlockSpec(
            (tile, width), lambda i, j, *_: (jnp.where(i == r, j, jnp.where(i < r, 0, steps - 1)), 0)
        )

    return launch(
        kernel,
        (count, steps),
        [fetch(r) for r in range(count)],
        pl.BlockSpec((tile, width), lambda i, j, order_ref: (order_ref[i] * steps + j, 0)),
        jax.ShapeDtypeStruct((share * count, width), parts[0].dtype),
        parts,
        scalars=(order,),
        moved=share * count * width * 4,
        after=after,
    )


def total_group(grads, own, received, places, slots_in_all, after=(), weight=1):
    n, rows, local = own.shape

    def kernel(places_ref, own_ref, *rest):
        out, squares = rest[-2:]
        total = own_ref[0].astype(F32)
        for ref in rest[: len(received)]:
            total += ref[0].astype(F32)
        out[0] = total

        @pl.when(pl.program_id(0) == 0)
        def _():
            squares[...] = jnp.zeros_like(squares)

        squares[...] += jnp.sum(total * total, 0, keepdims=True)

    piece = pl.BlockSpec((1, rows, local), lambda i, *_: (i, 0, 0))
    out = pl.BlockSpec((1, rows, local), lambda i, places_ref: (places_ref[i], 0, 0))
    first = grads is None
    return launch(
        kernel,
        (n,),
        [piece] * (1 + len(received)) + ([] if first else [ANY]),
        (out, whole(1, local)),
        (jax.ShapeDtypeStruct((slots_in_all, rows, local), F32), jax.ShapeDtypeStruct((1, local), F32)),
        (own, *received) + (() if first else (grads,)),
        scalars=(places,),
        aliases={} if first else {2 + len(received): 0},
        after=after,
        weight=weight,
    )


def collect(values, axis, count):
    rows = [values]
    for k in range(1, count):
        rows.append(lax.ppermute(values, axis, [(i, (i + k) % count) for i in range(count)]))
    rows = jnp.concatenate(rows[::-1] * 2, 0)
    return lax.dynamic_slice_in_dim(rows, count - 1 - lax.axis_index(axis), count, 0)


def total_over(values, axis, count):
    bit = 1
    while bit < count:
        values = values + lax.ppermute(values, axis, [(i, i ^ bit) for i in range(count)])
        bit *= 2
    return values


def shift(values, axis, count, inner, outer_by, inner_by):
    outer = count // inner
    pairs = [
        (o * inner + i, (o + outer_by) % outer * inner + (i + inner_by) % inner)
        for o in range(outer)
        for i in range(inner)
    ]
    return lax.ppermute(values, axis, pairs)


def body(
    block_input,
    cotangent,
    segment_ids,
    w_in,
    w_in_m,
    w_in_v,
    w_outs,
    w_outs_m,
    w_outs_v,
    in_bias,
    in_bias_m,
    in_bias_v,
    vectors,
    vectors_m,
    vectors_v,
):
    n_dp = lax.axis_size("dp")
    n_tensor = lax.axis_size("tensor")
    inner = 2
    outer = n_dp // inner
    cores = 2
    ways = n_tensor // cores
    me = lax.axis_index("dp")
    mine = lax.axis_index("tensor")
    my_outer, my_inner = me // inner, me % inner
    my_way, my_core = mine // cores, mine % cores
    tokens, width = block_input.shape
    _, slots_in, local = w_in.shape
    slots_out = w_outs.shape[1]
    hidden_slots = slots_out - 1

    def numbers(values):
        return jnp.stack([jnp.asarray(v, jnp.int32) for v in values])

    other_inner = 1 - my_inner
    inner_at = [numbers([my_inner]), numbers([other_inner])]
    both_inner = jnp.arange(inner, dtype=jnp.int32)
    lines = [[o * inner + i for o in range(outer)] for i in range(inner)]
    owner_places = numbers(
        [o * inner + i for i in (my_inner, other_inner) for o in range(outer)]
    )
    share_order = numbers(
        [(my_way - w) % ways * cores + (my_core - c) % cores for w in range(ways) for c in range(cores)]
    )
    share_dests = [
        numbers([(my_way + w) % ways * cores + (my_core + c) % cores for w in range(ways)])
        for c in range(cores)
    ]
    share_mine = numbers([mine])

    def to_partner(values):
        return shift(values, "dp", n_dp, inner, 0, 1)


    w_in_s = w_in.transpose(1, 0, 2)
    w_outs_s = w_outs.transpose(1, 0, 2)

    first_slots = [(0, 0), (0, 1), (0, 2), (1, 0)]
    gather_slots = [first_slots[:2], first_slots[2:]] + [[(0, 3 + s), (1, 1 + s)] for s in range(hidden_slots)]
    joined = [list(range(s, min(s + 2, hidden_slots))) for s in range(0, hidden_slots, 2)]
    group_slots = [first_slots] + [[at for s in some for at in ((0, 3 + s), (1, 1 + s))] for some in joined]

    small = jnp.concatenate([in_bias.reshape(1, -1), vectors.reshape(1, -1)], 1).astype(BF16).astype(F32)
    small = collect(small, "dp", n_dp)
    bias_size = in_bias.size
    bias = small[:, :bias_size].reshape((n_dp,) + in_bias.shape).transpose(1, 2, 0, 3).reshape(slots_in, local)
    vec = small[:, bias_size:].reshape((n_dp,) + vectors.shape).transpose(1, 0, 2).reshape(4, width)

    LINE.last = ()
    LINE.weight = 1
    turns = list(range(len(group_slots)))
    along = []
    for slots in gather_slots:
        cast = cast_group(w_in_s, w_outs_s, slots, LINE.last)
        LINE.last = (cast,)
        along.append(lax.all_gather(cast, "dp", axis=0, axis_index_groups=lines))
    groups = []

    def exchange(g):
        here = gate(along[g])[0]
        groups.append([here, to_partner(here)])

    seg = segment_ids[0]
    start = jnp.sum((seg[None, :] < seg[:, None]).astype(jnp.int32), 1)
    block = min(256, tokens)
    low = start[::block] // block
    place = (jnp.arange(tokens, dtype=jnp.int32) - start).astype(F32)
    freq = 10000.0 ** (-jnp.arange(ROT // 2, dtype=F32) * 2.0 / ROT)
    freq = jnp.tile(jnp.concatenate([freq, freq, jnp.zeros((HDIM - ROT,), F32)]), LANES // HDIM)
    theta = place[:, None] * freq[None, :]
    sine = jnp.sin(theta)
    feature = jnp.arange(LANES) % HDIM
    tables = jnp.stack(
        [
            jnp.cos(theta),
            jnp.where(feature < ROT // 2, -sine, 0.0),
            jnp.where((feature >= ROT // 2) & (feature < ROT), sine, 0.0),
        ]
    )
    LINE.last = LINE.last + (tables, low)

    normed, normed_t, g_t = in_line(normalize, block_input, cotangent, vec)

    hidden, d_hidden, d_bias_hidden, sides = [], [], [], {}

    def hidden_step(s):
        h, dz, db = in_line(hidden_slot, owner_places, normed, cotangent, bias[3 + s : 4 + s], groups[2 + s])
        hidden.append(h)
        d_hidden.append(dz)
        d_bias_hidden.append(db)
        sides.setdefault(1 + s // 2, []).extend([(0, [dz]), (1, [h])])

    legs, shares = {}, {}

    def scatter(out):
        outer_blocks, owners, n, rows, columns = out.shape
        out = out.reshape(outer_blocks * owners * n, rows, columns)
        out = lax.psum_scatter(out, "dp", scatter_dimension=0, axis_index_groups=lines, tiled=True)
        return out.reshape(owners, n, rows, columns)

    def first_next(g, weight=1):
        out = in_line(grad_blocks, inner_at[1], inner, normed_t, g_t, sides[g], [], weight=weight)
        legs[g] = [to_partner(out)]

    def second_next(g):
        out = in_line(grad_blocks, inner_at[0], inner, normed_t, g_t, sides[g], legs[g])
        shares[g] = (scatter(out)[0], [])

    def line_first(g):
        out = scatter(in_line(grad_blocks, both_inner, inner, normed_t, g_t, sides[g], []))
        sent = lax.dynamic_index_in_dim(out, other_inner, 0, False)
        shares[g] = (lax.dynamic_index_in_dim(out, my_inner, 0, False), [to_partner(sent)])

    exchange(0)
    exchange(1)
    groups[0][1] = gate(groups[0][1], weight=5)[0]
    exchange(2)
    to_exchange = list(range(3, 2 + hidden_slots))
    in_first = [(0, 0), (0, 1), (1, 0), (1, 1)]
    qkvd = in_line(qkv_project, owner_places, normed, cotangent, bias, tables, groups[:2], in_first)
    held = ()
    for first in range(local // (attend_pairs(local) * LANES)):
        held = in_line(attend, first, held, low, *qkvd, start.reshape(1, tokens), tables)
        if to_exchange:
            exchange(to_exchange.pop(0))
    attn, d_query, d_keys, d_vals, d_bias_attn = held
    sides[0] = [(0, [d_query]), (0, [d_keys]), (0, [d_vals]), (1, [attn])]
    line_first(0)
    while to_exchange:
        exchange(to_exchange.pop(0))
    for s in joined[0]:
        hidden_step(s)
    ahead_of = len(groups) - 1
    for s in range(len(joined[0]), hidden_slots - 1):
        groups[2 + s][1] = gate(groups[2 + s][1])[0]
        hidden_step(s)
    for g in range(min(ahead_of, 2 + len(hidden)), len(groups)):
        groups[g][1] = gate(groups[g][1])[0]
    first_next(1, 5000)
    for s in range(len(hidden), hidden_slots):
        hidden_step(s)
    LINE.weight = 5000

    def first_half(lefts, slots):
        received = []
        for c in range(1, cores):
            out = in_line(project_back, owner_places, share_dests[c], lefts, groups, slots, [], False)
            received.append(shift(out, "tensor", n_tensor, cores, 0, c))
        return received

    def second_half(lefts, slots, received):
        outs = in_line(project_back, owner_places, share_dests[0], lefts, groups, slots, received, True)
        return outs[0], [shift(outs[w], "tensor", n_tensor, cores, w, 0) for w in range(1, ways)]

    def send_share(own):
        return [own] + [shift(own, "tensor", n_tensor, cores, w, 0) for w in range(1, ways)]

    def gather_share(held):
        return [held[0]] + gate(*held[1:])

    def spread_share(held):
        parts = []
        for part in held:
            parts.append(part)
            for c in range(1, cores):
                parts.append(shift(part, "tensor", n_tensor, cores, 0, c))
        return parts

    back = (
        [d_query, d_keys, d_vals] + d_hidden,
        in_first[:3] + [(2 + s, 0) for s in range(hidden_slots)],
    )
    ahead = ([attn] + hidden, in_first[3:] + [(2 + s, 1) for s in range(hidden_slots)])
    grads, squares = None, []

    def total_next(g, weight=1):
        slots, (own, received) = group_slots[g], shares[g]
        places = jnp.asarray([s if which == 0 else slots_in + s for which, s in slots], jnp.int32)
        out, part = in_line(total_group, grads, own, received, places, slots_in + slots_out, weight=weight)
        squares.append(part)
        return out

    for g in range(2, 1 + len(joined)):
        first_next(g)
    back_half = first_half(*back)
    ahead_half = first_half(*ahead)
    own, received = second_half(*back, back_half)
    second_next(1)
    ahead_own, ahead_received = second_half(*ahead, ahead_half)
    d_x, vector_rows = in_line(finish_input, share_mine, own, received, block_input, cotangent, vec)
    back_held = send_share(d_x)
    out_held = send_share(
        in_line(finish_output, share_mine, ahead_own, ahead_received, block_input, vec)
    )
    for g in range(2, 1 + len(joined)):
        second_next(g)
    grads = total_next(0)
    vector_rows = total_over(vector_rows.reshape(1, -1), "tensor", n_tensor)
    d_bias = jnp.concatenate([d_bias_attn] + d_bias_hidden, 0)
    small = total_over(jnp.concatenate([d_bias.reshape(1, -1), vector_rows], 1), "dp", n_dp)
    g_bias = lax.dynamic_index_in_dim(
        small[0, : slots_in * local].reshape(slots_in, in_bias.shape[1], n_dp, in_bias.shape[2]), me, 2, False
    )
    g_vec = lax.dynamic_index_in_dim(small[0, slots_in * local :].reshape(3, n_dp, width // n_dp), me, 1, False)
    g_vec = jnp.concatenate([g_vec, g_vec[2:]], 0)

    back_parts = spread_share(gather_share(back_held))
    for g in turns[1:-1]:
        grads = total_next(g)
    block_input_gradient = in_line(lay_out, share_order, back_parts)
    out_parts = spread_share(gather_share(out_held))
    LINE.last = LINE.last + (g_bias, g_vec)
    grads = total_next(turns[-1])
    output = in_line(lay_out, share_order, out_parts)
    LINE.weight = 1
    g_in, g_outs = grads[:slots_in], grads[slots_in:]
    local_squares = (
        jnp.sum(jnp.concatenate(squares, 0)) + jnp.sum(g_bias * g_bias) + jnp.sum(g_vec * g_vec) * (1.0 / n_tensor)
    )
    local_squares = total_over(jnp.full((1, LANES), local_squares), "tensor", n_tensor)
    local_squares = total_over(local_squares, "dp", n_dp)
    grad_norm = jnp.sqrt(local_squares[0, 0])
    factor = CLIP_AT / jnp.maximum(grad_norm, CLIP_AT)

    def slot_major(*arrays):
        return [a.transpose(1, 0, 2) for a in arrays]

    new_in = slot_major(*adamw(w_in_s, *slot_major(w_in_m, w_in_v), g_in, factor, RATE_MATRIX, DECAY_MATRIX))
    new_outs = slot_major(*adamw(w_outs_s, *slot_major(w_outs_m, w_outs_v), g_outs, factor, RATE_MATRIX, DECAY_MATRIX))
    new_bias = adamw(in_bias, in_bias_m, in_bias_v, g_bias, factor, RATE_VECTOR, 0.0)
    new_vec = adamw(vectors, vectors_m, vectors_v, g_vec, factor, RATE_VECTOR, 0.0)
    return (output, block_input_gradient, grad_norm, *new_in, *new_outs, *new_bias, *new_vec)


def solution(mesh):
    rows = P("dp", None)
    matrix = P("dp", None, "tensor")
    small = P(None, "tensor", "dp")
    vector = P(None, "dp")
    return jax.shard_map(
        body,
        mesh=mesh,
        in_specs=(rows,) * 3 + (matrix,) * 6 + (small,) * 3 + (vector,) * 3,
        out_specs=(rows, rows, P()) + (matrix,) * 6 + (small,) * 3 + (vector,) * 3,
        check_vma=False,
    )
```

```python
import jax
import jax.numpy as jnp
from jax import lax
from jax.experimental import pallas as pl
from jax.experimental.pallas import tpu as pltpu
from jax.sharding import PartitionSpec as P

HDIM = 64
ROT = 32
STEP = 10

BETA_ONE = 0.9
BETA_TWO = 0.95
EPSILON = 1e-08
CLIP_AT = 1.0
RATE_MATRIX = 0.06
RATE_VECTOR = 0.6
DECAY_MATRIX = 0.1

F32 = jnp.float32
BF16 = jnp.bfloat16
LANES = 128
ANY = pl.BlockSpec(memory_space=pltpu.HBM)
VMEM_LIMIT = 60 * 1024 * 1024


def nn(a, b):
    return lax.dot_general(a, b, (((1,), (0,)), ((), ())), preferred_element_type=F32)


def nt(a, b):
    return lax.dot_general(a, b, (((1,), (1,)), ((), ())), preferred_element_type=F32)


def whole(*shape):
    return pl.BlockSpec(shape, lambda *_: (0,) * len(shape))


class Line:
    def __init__(self):
        self.last = ()
        self.weight = 1


LINE = Line()


def launch(kernel, grid, in_specs, out_specs, out_shape, args, *, scalars=(), scratch=(), flops=0, moved=0, aliases={}, after=(), weight=1):
    extra = len(after)
    ahead = len(scalars) + len(args)

    def trimmed(*refs):
        return kernel(*refs[:ahead], *refs[ahead + extra :])

    return pl.pallas_call(
        trimmed,
        grid_spec=pltpu.PrefetchScalarGridSpec(
            num_scalar_prefetch=len(scalars),
            grid=grid,
            in_specs=list(in_specs) + [ANY] * extra,
            out_specs=out_specs,
            scratch_shapes=list(scratch),
        ),
        out_shape=out_shape,
        input_output_aliases=aliases,
        compiler_params=pltpu.CompilerParams(vmem_limit_bytes=VMEM_LIMIT),
        cost_estimate=pl.CostEstimate(flops=200000000 * weight * LINE.weight, bytes_accessed=1, transcendentals=0),
    )(*scalars, *args, *after)


def in_line(call, *args, **more):
    out = call(*args, after=LINE.last, **more)
    LINE.last = (out[-1] if isinstance(out, (tuple, list)) else out,)
    return out


def gate(*arrays, weight=1):
    n = len(arrays)

    def kernel(*refs):
        pass

    out = in_line(
        launch,
        kernel,
        (1,),
        [ANY] * n,
        (ANY,) * n,
        tuple(jax.ShapeDtypeStruct(a.shape, a.dtype) for a in arrays),
        arrays,
        aliases={i: i for i in range(n)},
        weight=weight,
    )
    return list(out)


def adamw(weight, first, second, grad, factor, rate, decay):
    clipped = grad * factor
    first = BETA_ONE * first + (1.0 - BETA_ONE) * clipped
    second = BETA_TWO * second + (1.0 - BETA_TWO) * clipped * clipped
    first_hat = first / (1.0 - BETA_ONE**STEP)
    second_hat = second / (1.0 - BETA_TWO**STEP)
    weight = weight - rate * (first_hat / (jnp.sqrt(second_hat) + EPSILON) + decay * weight)
    return (weight, first, second)


def load_weights(place_ref, groups, slots, store, sem):
    copies = []
    for column, (group, slot) in enumerate(slots):
        at = 0
        for part in groups[group]:
            owners, _, rows, local = part.shape
            for r in range(owners):
                to = pl.ds(pl.multiple_of(place_ref[at] * rows, rows), rows)
                copies.append(
                    pltpu.make_async_copy(
                        part.at[r, slot], store.at[to, column * local : (column + 1) * local], sem
                    )
                )
                at += 1
    for copy in copies:
        copy.start()
    for copy in copies:
        copy.wait()


def turn(values, table, sign):
    return (
        values * table[0]
        + sign * (pltpu.roll(values, LANES - ROT // 2, 1) * table[1])
        + sign * (pltpu.roll(values, ROT // 2, 1) * table[2])
    )


def cast_group(w_in, w_outs, slots, deps):
    _, rows, local = w_in.shape

    def kernel(*refs):
        ins, out = refs[: len(slots)], refs[-1]
        for i, ref in enumerate(ins):
            out[i] = ref[0].astype(BF16)

    specs = [
        pl.BlockSpec((1, rows, local), lambda i, s=slot: (s, 0, 0)) for _, slot in slots
    ]
    args = [w_in if which == 0 else w_outs for which, _ in slots]
    n = len(slots)
    return launch(
        kernel,
        (1,),
        specs,
        whole(n, rows, local),
        jax.ShapeDtypeStruct((n, rows, local), BF16),
        args,
        moved=n * rows * local * 6,
        after=deps,
    )


def norm_kernel(x_ref, g_ref, vec_ref, normed_ref, normed_t_ref, g_t_ref):
    x = x_ref[...].astype(F32)
    mean = jnp.mean(x, -1, keepdims=True)
    centered = x - mean
    var = jnp.mean(centered * centered, -1, keepdims=True)
    hat = centered * lax.rsqrt(var + 1e-05)
    normed = (hat * vec_ref[0:1, :] + vec_ref[1:2, :]).astype(BF16)
    normed_ref[...] = normed
    normed_t_ref[...] = normed.T
    g_t_ref[...] = g_ref[...].T


def normalize(x, g, vec, after=()):
    tokens, width = x.shape
    tile = min(256, tokens)
    row = pl.BlockSpec((tile, width), lambda i: (i, 0))
    col = pl.BlockSpec((width, tile), lambda i: (0, i))
    shape = jax.ShapeDtypeStruct((tokens, width), BF16)
    shape_t = jax.ShapeDtypeStruct((width, tokens), BF16)
    return launch(
        norm_kernel,
        (tokens // tile,),
        [row, row, whole(4, width)],
        (row, col, col),
        (shape, shape_t, shape_t),
        (x, g, vec),
        flops=tokens * width * 10,
        moved=tokens * width * 10,
        after=after,
    )


def qkv_project(places, normed, g, bias, tables, groups, slots, after=()):
    tokens, width = normed.shape
    local = groups[0][0].shape[3]
    flat = [part for group in groups for part in group]
    cut = len(groups[0])
    tile = min(512, tokens)

    def kernel(place_ref, x_ref, g_ref, bias_ref, table_ref, *rest):
        parts, (q_ref, k_ref, v_ref, da_ref, store, sem) = rest[:-6], rest[-6:]

        @pl.when(pl.program_id(0) == 0)
        def _():
            nested = [parts[k : k + cut] for k in range(0, len(flat), cut)]
            load_weights(place_ref, nested, slots, store, sem)

        x = x_ref[...]
        for slot, out, scale in ((0, q_ref, HDIM ** (-0.5)), (1, k_ref, 1.0)):
            z = nn(x, store[:, slot * local : (slot + 1) * local]) + bias_ref[slot : slot + 1, :]
            for pair in range(local // LANES):
                at = slice(pair * LANES, (pair + 1) * LANES)
                out[:, at] = (turn(z[:, at], table_ref, 1.0) * scale).astype(BF16)
        v_ref[...] = (nn(x, store[:, 2 * local : 3 * local]) + bias_ref[2:3, :]).astype(BF16)
        da_ref[...] = nn(g_ref[...], store[:, 3 * local : 4 * local]).astype(BF16)

    row = pl.BlockSpec((tile, width), lambda i, *_: (i, 0))
    out = pl.BlockSpec((tile, local), lambda i, *_: (i, 0))
    shape = jax.ShapeDtypeStruct((tokens, local), BF16)
    return launch(
        kernel,
        (tokens // tile,),
        [row, row, whole(7, local), pl.BlockSpec((3, tile, LANES), lambda i, *_: (0, i, 0))] + [ANY] * len(flat),
        (out,) * 4,
        (shape,) * 4,
        (normed, g, bias, tables, *flat),
        scalars=(places,),
        scratch=(pltpu.VMEM((width, 4 * local), BF16), pltpu.SemaphoreType.DMA),
        flops=2 * tokens * width * 4 * local,
        moved=tokens * width * 4 + width * local * 8,
        after=after,
    )


def attend(first, held, low, query, keys, vals, d_attn, start, tables, after=()):
    tokens, local = query.shape
    block = min(256, tokens)
    count = tokens // block
    pairs = attend_pairs(local)
    heads = 2 * pairs
    wide = pairs * LANES
    scale = HDIM ** (-0.5)
    lanes = [slice(p * LANES, (p + 1) * LANES) for p in range(pairs)]

    def kernel(low_ref, q_ref, k_ref, v_ref, do_ref, start_ref, table_ref, *rest):
        (o_ref, dq_ref, dk_ref, dv_ref, db_ref,
         k_half, v_half, k_t, v_t, s_buf, dp_buf, o_t, dq_t, dk_sum, dv_sum) = rest[len(held):]
        i = pl.program_id(0)
        first_lanes = lax.broadcasted_iota(jnp.int32, (1, LANES), 1) < HDIM
        zero = jnp.zeros((), BF16)

        def apart(pair):
            return jnp.where(first_lanes, pair, zero), jnp.where(first_lanes, zero, pair)

        @pl.when(i == 0)
        def _():
            for b in range(count):
                at = slice(b * block, (b + 1) * block)
                for source, half, flipped in ((k_ref, k_half, k_t), (v_ref, v_half, v_t)):
                    for p in range(pairs):
                        part = source[at, lanes[p]]
                        half[2 * p, at, :], half[2 * p + 1, at, :] = apart(part)
                        flipped[p, b] = part.T
            dk_sum[...] = jnp.zeros_like(dk_sum)
            dv_sum[...] = jnp.zeros_like(dv_sum)
            db_ref[...] = jnp.zeros_like(db_ref)

        q = [q_ref[:, at] for at in lanes]
        do = [do_ref[:, at] for at in lanes]
        q_cat = [jnp.concatenate(apart(pair), 0) for pair in q]
        do_cat = [jnp.concatenate(apart(pair), 0) for pair in do]
        t_place = i * block + lax.broadcasted_iota(jnp.int32, (1, block), 1)
        t_start = start_ref[...]
        low_block = low_ref[i]
        o_t[...] = jnp.zeros_like(o_t)
        dq_t[...] = jnp.zeros_like(dq_t)

        def score(b, tops):
            at = pl.ds(pl.multiple_of(b * block, block), block)
            u_place = b * block + lax.broadcasted_iota(jnp.int32, (block, 1), 0)
            allowed = (u_place >= t_start) & (u_place <= t_place)
            new = []
            for h in range(heads):
                s = jnp.where(allowed, nt(k_half[h, at, :], q[h // 2]), -1e30)
                s_buf[h, b] = s
                dp_buf[h, b] = nt(v_half[h, at, :], do[h // 2])
                new.append(jnp.maximum(tops[h], jnp.max(s, 0, keepdims=True)))
            return tuple(new)

        lowest = jnp.full((1, block), -jnp.inf, F32)
        tops = lax.fori_loop(low_block, i + 1, score, (lowest,) * heads)

        def weigh(b, sums):
            new = []
            for h in range(heads):
                p = jnp.exp(s_buf[h, b] - tops[h])
                s_buf[h, b] = p
                new.append(sums[2 * h] + jnp.sum(p, 0, keepdims=True))
                new.append(sums[2 * h + 1] + jnp.sum(p * dp_buf[h, b], 0, keepdims=True))
            return tuple(new)

        none = jnp.zeros((1, block), F32)
        sums = lax.fori_loop(low_block, i + 1, weigh, (none,) * (2 * heads))
        inverse = [1.0 / sums[2 * h] for h in range(heads)]
        delta = [sums[2 * h + 1] * inverse[h] for h in range(heads)]

        def spread(b, carry):
            at = pl.ds(pl.multiple_of(b * block, block), block)
            probs, grads = [], []
            for h in range(heads):
                rows = slice(h * HDIM, (h + 1) * HDIM)
                inside = slice(h % 2 * HDIM, (h % 2 + 1) * HDIM)
                p = s_buf[h, b] * inverse[h]
                ds = (p * (dp_buf[h, b] - delta[h])).astype(BF16)
                p = p.astype(BF16)
                o_t[rows, :] += nn(v_t[h // 2, b, inside, :], p)
                dq_t[rows, :] += nn(k_t[h // 2, b, inside, :], ds)
                probs.append(p)
                grads.append(ds)
            for p in range(pairs):
                dv_sum[at, lanes[p]] += nn(jnp.concatenate(probs[2 * p : 2 * p + 2], 1), do_cat[p])
                dk_sum[at, lanes[p]] += nn(jnp.concatenate(grads[2 * p : 2 * p + 2], 1), q_cat[p])
            return carry

        lax.fori_loop(low_block, i + 1, spread, 0)
        o_ref[...] = o_t[...].T.astype(BF16)
        here = pl.ds(pl.multiple_of(i * block, block), block)
        table = [table_ref[n, here, :] for n in range(3)]
        for at in lanes:
            dq = turn(dq_t[at, :].T * scale, table, -1.0).astype(BF16)
            dq_ref[:, at] = dq
            db_ref[0:1, at] += jnp.sum(dq.astype(F32), 0, keepdims=True)

        @pl.when(i == count - 1)
        def _():
            for at in lanes:
                dk = turn(dk_sum[:, at], table_ref, -1.0).astype(BF16)
                dv = dv_sum[:, at].astype(BF16)
                dk_ref[:, at] = dk
                dv_ref[:, at] = dv
                db_ref[1:2, at] = jnp.sum(dk.astype(F32), 0, keepdims=True)
                db_ref[2:3, at] = jnp.sum(dv.astype(F32), 0, keepdims=True)

    part = pl.BlockSpec((block, wide), lambda i, *_: (i, first))
    column = pl.BlockSpec((tokens, wide), lambda i, *_: (0, first))
    shape = jax.ShapeDtypeStruct((tokens, local), BF16)
    return launch(
        kernel,
        (count,),
        [part, column, column, part, pl.BlockSpec((1, block), lambda i, *_: (0, i)), whole(3, tokens, LANES)]
        + [ANY] * len(held),
        (part, part, column, column, pl.BlockSpec((3, wide), lambda i, *_: (0, first))),
        (shape,) * 4 + (jax.ShapeDtypeStruct((3, local), F32),),
        (query, keys, vals, d_attn, start, tables, *held),
        scalars=(low,),
        aliases={7 + i: i for i in range(len(held))},
        scratch=(
            pltpu.VMEM((heads, tokens, LANES), BF16),
            pltpu.VMEM((heads, tokens, LANES), BF16),
            pltpu.VMEM((pairs, count, LANES, block), BF16),
            pltpu.VMEM((pairs, count, LANES, block), BF16),
            pltpu.VMEM((heads, count, block, block), F32),
            pltpu.VMEM((heads, count, block, block), F32),
            pltpu.VMEM((wide, block), F32),
            pltpu.VMEM((wide, block), F32),
            pltpu.VMEM((tokens, wide), F32),
            pltpu.VMEM((tokens, wide), F32),
        ),
        after=after,
    )


def attend_pairs(local):
    return 2 if local % (2 * LANES) == 0 else 1


def hidden_slot(places, normed, g, bias, group, after=()):
    tokens, width = normed.shape
    local = group[0].shape[3]
    tile = min(512, tokens)

    def kernel(place_ref, x_ref, g_ref, bias_ref, *rest):
        parts, (h_ref, dz_ref, db_ref, store, sem) = rest[:-5], rest[-5:]

        @pl.when(pl.program_id(0) == 0)
        def _():
            load_weights(place_ref, [parts], [(0, 0), (0, 1)], store, sem)
            db_ref[...] = jnp.zeros_like(db_ref)

        v = nn(x_ref[...], store[:, :local]) + bias_ref[...]
        dh = nn(g_ref[...], store[:, local:])
        square = v * v
        t = jnp.tanh(0.7978845608 * (v + 0.044715 * (square * v)))
        half = 0.5 * (1.0 + t)
        h_ref[...] = (v * half).astype(BF16)
        slope = half + (0.5 * v) * (1.0 - t * t) * (0.7978845608 + (3.0 * 0.044715 * 0.7978845608) * square)
        dz = (dh * slope).astype(BF16)
        dz_ref[...] = dz
        db_ref[...] += jnp.sum(dz.astype(F32), 0, keepdims=True)

    row = pl.BlockSpec((tile, width), lambda i, *_: (i, 0))
    out = pl.BlockSpec((tile, local), lambda i, *_: (i, 0))
    shape = jax.ShapeDtypeStruct((tokens, local), BF16)
    return launch(
        kernel,
        (tokens // tile,),
        [row, row, whole(1, local)] + [ANY] * len(group),
        (out, out, whole(1, local)),
        (shape, shape, jax.ShapeDtypeStruct((1, local), F32)),
        (normed, g, bias, *group),
        scalars=(places,),
        scratch=(pltpu.VMEM((width, 2 * local), BF16), pltpu.SemaphoreType.DMA),
        flops=4 * tokens * width * local,
        moved=tokens * width * 4 + width * local * 4,
        after=after,
        weight=5,
    )


def grad_blocks(inner_at, inner, normed_t, g_t, sides, received, after=(), weight=1):
    width, tokens = normed_t.shape
    outer = lax.axis_size("dp") // inner
    owners = inner_at.shape[0]
    n = len(sides)
    cuts = len(sides[0][1])
    piece_width = sides[0][1][0].shape[1]
    local = cuts * piece_width
    rows = width // (outer * inner)

    def kernel(inner_ref, *rest):
        lefts = rest[:2]
        rights = rest[2 : 2 + n * cuts]
        adds = rest[2 + n * cuts : -1]
        out = rest[-1]
        step = pl.program_id(1)
        for i, (side, _) in enumerate(sides):

            @pl.when(step == i)
            def _(i=i, side=side):
                left = lefts[side][...].reshape(outer * rows, tokens)
                for c in range(cuts):
                    at = slice(c * piece_width, (c + 1) * piece_width)
                    total = nn(left, rights[i * cuts + c][...]).reshape(outer, rows, piece_width)
                    for add in adds:
                        total += add[:, 0, 0, :, at].astype(F32)
                    out[:, 0, 0, :, at] = total.astype(BF16)

    left = pl.BlockSpec((outer, 1, rows, tokens), lambda o, i, inner_ref, *_: (0, inner_ref[o], 0, 0))
    piece = pl.BlockSpec((outer, 1, 1, rows, local), lambda o, i, *_: (0, o, i, 0, 0))
    four = (outer, inner, rows, tokens)
    return launch(
        kernel,
        (owners, n),
        [left, left] + [whole(tokens, piece_width)] * (n * cuts) + [piece] * len(received),
        piece,
        jax.ShapeDtypeStruct((outer, owners, n, rows, local), BF16),
        (normed_t.reshape(four), g_t.reshape(four), *[right for _, rights in sides for right in rights], *received),
        scalars=(inner_at,),
        after=after,
        weight=weight,
    )


def project_back(places, shares, lefts, groups, slots, received, split, after=()):
    tokens = lefts[0].shape[0]
    local = groups[0][0].shape[3]
    count = shares.shape[0]
    share = tokens // lax.axis_size("tensor")
    tile = min(512, share)
    steps = share // tile
    width = places.shape[0] * groups[0][0].shape[2]
    m = len(lefts)
    depth = len(slots) * local
    flat = [part for group in groups for part in group]
    cut = len(groups[0])
    n_groups = len(flat)

    def kernel(place_ref, shares_ref, *rest):
        left_refs = rest[:m]
        refs = rest[m : m + n_groups]
        adds = rest[m + n_groups : m + n_groups + len(received)]
        outs = rest[m + n_groups + len(received) : -2]
        store, sem = rest[-2:]
        step, part = pl.program_id(0), pl.program_id(1)

        @pl.when((step == 0) & (part == 0))
        def _():
            nested = [refs[k : k + cut] for k in range(0, n_groups, cut)]
            load_weights(place_ref, nested, slots, store, sem)

        total = nt(jnp.concatenate([left[...] for left in left_refs], 1), store[...])
        for add in adds:
            total += add[...].astype(F32)
        if not split:
            outs[0][...] = total.astype(BF16)
        else:
            at = pl.ds(pl.multiple_of(part * tile, tile), tile)
            for j, out in enumerate(outs):

                @pl.when(step == j)
                def _(out=out):
                    out[at, :] = total.astype(out.dtype)

    def left(array):
        return pl.BlockSpec((tile, array.shape[1]), lambda i, j, p_ref, s_ref: (s_ref[i] * steps + j, 0))

    piece = pl.BlockSpec((tile, width), lambda i, j, *_: (i * steps + j, 0))
    if split:
        out_specs = (whole(share, width),) * count
        out_shape = tuple(jax.ShapeDtypeStruct((share, width), F32 if j == 0 else BF16) for j in range(count))
    else:
        out_specs = piece
        out_shape = jax.ShapeDtypeStruct((count * share, width), BF16)
    return launch(
        kernel,
        (count, steps),
        [left(array) for array in lefts] + [ANY] * n_groups + [piece] * len(received),
        out_specs,
        out_shape,
        (*lefts, *flat, *received),
        scalars=(places, shares),
        scratch=(pltpu.VMEM((width, depth), BF16), pltpu.SemaphoreType.DMA),
        flops=2 * count * share * width * depth,
        moved=width * depth * 2 + count * share * (depth + width) * 2,
        after=after,
    )


def finish_output(mine, own, received, x, vec, after=()):
    share, width = own.shape
    tile = min(256, share)
    steps = share // tile

    def kernel(mine_ref, own_ref, x_ref, vec_ref, *rest):
        total = own_ref[...]
        for ref in rest[:-1]:
            total += ref[...].astype(F32)
        rest[-1][...] = (x_ref[...].astype(F32) + total + vec_ref[2:3, :] + vec_ref[3:4, :]).astype(BF16)

    row = pl.BlockSpec((tile, width), lambda i, *_: (i, 0))
    far = pl.BlockSpec((tile, width), lambda i, mine_ref: (mine_ref[0] * steps + i, 0))
    return launch(
        kernel,
        (steps,),
        [row, far, whole(4, width)] + [row] * len(received),
        row,
        jax.ShapeDtypeStruct((share, width), BF16),
        (own, x, vec, *received),
        scalars=(mine,),
        moved=share * width * 10,
        after=after,
    )


def finish_input(mine, own, received, x, g, vec, after=()):
    share, width = own.shape
    tile = min(256, share)
    steps = share // tile

    def kernel(mine_ref, own_ref, x_ref, g_ref, vec_ref, *rest):
        grad_ref, rows_ref = rest[-2:]
        dn = own_ref[...]
        for ref in rest[:-2]:
            dn += ref[...].astype(F32)
        x = x_ref[...].astype(F32)
        g = g_ref[...].astype(F32)
        mean = jnp.mean(x, -1, keepdims=True)
        centered = x - mean
        var = jnp.mean(centered * centered, -1, keepdims=True)
        inverse = lax.rsqrt(var + 1e-05)
        hat = centered * inverse
        e = dn * vec_ref[0:1, :]
        back = inverse * (e - jnp.mean(e, -1, keepdims=True) - hat * jnp.mean(e * hat, -1, keepdims=True))
        grad_ref[...] = (g + back).astype(BF16)

        @pl.when(pl.program_id(0) == 0)
        def _():
            rows_ref[...] = jnp.zeros_like(rows_ref)

        rows_ref[0:1, :] += jnp.sum(dn * hat, 0, keepdims=True)
        rows_ref[1:2, :] += jnp.sum(dn, 0, keepdims=True)
        rows_ref[2:3, :] += jnp.sum(g, 0, keepdims=True)

    row = pl.BlockSpec((tile, width), lambda i, *_: (i, 0))
    far = pl.BlockSpec((tile, width), lambda i, mine_ref: (mine_ref[0] * steps + i, 0))
    return launch(
        kernel,
        (steps,),
        [row, far, far, whole(4, width)] + [row] * len(received),
        (row, whole(3, width)),
        (jax.ShapeDtypeStruct((share, width), BF16), jax.ShapeDtypeStruct((3, width), F32)),
        (own, x, g, vec, *received),
        scalars=(mine,),
        moved=share * width * 12,
        after=after,
    )


def lay_out(order, parts, after=()):
    share, width = parts[0].shape
    count = len(parts)
    tile = min(256, share)
    steps = share // tile

    def kernel(order_ref, *rest):
        for r in range(count):

            @pl.when(pl.program_id(0) == r)
            def _(r=r):
                rest[count][...] = rest[r][...]

    def fetch(r):
        return pl.BlockSpec(
            (tile, width), lambda i, j, *_: (jnp.where(i == r, j, jnp.where(i < r, 0, steps - 1)), 0)
        )

    return launch(
        kernel,
        (count, steps),
        [fetch(r) for r in range(count)],
        pl.BlockSpec((tile, width), lambda i, j, order_ref: (order_ref[i] * steps + j, 0)),
        jax.ShapeDtypeStruct((share * count, width), parts[0].dtype),
        parts,
        scalars=(order,),
        moved=share * count * width * 4,
        after=after,
    )


def total_group(grads, own, received, places, slots_in_all, after=(), weight=1):
    n, rows, local = own.shape

    def kernel(places_ref, own_ref, *rest):
        out, squares = rest[-2:]
        total = own_ref[0].astype(F32)
        for ref in rest[: len(received)]:
            total += ref[0].astype(F32)
        out[0] = total

        @pl.when(pl.program_id(0) == 0)
        def _():
            squares[...] = jnp.zeros_like(squares)

        squares[...] += jnp.sum(total * total, 0, keepdims=True)

    piece = pl.BlockSpec((1, rows, local), lambda i, *_: (i, 0, 0))
    out = pl.BlockSpec((1, rows, local), lambda i, places_ref: (places_ref[i], 0, 0))
    first = grads is None
    return launch(
        kernel,
        (n,),
        [piece] * (1 + len(received)) + ([] if first else [ANY]),
        (out, whole(1, local)),
        (jax.ShapeDtypeStruct((slots_in_all, rows, local), F32), jax.ShapeDtypeStruct((1, local), F32)),
        (own, *received) + (() if first else (grads,)),
        scalars=(places,),
        aliases={} if first else {2 + len(received): 0},
        after=after,
        weight=weight,
    )


def collect(values, axis, count):
    rows = [values]
    for k in range(1, count):
        rows.append(lax.ppermute(values, axis, [(i, (i + k) % count) for i in range(count)]))
    rows = jnp.concatenate(rows[::-1] * 2, 0)
    return lax.dynamic_slice_in_dim(rows, count - 1 - lax.axis_index(axis), count, 0)


def total_over(values, axis, count):
    bit = 1
    while bit < count:
        values = values + lax.ppermute(values, axis, [(i, i ^ bit) for i in range(count)])
        bit *= 2
    return values


def shift(values, axis, count, inner, outer_by, inner_by):
    outer = count // inner
    pairs = [
        (o * inner + i, (o + outer_by) % outer * inner + (i + inner_by) % inner)
        for o in range(outer)
        for i in range(inner)
    ]
    return lax.ppermute(values, axis, pairs)


def body(
    block_input,
    cotangent,
    segment_ids,
    w_in,
    w_in_m,
    w_in_v,
    w_outs,
    w_outs_m,
    w_outs_v,
    in_bias,
    in_bias_m,
    in_bias_v,
    vectors,
    vectors_m,
    vectors_v,
):
    n_dp = lax.axis_size("dp")
    n_tensor = lax.axis_size("tensor")
    inner = 2
    outer = n_dp // inner
    cores = 2
    ways = n_tensor // cores
    me = lax.axis_index("dp")
    mine = lax.axis_index("tensor")
    my_outer, my_inner = me // inner, me % inner
    my_way, my_core = mine // cores, mine % cores
    tokens, width = block_input.shape
    _, slots_in, local = w_in.shape
    slots_out = w_outs.shape[1]
    hidden_slots = slots_out - 1

    def numbers(values):
        return jnp.stack([jnp.asarray(v, jnp.int32) for v in values])

    other_inner = 1 - my_inner
    inner_at = [numbers([my_inner]), numbers([other_inner])]
    both_inner = jnp.arange(inner, dtype=jnp.int32)
    lines = [[o * inner + i for o in range(outer)] for i in range(inner)]
    owner_places = numbers(
        [o * inner + i for i in (my_inner, other_inner) for o in range(outer)]
    )
    share_order = numbers(
        [(my_way - w) % ways * cores + (my_core - c) % cores for w in range(ways) for c in range(cores)]
    )
    share_dests = [
        numbers([(my_way + w) % ways * cores + (my_core + c) % cores for w in range(ways)])
        for c in range(cores)
    ]
    share_mine = numbers([mine])

    def to_partner(values):
        return shift(values, "dp", n_dp, inner, 0, 1)


    w_in_s = w_in.transpose(1, 0, 2)
    w_outs_s = w_outs.transpose(1, 0, 2)

    first_slots = [(0, 0), (0, 1), (0, 2), (1, 0)]
    gather_slots = [first_slots[:2], first_slots[2:]] + [[(0, 3 + s), (1, 1 + s)] for s in range(hidden_slots)]
    joined = [list(range(s, min(s + 2, hidden_slots))) for s in range(0, hidden_slots, 2)]
    group_slots = [first_slots] + [[at for s in some for at in ((0, 3 + s), (1, 1 + s))] for some in joined]

    small = jnp.concatenate([in_bias.reshape(1, -1), vectors.reshape(1, -1)], 1).astype(BF16).astype(F32)
    small = collect(small, "dp", n_dp)
    bias_size = in_bias.size
    bias = small[:, :bias_size].reshape((n_dp,) + in_bias.shape).transpose(1, 2, 0, 3).reshape(slots_in, local)
    vec = small[:, bias_size:].reshape((n_dp,) + vectors.shape).transpose(1, 0, 2).reshape(4, width)

    LINE.last = ()
    LINE.weight = 1
    turns = list(range(len(group_slots)))
    along = []
    for slots in gather_slots:
        cast = cast_group(w_in_s, w_outs_s, slots, LINE.last)
        LINE.last = (cast,)
        along.append(lax.all_gather(cast, "dp", axis=0, axis_index_groups=lines))
    groups = []

    def exchange(g):
        here = gate(along[g])[0]
        groups.append([here, to_partner(here)])

    seg = segment_ids[0]
    start = jnp.sum((seg[None, :] < seg[:, None]).astype(jnp.int32), 1)
    block = min(256, tokens)
    low = start[::block] // block
    place = (jnp.arange(tokens, dtype=jnp.int32) - start).astype(F32)
    freq = 10000.0 ** (-jnp.arange(ROT // 2, dtype=F32) * 2.0 / ROT)
    freq = jnp.tile(jnp.concatenate([freq, freq, jnp.zeros((HDIM - ROT,), F32)]), LANES // HDIM)
    theta = place[:, None] * freq[None, :]
    sine = jnp.sin(theta)
    feature = jnp.arange(LANES) % HDIM
    tables = jnp.stack(
        [
            jnp.cos(theta),
            jnp.where(feature < ROT // 2, -sine, 0.0),
            jnp.where((feature >= ROT // 2) & (feature < ROT), sine, 0.0),
        ]
    )
    LINE.last = LINE.last + (tables, low)

    normed, normed_t, g_t = in_line(normalize, block_input, cotangent, vec)

    hidden, d_hidden, d_bias_hidden, sides = [], [], [], {}

    def hidden_step(s):
        h, dz, db = in_line(hidden_slot, owner_places, normed, cotangent, bias[3 + s : 4 + s], groups[2 + s])
        hidden.append(h)
        d_hidden.append(dz)
        d_bias_hidden.append(db)
        sides.setdefault(1 + s // 2, []).extend([(0, [dz]), (1, [h])])

    legs, shares = {}, {}

    def scatter(out):
        outer_blocks, owners, n, rows, columns = out.shape
        out = out.reshape(outer_blocks * owners * n, rows, columns)
        out = lax.psum_scatter(out, "dp", scatter_dimension=0, axis_index_groups=lines, tiled=True)
        return out.reshape(owners, n, rows, columns)

    def first_next(g, weight=1):
        out = in_line(grad_blocks, inner_at[1], inner, normed_t, g_t, sides[g], [], weight=weight)
        legs[g] = [to_partner(out)]

    def second_next(g):
        out = in_line(grad_blocks, inner_at[0], inner, normed_t, g_t, sides[g], legs[g])
        shares[g] = (scatter(out)[0], [])

    def line_first(g):
        out = scatter(in_line(grad_blocks, both_inner, inner, normed_t, g_t, sides[g], []))
        sent = lax.dynamic_index_in_dim(out, other_inner, 0, False)
        shares[g] = (lax.dynamic_index_in_dim(out, my_inner, 0, False), [to_partner(sent)])

    exchange(0)
    exchange(1)
    groups[0][1] = gate(groups[0][1], weight=5)[0]
    exchange(2)
    to_exchange = list(range(3, 2 + hidden_slots))
    in_first = [(0, 0), (0, 1), (1, 0), (1, 1)]
    qkvd = in_line(qkv_project, owner_places, normed, cotangent, bias, tables, groups[:2], in_first)
    held = ()
    for first in range(local // (attend_pairs(local) * LANES)):
        held = in_line(attend, first, held, low, *qkvd, start.reshape(1, tokens), tables)
        if to_exchange:
            exchange(to_exchange.pop(0))
    attn, d_query, d_keys, d_vals, d_bias_attn = held
    sides[0] = [(0, [d_query]), (0, [d_keys]), (0, [d_vals]), (1, [attn])]
    line_first(0)
    while to_exchange:
        exchange(to_exchange.pop(0))
    for s in joined[0]:
        hidden_step(s)
    ahead_of = len(groups) - 1
    for s in range(len(joined[0]), hidden_slots - 1):
        groups[2 + s][1] = gate(groups[2 + s][1])[0]
        hidden_step(s)
    for g in range(min(ahead_of, 2 + len(hidden)), len(groups)):
        groups[g][1] = gate(groups[g][1])[0]
    first_next(1, 5000)
    for s in range(len(hidden), hidden_slots):
        hidden_step(s)
    LINE.weight = 5000

    def first_half(lefts, slots):
        received = []
        for c in range(1, cores):
            out = in_line(project_back, owner_places, share_dests[c], lefts, groups, slots, [], False)
            received.append(shift(out, "tensor", n_tensor, cores, 0, c))
        return received

    def second_half(lefts, slots, received):
        outs = in_line(project_back, owner_places, share_dests[0], lefts, groups, slots, received, True)
        return outs[0], [shift(outs[w], "tensor", n_tensor, cores, w, 0) for w in range(1, ways)]

    def send_share(own):
        return [own] + [shift(own, "tensor", n_tensor, cores, w, 0) for w in range(1, ways)]

    def gather_share(held):
        return [held[0]] + gate(*held[1:])

    def spread_share(held):
        parts = []
        for part in held:
            parts.append(part)
            for c in range(1, cores):
                parts.append(shift(part, "tensor", n_tensor, cores, 0, c))
        return parts

    back = (
        [d_query, d_keys, d_vals] + d_hidden,
        in_first[:3] + [(2 + s, 0) for s in range(hidden_slots)],
    )
    ahead = ([attn] + hidden, in_first[3:] + [(2 + s, 1) for s in range(hidden_slots)])
    grads, squares = None, []

    def total_next(g, weight=1):
        slots, (own, received) = group_slots[g], shares[g]
        places = jnp.asarray([s if which == 0 else slots_in + s for which, s in slots], jnp.int32)
        out, part = in_line(total_group, grads, own, received, places, slots_in + slots_out, weight=weight)
        squares.append(part)
        return out

    for g in range(2, 1 + len(joined)):
        first_next(g)
    back_half = first_half(*back)
    ahead_half = first_half(*ahead)
    own, received = second_half(*back, back_half)
    second_next(1)
    ahead_own, ahead_received = second_half(*ahead, ahead_half)
    d_x, vector_rows = in_line(finish_input, share_mine, own, received, block_input, cotangent, vec)
    back_held = send_share(d_x)
    out_held = send_share(
        in_line(finish_output, share_mine, ahead_own, ahead_received, block_input, vec)
    )
    for g in range(2, 1 + len(joined)):
        second_next(g)
    grads = total_next(0)
    vector_rows = total_over(vector_rows.reshape(1, -1), "tensor", n_tensor)
    d_bias = jnp.concatenate([d_bias_attn] + d_bias_hidden, 0)
    small = total_over(jnp.concatenate([d_bias.reshape(1, -1), vector_rows], 1), "dp", n_dp)
    g_bias = lax.dynamic_index_in_dim(
        small[0, : slots_in * local].reshape(slots_in, in_bias.shape[1], n_dp, in_bias.shape[2]), me, 2, False
    )
    g_vec = lax.dynamic_index_in_dim(small[0, slots_in * local :].reshape(3, n_dp, width // n_dp), me, 1, False)
    g_vec = jnp.concatenate([g_vec, g_vec[2:]], 0)

    back_parts = spread_share(gather_share(back_held))
    for g in turns[1:-1]:
        grads = total_next(g)
    out_parts = spread_share(gather_share(out_held))
    block_input_gradient = in_line(lay_out, share_order, back_parts)
    output = in_line(lay_out, share_order, out_parts)
    LINE.last = LINE.last + (g_bias, g_vec)
    grads = total_next(turns[-1])
    LINE.weight = 1
    g_in, g_outs = grads[:slots_in], grads[slots_in:]
    local_squares = (
        jnp.sum(jnp.concatenate(squares, 0)) + jnp.sum(g_bias * g_bias) + jnp.sum(g_vec * g_vec) * (1.0 / n_tensor)
    )
    local_squares = total_over(jnp.full((1, LANES), local_squares), "tensor", n_tensor)
    local_squares = total_over(local_squares, "dp", n_dp)
    grad_norm = jnp.sqrt(local_squares[0, 0])
    factor = CLIP_AT / jnp.maximum(grad_norm, CLIP_AT)

    def slot_major(*arrays):
        return [a.transpose(1, 0, 2) for a in arrays]

    new_in = slot_major(*adamw(w_in_s, *slot_major(w_in_m, w_in_v), g_in, factor, RATE_MATRIX, DECAY_MATRIX))
    new_outs = slot_major(*adamw(w_outs_s, *slot_major(w_outs_m, w_outs_v), g_outs, factor, RATE_MATRIX, DECAY_MATRIX))
    new_bias = adamw(in_bias, in_bias_m, in_bias_v, g_bias, factor, RATE_VECTOR, 0.0)
    new_vec = adamw(vectors, vectors_m, vectors_v, g_vec, factor, RATE_VECTOR, 0.0)
    return (output, block_input_gradient, grad_norm, *new_in, *new_outs, *new_bias, *new_vec)


def solution(mesh):
    rows = P("dp", None)
    matrix = P("dp", None, "tensor")
    small = P(None, "tensor", "dp")
    vector = P(None, "dp")
    return jax.shard_map(
        body,
        mesh=mesh,
        in_specs=(rows,) * 3 + (matrix,) * 6 + (small,) * 3 + (vector,) * 3,
        out_specs=(rows, rows, P()) + (matrix,) * 6 + (small,) * 3 + (vector,) * 3,
        check_vma=False,
    )
```
